32 devices in a mesh: dp: 4 (over z), ctx: 8 (over y, x, core).
Axes of the slice: x: 2, y: 2, z: 4, core: 2. Of those that a mesh axis runs over, the one named last changes fastest.
Arguments:
- tokens: bfloat16 [1536, 4096], P('ctx'), may hold values from -6 to 6
- w_in: bfloat16 [4096, 3, 4096], P('ctx', None, 'dp'), may hold values from -0.09375 to 0.09375
- short_filter: float32 [3, 3, 4096], P(None, None, 'dp'), may hold values from -3.5 to 3.5
- mode_decay: float32 [8, 4096], P(None, 'dp'), may hold values from 0 to 1
- residue: float32 [8, 4096], P(None, 'dp'), may hold values from -2 to 2
- w_out: bfloat16 [4096, 4096], P('dp'), may hold values from -0.125 to 0.125
Outputs:
- block_out: bfloat16 [1536, 4096], P('ctx', 'dp')
The draws below stay inside these ranges and needn't reach their ends.
All inputs are finite; a program needn't handle non-finite values.
Results may differ from the reference program's by a relative error of at most 0.018.
Values may be sent and summed in bfloat16 or wider, within the bound.
No kernel may reach another device: no remote copies, remote signals or barrier semaphores. Data moves between devices by JAX's collectives and lax.ppermute only.
A program may use at most 128 MiB of HBM per device.

```python
import jax
import jax.numpy as jnp
from jax import lax

D = 4096
ST = 3
MODES = 8
TOKENS = 1536
CHANNELS = 1024


def draw_mode_decay(key, part):
    slow_key, fast_key, pick_key = jax.random.split(key, 3)
    shape = (MODES, D)
    share = 0.5
    picked = jax.random.uniform(pick_key, shape, jnp.float32) < share
    slow_rate = jnp.exp(jax.random.uniform(slow_key, shape, jnp.float32, jnp.log(0.3 / TOKENS), jnp.log(2.0 / TOKENS)))
    fast_rate = jnp.exp(jax.random.uniform(fast_key, shape, jnp.float32, jnp.log(1.0 / 50.0), jnp.log(1.0 / 30.0)))
    return jnp.exp(-jnp.where(picked, slow_rate, fast_rate)).astype(jnp.float32)


def strengthened(array, rng, source, target, parts, factor):
    owner, partner = [(jnp.arange(array.shape[position]) // (array.shape[position] // parts)).reshape([-1 if axis == position else 1 for axis in range(array.ndim)]) for position in (source, target)]
    chosen = jax.random.permutation(rng, parts)[partner]
    strong = (owner == chosen) | (owner == (partner + parts // 2) % parts)
    return jnp.where(strong, factor * array, array)


def block_levels(own_key, shape, shards, low, largest):
    factor_of, own = 1.0, jax.random.fold_in(own_key, 6)
    for dim, parts in shards:
        heights = jnp.exp(jax.random.uniform(jax.random.fold_in(own, dim), (parts,), jnp.float32, low / len(shards), largest / len(shards)))
        factor_of = factor_of * jnp.repeat(heights, shape[dim] // parts).reshape([-1 if axis == dim else 1 for axis in range(len(shape))])
    return factor_of


def bell_draw(key, extent, scale, reach, shards=(), kind=jnp.bfloat16):
    values = scale * jax.random.normal(key, extent, jnp.float32)
    if shards:
        values = values * block_levels(key, extent, shards, -0.22, 0.18)
    return jnp.clip(values, -reach, reach).astype(kind)


def bell_draw_with(own_key, shape, width, limit, cuts, heavy, kind=jnp.bfloat16):
    values = width * jax.random.normal(own_key, shape, jnp.float32)
    if cuts:
        values = values * block_levels(own_key, shape, cuts, -0.22, 0.18)
    return jnp.clip(strengthened(values, jax.random.fold_in(own_key, 3), *heavy), -limit, limit).astype(kind)


def setup_inputs(seed: int = 0) -> dict:
    keys = jax.random.split(jax.random.key(seed), 7)
    tokens = bell_draw(keys[0], (TOKENS, D), 1.0, 6.0, ((0, 8),))
    w_in = bell_draw(keys[1], (D, 3, D), D ** -0.5, 0.09375, ((0, 8), (2, 4)))
    short_filter = bell_draw(keys[2], (ST, 3, D), ST ** -0.5, 3.5, ((2, 4),), jnp.float32)
    mode_decay = draw_mode_decay(jax.random.fold_in(keys[6], 71), 0)
    residue = bell_draw(keys[4], (MODES, D), MODES ** -0.5, 2.0, ((1, 4),), jnp.float32)
    w_out = bell_draw_with(keys[5], (D, D), D ** -0.5, 0.125, ((0, 4),), (0, 1, 4, 2.0))
    return dict(tokens=tokens, w_in=w_in, short_filter=short_filter, mode_decay=mode_decay, residue=residue, w_out=w_out)


def causal_taps(signal, tap_table):
    tap_count = tap_table.shape[0]
    seq_length = signal.shape[0]
    padded = jnp.concatenate([jnp.zeros((tap_count - 1,) + signal.shape[1:], signal.dtype), signal], 0)

    def add_tap(j, running):
        window = lax.dynamic_slice_in_dim(padded, tap_count - 1 - j, seq_length, 0).astype(jnp.float32)
        weight = lax.dynamic_index_in_dim(tap_table, j, 0, keepdims=False)
        return running + weight * window
    return lax.fori_loop(0, tap_count, add_tap, jnp.zeros(signal.shape, jnp.float32))

def long_block(operands):
    signal, decay_block, residue_block = operands
    mode_gain = residue_block * jnp.sqrt(1.0 - decay_block * decay_block)
    step_times = jnp.arange(TOKENS).astype(jnp.float32)
    kernel = jnp.zeros(signal.shape, jnp.float32)
    for n in range(MODES):
        kernel = kernel + mode_gain[n][None, :] * jnp.power(decay_block[n][None, :], step_times[:, None])
    fft_length = 2 * TOKENS
    spectrum = jnp.fft.rfft(signal, n=fft_length, axis=0) * jnp.fft.rfft(kernel, n=fft_length, axis=0)
    return jnp.fft.irfft(spectrum, n=fft_length, axis=0)[:TOKENS]

def reference(tokens, w_in, short_filter, mode_decay, residue, w_out):
    projected = jnp.dot(tokens, w_in.reshape(D, 3 * D), preferred_element_type=jnp.float32).reshape(TOKENS, 3, D)
    featured = causal_taps(projected, short_filter)
    mixed = (featured[:, 1] * featured[:, 2]).astype(jnp.bfloat16)
    medium = mixed.astype(jnp.float32)
    groups = D // CHANNELS
    signal = medium.reshape(TOKENS, groups, CHANNELS).transpose(1, 0, 2)
    decays = mode_decay.reshape(MODES, groups, CHANNELS).transpose(1, 0, 2)
    residues = residue.reshape(MODES, groups, CHANNELS).transpose(1, 0, 2)
    long_part = lax.map(long_block, (signal, decays, residues))
    long_part = long_part.transpose(1, 0, 2).reshape(TOKENS, D)
    gated = (featured[:, 0] * long_part).astype(jnp.bfloat16)
    result = jnp.zeros((TOKENS, D), jnp.float32)
    for g in range(groups):
        first_chan = g * CHANNELS
        partial_sum = jnp.dot(gated[:, first_chan:first_chan + CHANNELS], w_out[first_chan:first_chan + CHANNELS], preferred_element_type=jnp.float32).astype(jnp.bfloat16)
        partial_sum = lax.optimization_barrier(partial_sum)
        result = result + partial_sum.astype(jnp.float32)
    return result.astype(jnp.bfloat16)
```

```python
import functools

import jax
import jax.numpy as jnp
from jax import lax
from jax.experimental import pallas as pl
from jax.experimental.pallas import tpu as pltpu
from jax.sharding import PartitionSpec as P

BLK = 64
F32, BF16 = jnp.float32, jnp.bfloat16
VMEM_LIMIT = 48 * 1024 * 1024


def from_behind(block, axis, distance):
    devices = range(lax.axis_size(axis))
    route = [(i - distance, i) for i in devices if i - distance in devices]
    return lax.ppermute(block, axis, route)


def prefix(value, axis, join, neutral):
    count, mine = (lax.axis_size(axis), lax.axis_index(axis))
    pieces = jax.tree.map(lambda part: lax.all_gather(part, axis), value)
    subtotal = jax.tree.map(
        lambda part, zero: jnp.full_like(part, 0) + jnp.asarray(zero, part.dtype), value, neutral
    )

    def lap(position, subtotal):
        longer = join(subtotal, jax.tree.map(lambda part: part[position], pieces))
        return jax.tree.map(lambda new, old: jnp.where(position < mine, new, old), longer, subtotal)

    return lax.fori_loop(0, count - 1, lap, subtotal)


def on_device_any(tokens, w_in, short_filter, mode_decay, residue, w_out):
    row_count = tokens.shape[0]
    chan_count = w_in.shape[2]
    short_count = short_filter.shape[0]
    mode_count = mode_decay.shape[0]
    earlier_rows = from_behind(tokens[row_count - (short_count - 1) :], "ctx", 1)
    source = jnp.concatenate([earlier_rows, tokens], 0)
    projected = jnp.einsum(
        "td,dgc->tgc",
        source,
        lax.all_gather(w_in, "ctx", axis=0, tiled=True),
        preferred_element_type=jnp.float32,
    )
    featured = jnp.zeros((row_count, 3, chan_count), jnp.float32)
    for j in range(short_count):
        featured = (
            featured
            + short_filter[j] * projected[short_count - 1 - j : short_count - 1 - j + row_count]
        )
    mixed = (featured[:, 1] * featured[:, 2]).astype(jnp.bfloat16)
    medium = mixed.astype(jnp.float32)
    highest = lax.Precision.HIGHEST
    mode_gain = residue * jnp.sqrt(1.0 - mode_decay * mode_decay)
    block_len = BLK
    block_times = jnp.arange(block_len).astype(jnp.float32)
    power_in = jnp.power(mode_decay[None], block_times[:, None, None])
    kernel_head = jnp.sum(mode_gain[None] * power_in, 1)
    lag_index = jnp.arange(block_len)[:, None] - jnp.arange(block_len)[None, :]
    toeplitz = jnp.where(
        (lag_index >= 0)[:, :, None], kernel_head[jnp.clip(lag_index, 0, block_len - 1)], 0.0
    )
    carry_weights = mode_gain[None] * power_in * mode_decay[None]
    state_weights = power_in[::-1]
    decay_block = jnp.power(mode_decay, float(block_len))
    blocks = medium.reshape(row_count // block_len, block_len, chan_count)

    def block_step(carried, block_rows):
        inner = jnp.einsum("tsc,sc->tc", toeplitz, block_rows, precision=highest)
        inner = inner + jnp.einsum("tnc,nc->tc", carry_weights, carried, precision=highest)
        carried = decay_block * carried + jnp.einsum(
            "snc,sc->nc", state_weights, block_rows, precision=highest
        )
        return (carried, inner)

    zero_state = jnp.zeros((mode_count, chan_count), jnp.float32)
    local_end, local_part = lax.scan(block_step, zero_state, blocks)
    local_part = local_part.reshape(row_count, chan_count)
    decay_device = jnp.power(mode_decay, float(row_count))

    def combine_states(earlier, later):
        return (earlier[0] * later[0], later[0] * earlier[1] + later[1])

    identity = (jnp.ones((mode_count, chan_count), jnp.float32), zero_state)
    scanned = prefix((decay_device, local_end), "ctx", combine_states, identity)
    entering = scanned[1]
    row_times = jnp.arange(1, row_count + 1).astype(jnp.float32)
    entry_weights = mode_gain[None] * jnp.power(mode_decay[None], row_times[:, None, None])
    long_part = local_part + jnp.einsum("tnc,nc->tc", entry_weights, entering, precision=highest)
    gated = (featured[:, 0] * long_part).astype(jnp.bfloat16)
    out_term = jnp.dot(gated, w_out, preferred_element_type=jnp.float32)
    return lax.psum_scatter(out_term.astype(jnp.bfloat16), "dp", scatter_dimension=1, tiled=True)


def project_kernel(order, *refs, pieces):
    x_refs, (own_ref, other_ref, out_ref, rows) = refs[:pieces], refs[pieces:]
    high = x_refs[0].shape[0]
    depth = own_ref.shape[1]
    half = out_ref.shape[-1]

    @pl.when((pl.program_id(0) == 0) & (pl.program_id(1) == 0))
    def _():
        for i, x_ref in enumerate(x_refs):
            rows[pl.ds(pl.multiple_of(order[i] * high, high), high), :] = x_ref[...]

    total = jnp.dot(rows[:, :depth], own_ref[0], preferred_element_type=F32)
    total += jnp.dot(rows[:, depth:], other_ref[0], preferred_element_type=F32)
    core = order[2 * pieces]
    for h in range(2):
        out_ref[0, core ^ h] = total[:, h * half : (h + 1) * half].astype(out_ref.dtype)


def project(order, xs, own, other, slots, kind):
    pieces = len(xs)
    streams, depth, chans = own.shape
    high = xs[0].shape[0]
    wide = chans // pieces
    half = wide // 2
    first = slots[0]
    step = slots[1] - slots[0] if len(slots) > 1 else 0
    weight = pl.BlockSpec(
        (1, depth, wide), lambda s, g, order: (g, 0, order[pieces + first + step * s])
    )
    return pl.pallas_call(
        functools.partial(project_kernel, pieces=pieces),
        out_shape=jax.ShapeDtypeStruct((len(slots), 2, pieces * high, streams * half), kind),
        grid_spec=pltpu.PrefetchScalarGridSpec(
            num_scalar_prefetch=1,
            grid=(len(slots), streams),
            in_specs=[pl.BlockSpec(x.shape, lambda s, g, order: (0, 0)) for x in xs]
            + [weight, weight],
            out_specs=pl.BlockSpec(
                (1, 2, pieces * high, half), lambda s, g, order: (s, 0, 0, g)
            ),
            scratch_shapes=[pltpu.VMEM((pieces * high, 2 * depth), BF16)],
        ),
        compiler_params=pltpu.CompilerParams(vmem_limit_bytes=VMEM_LIMIT),
        cost_estimate=pl.CostEstimate(
            flops=2 * len(slots) * pieces * high * 2 * depth * streams * wide,
            bytes_accessed=len(slots) * 2 * depth * streams * wide * 2,
            transcendentals=0,
        ),
        name="project",
    )(order, *xs, own, other)


def hyena_kernel(
    core, own_ref, near_ref, far_ref, swap_ref, filt_ref, decay_ref, residue_ref,
    out_ref, rows, mixed_s, gate_s, state, enter, edge, *, blocks,
):
    high = rows.shape[1] // blocks
    chans = rows.shape[2]
    modes = decay_ref.shape[0]
    taps = filt_ref.shape[0]
    mine = core[0]

    def place(p, _):
        here = pl.ds(pl.multiple_of(p * high, high), high)
        own_at = pl.ds(pl.multiple_of((2 * p + mine) * high, high), high)
        swap_at = pl.ds(pl.multiple_of((2 * p + 1 - mine) * high, high), high)
        for g in range(3):
            lanes = slice(g * chans, (g + 1) * chans)
            rows[g, own_at, :] = (
                own_ref[here, lanes]
                + near_ref[here, lanes].astype(F32)
                + far_ref[here, lanes].astype(F32)
            )
            rows[g, swap_at, :] = swap_ref[here, lanes].astype(F32)
        return 0

    lax.fori_loop(0, blocks // 2, place, 0)

    for k in range(1, taps):
        for g in range(3):
            edge[k - 1, g, 0:1, :] = jnp.zeros((1, chans), F32)
            for b in range(1, blocks):
                edge[k - 1, g, b : b + 1, :] = rows[g, b * high - k : b * high - k + 1, :]

    decay = [jnp.broadcast_to(decay_ref[n : n + 1, :], (blocks, chans)) for n in range(modes)]
    filt = [
        [jnp.broadcast_to(filt_ref[j, g : g + 1, :], (blocks, chans)) for g in range(3)]
        for j in range(taps)
    ]

    def first_pass(t, carry):
        states, earlier = carry
        now = [rows[g, pl.ds(t, blocks, stride=high), :] for g in range(3)]
        featured = []
        for g in range(3):
            value = filt[0][g] * now[g]
            for k in range(1, taps):
                value = value + filt[k][g] * earlier[k - 1][g]
            featured.append(value)
        mixed = (featured[1] * featured[2]).astype(BF16).astype(F32)
        mixed_s[t] = mixed
        gate_s[t] = featured[0]
        states = tuple(decay[n] * states[n] + mixed for n in range(modes))
        return states, (tuple(now),) + tuple(earlier[:-1])

    zeros = tuple(jnp.zeros((blocks, chans), F32) for _ in range(modes))
    before = tuple(tuple(edge[k, g] for g in range(3)) for k in range(taps - 1))
    states, _ = lax.fori_loop(0, high, first_pass, (zeros, before), unroll=4)
    for n in range(modes):
        state[n * blocks : (n + 1) * blocks, :] = states[n]

    rate = decay_ref[...]
    across = jnp.ones_like(rate)
    power, left = rate, high
    while left:
        if left & 1:
            across = across * power
        left >>= 1
        if left:
            power = power * power
    entering = jnp.zeros((modes, chans), F32)
    for b in range(blocks):
        enter[pl.ds(b, modes, stride=blocks), :] = entering
        entering = across * entering + state[pl.ds(b, modes, stride=blocks), :]

    gain = residue_ref[...] * jnp.sqrt(1.0 - rate * rate)
    gains = [jnp.broadcast_to(gain[n : n + 1, :], (blocks, chans)) for n in range(modes)]

    def second_pass(t, states):
        mixed = mixed_s[t]
        states = tuple(decay[n] * states[n] + mixed for n in range(modes))
        terms = [gains[n] * states[n] for n in range(modes)]
        while len(terms) > 1:
            terms = [sum(terms[i : i + 2][1:], terms[i]) for i in range(0, len(terms), 2)]
        rows[0, pl.ds(t, blocks, stride=high), :] = gate_s[t] * terms[0]
        return states

    begin = tuple(enter[n * blocks : (n + 1) * blocks, :] for n in range(modes))
    lax.fori_loop(0, high, second_pass, begin, unroll=4)
    out_ref[...] = rows[0].astype(BF16)


def hyena(core, own, near, far, swap, short_filter, mode_decay, residue, blocks):
    rows_count, lanes = own.shape
    chans = lanes // 3
    total = 2 * rows_count
    high = total // blocks
    modes = mode_decay.shape[0]
    taps = short_filter.shape[0]
    whole = pl.BlockSpec(memory_space=pltpu.VMEM)
    return pl.pallas_call(
        functools.partial(hyena_kernel, blocks=blocks),
        out_shape=jax.ShapeDtypeStruct((total, chans), BF16),
        in_specs=[pl.BlockSpec(memory_space=pltpu.SMEM)] + [whole] * 7,
        out_specs=whole,
        scratch_shapes=[
            pltpu.VMEM((3, total, chans), F32),
            pltpu.VMEM((high, blocks, chans), F32),
            pltpu.VMEM((high, blocks, chans), F32),
            pltpu.VMEM((modes * blocks, chans), F32),
            pltpu.VMEM((modes * blocks, chans), F32),
            pltpu.VMEM((taps - 1, 3, blocks, chans), F32),
        ],
        compiler_params=pltpu.CompilerParams(vmem_limit_bytes=VMEM_LIMIT),
        cost_estimate=pl.CostEstimate(
            flops=total * chans * 60, bytes_accessed=total * chans * 20, transcendentals=0
        ),
        name="hyena",
    )(core, own, near, far, swap, short_filter, mode_decay, residue)


def out_kernel(pick, x_ref, w_ref, out_ref):
    out_ref[...] = jnp.dot(x_ref[...], w_ref[...], preferred_element_type=F32).astype(out_ref.dtype)


def out_columns(pick, x, w, groups, kind):
    rows, depth = x.shape
    wide = w.shape[1] // groups
    tile = min(wide, 512)
    tiles = wide // tile
    return pl.pallas_call(
        out_kernel,
        out_shape=jax.ShapeDtypeStruct((rows, wide), kind),
        grid_spec=pltpu.PrefetchScalarGridSpec(
            num_scalar_prefetch=1,
            grid=(tiles,),
            in_specs=[
                pl.BlockSpec((rows, depth), lambda i, pick: (0, 0)),
                pl.BlockSpec((depth, tile), lambda i, pick: (0, pick[0] * tiles + i)),
            ],
            out_specs=pl.BlockSpec((rows, tile), lambda i, pick: (0, i)),
        ),
        compiler_params=pltpu.CompilerParams(vmem_limit_bytes=VMEM_LIMIT),
        cost_estimate=pl.CostEstimate(
            flops=2 * rows * depth * wide, bytes_accessed=depth * wide * 2, transcendentals=0
        ),
        name="out_columns",
    )(pick, x, w)


def output_over_line(gated, w_out):
    z = lax.axis_index("dp")
    table = jnp.array([[3, 0, 3, 0], [1, 2, 1, 2], [2, 3, 0, 1], [0, 1, 2, 3]], jnp.int32)
    picks = lax.dynamic_slice_in_dim(table, z, 1, 1)
    pair = out_columns(picks[0], gated, w_out, 4, BF16)
    pair_in = lax.ppermute(pair, "dp", [(0, 1), (1, 0), (2, 3), (3, 2)])
    side = out_columns(picks[1], gated, w_out, 4, BF16)
    middle_in = lax.ppermute(side, "dp", [(1, 2), (2, 1)])
    far = out_columns(picks[2], gated, w_out, 4, F32)
    own = out_columns(picks[3], gated, w_out, 4, F32)
    inner = (z == 1) | (z == 2)
    pair_in = pair_in.astype(F32)
    far = jnp.where(inner, far + pair_in, far).astype(BF16)
    far_in = lax.ppermute(far, "dp", [(0, 2), (1, 3), (2, 0), (3, 1)])
    side_in = lax.ppermute(side, "dp", [(0, 1), (3, 2)])
    own = own + middle_in.astype(F32) + jnp.where(inner, 0.0, pair_in)
    return (own + far_in.astype(F32) + side_in.astype(F32)).astype(BF16)


def on_device_chips(tokens, w_in, short_filter, mode_decay, residue, w_out):
    count = lax.axis_size("ctx")
    chips = count // 2
    me = lax.axis_index("ctx")
    core, chip = me % 2, me // 2
    depth, streams, chans = w_in.shape
    part = chans // count

    def across(i, slot):
        high_bit, low_bit = slot >> 1, slot & 1
        step = (high_bit + 2 * low_bit) if i % 2 == 0 else (2 * high_bit + low_bit)
        return i ^ (2 * step)

    def route(slot):
        return [(i, across(i, slot)) for i in range(count)]

    def relative(slot):
        high_bit, low_bit = slot >> 1, slot & 1
        return jnp.where(core == 0, high_bit + 2 * low_bit, 2 * high_bit + low_bit)

    slot_chip = [chip ^ relative(s) for s in range(chips)]
    order = jnp.stack(slot_chip + slot_chip + [core]).astype(jnp.int32)

    own_w = jnp.transpose(w_in, (1, 0, 2))
    swap = [(i, i ^ 1) for i in range(count)]
    other_w = lax.ppermute(own_w, "ctx", swap)

    xs = []
    for s in range(chips):
        block = jnp.concatenate(
            [
                lax.dynamic_slice_in_dim(tokens, (2 * slot_chip[s] + (core ^ h)) * depth, depth, 1)
                for h in range(2)
            ],
            1,
        )
        xs.append(block if s == 0 else lax.ppermute(block, "ctx", route(s)))

    both = project(order, xs, own_w, other_w, [3], BF16)
    both_in = lax.ppermute(both, "ctx", route(2))
    first = project(order, xs, own_w, other_w, [2], BF16)
    first_in = lax.ppermute(first, "ctx", route(2))
    second = project(order, xs, own_w, other_w, [1], F32)
    own = project(order, xs, own_w, other_w, [0], F32)[0]
    second = (second + both_in.astype(F32)).astype(BF16)[0]
    second_in = [lax.ppermute(second[h], "ctx", route(1)) for h in (1, 0)][::-1]
    first_in = first_in[0]
    other_half = (own[1] + first_in[1].astype(F32) + second_in[1].astype(F32)).astype(BF16)
    other_half = lax.ppermute(other_half, "ctx", swap)

    here = me * part
    taps = lax.dynamic_slice_in_dim(short_filter, here, part, 2)
    decay = lax.dynamic_slice_in_dim(mode_decay, here, part, 1)
    weight = lax.dynamic_slice_in_dim(residue, here, part, 1)
    gated = hyena(
        core.astype(jnp.int32)[None], own[0], first_in[0], second_in[0], other_half,
        taps, decay, weight, count,
    )
    gated = lax.all_to_all(gated, "ctx", 0, 1, tiled=True)
    return output_over_line(gated, w_out)


def solution(mesh):
    count, groups = mesh.shape["ctx"], mesh.shape["dp"]

    def on_device(tokens, w_in, *rest):
        lanes = w_in.shape[2] // count
        chips = count == 8 and groups == 4 and w_in.shape[2] % count == 0 and lanes % 128 == 0
        return (on_device_chips if chips else on_device_any)(tokens, w_in, *rest)

    return jax.shard_map(
        on_device,
        mesh=mesh,
        in_specs=(
            P("ctx", None),
            P("ctx", None, "dp"),
            P(None, None, "dp"),
            P(None, "dp"),
            P(None, "dp"),
            P("dp", None),
        ),
        out_specs=P("ctx", "dp"),
        check_vma=False,
    )
```

```python
import functools

import jax
import jax.numpy as jnp
from jax import lax
from jax.experimental import pallas as pl
from jax.experimental.pallas import tpu as pltpu
from jax.sharding import PartitionSpec as P

BLK = 64
F32, BF16 = jnp.float32, jnp.bfloat16
VMEM_LIMIT = 12 * 1024 * 1024


def from_behind(block, axis, distance):
    devices = range(lax.axis_size(axis))
    route = [(i - distance, i) for i in devices if i - distance in devices]
    return lax.ppermute(block, axis, route)


def prefix(value, axis, join, neutral):
    count, mine = (lax.axis_size(axis), lax.axis_index(axis))
    pieces = jax.tree.map(lambda part: lax.all_gather(part, axis), value)
    subtotal = jax.tree.map(
        lambda part, zero: jnp.full_like(part, 0) + jnp.asarray(zero, part.dtype), value, neutral
    )

    def lap(position, subtotal):
        longer = join(subtotal, jax.tree.map(lambda part: part[position], pieces))
        return jax.tree.map(lambda new, old: jnp.where(position < mine, new, old), longer, subtotal)

    return lax.fori_loop(0, count - 1, lap, subtotal)


def on_device_any(tokens, w_in, short_filter, mode_decay, residue, w_out):
    row_count = tokens.shape[0]
    chan_count = w_in.shape[2]
    short_count = short_filter.shape[0]
    mode_count = mode_decay.shape[0]
    earlier_rows = from_behind(tokens[row_count - (short_count - 1) :], "ctx", 1)
    source = jnp.concatenate([earlier_rows, tokens], 0)
    projected = jnp.einsum(
        "td,dgc->tgc",
        source,
        lax.all_gather(w_in, "ctx", axis=0, tiled=True),
        preferred_element_type=jnp.float32,
    )
    featured = jnp.zeros((row_count, 3, chan_count), jnp.float32)
    for j in range(short_count):
        featured = (
            featured
            + short_filter[j] * projected[short_count - 1 - j : short_count - 1 - j + row_count]
        )
    mixed = (featured[:, 1] * featured[:, 2]).astype(jnp.bfloat16)
    medium = mixed.astype(jnp.float32)
    highest = lax.Precision.HIGHEST
    mode_gain = residue * jnp.sqrt(1.0 - mode_decay * mode_decay)
    block_len = BLK
    block_times = jnp.arange(block_len).astype(jnp.float32)
    power_in = jnp.power(mode_decay[None], block_times[:, None, None])
    kernel_head = jnp.sum(mode_gain[None] * power_in, 1)
    lag_index = jnp.arange(block_len)[:, None] - jnp.arange(block_len)[None, :]
    toeplitz = jnp.where(
        (lag_index >= 0)[:, :, None], kernel_head[jnp.clip(lag_index, 0, block_len - 1)], 0.0
    )
    carry_weights = mode_gain[None] * power_in * mode_decay[None]
    state_weights = power_in[::-1]
    decay_block = jnp.power(mode_decay, float(block_len))
    blocks = medium.reshape(row_count // block_len, block_len, chan_count)

    def block_step(carried, block_rows):
        inner = jnp.einsum("tsc,sc->tc", toeplitz, block_rows, precision=highest)
        inner = inner + jnp.einsum("tnc,nc->tc", carry_weights, carried, precision=highest)
        carried = decay_block * carried + jnp.einsum(
            "snc,sc->nc", state_weights, block_rows, precision=highest
        )
        return (carried, inner)

    zero_state = jnp.zeros((mode_count, chan_count), jnp.float32)
    local_end, local_part = lax.scan(block_step, zero_state, blocks)
    local_part = local_part.reshape(row_count, chan_count)
    decay_device = jnp.power(mode_decay, float(row_count))

    def combine_states(earlier, later):
        return (earlier[0] * later[0], later[0] * earlier[1] + later[1])

    identity = (jnp.ones((mode_count, chan_count), jnp.float32), zero_state)
    scanned = prefix((decay_device, local_end), "ctx", combine_states, identity)
    entering = scanned[1]
    row_times = jnp.arange(1, row_count + 1).astype(jnp.float32)
    entry_weights = mode_gain[None] * jnp.power(mode_decay[None], row_times[:, None, None])
    long_part = local_part + jnp.einsum("tnc,nc->tc", entry_weights, entering, precision=highest)
    gated = (featured[:, 0] * long_part).astype(jnp.bfloat16)
    out_term = jnp.dot(gated, w_out, preferred_element_type=jnp.float32)
    return lax.psum_scatter(out_term.astype(jnp.bfloat16), "dp", scatter_dimension=1, tiled=True)


def local(kernel, name, shapes, scalars, arrays, scratch=()):
    whole = pl.BlockSpec(memory_space=pltpu.VMEM)
    out = [jax.ShapeDtypeStruct(*shape) for shape in shapes]
    return pl.pallas_call(
        kernel,
        out_shape=out if len(out) > 1 else out[0],
        in_specs=[pl.BlockSpec(memory_space=pltpu.SMEM)] + [whole] * len(arrays),
        out_specs=[whole] * len(out) if len(out) > 1 else whole,
        scratch_shapes=list(scratch),
        compiler_params=pltpu.CompilerParams(vmem_limit_bytes=VMEM_LIMIT),
        name=name,
    )(scalars, *arrays)


def columns(index, wide):
    return pl.ds(pl.multiple_of(index * wide, wide), wide)


def cut(order, tokens, pieces):
    high, wide = tokens.shape[0], tokens.shape[1] // pieces

    def kernel(order, tokens_ref, *out_refs):
        for s, out_ref in enumerate(out_refs):
            out_ref[...] = tokens_ref[:, columns(order[s], wide)]

    return local(kernel, "cut", [((high, wide), tokens.dtype)] * pieces, order, [tokens])


def stage(*arrays):
    count = len(arrays)

    def kernel(*refs):
        sems = refs[2 * count]
        copies = [
            pltpu.make_async_copy(refs[i], refs[count + i], sems.at[i]) for i in range(count)
        ]
        for copy in copies:
            copy.start()
        for copy in copies:
            copy.wait()

    return pl.pallas_call(
        kernel,
        out_shape=[jax.ShapeDtypeStruct(x.shape, x.dtype) for x in arrays],
        in_specs=[pl.BlockSpec(memory_space=pl.ANY)] * count,
        out_specs=[pl.BlockSpec(memory_space=pltpu.VMEM)] * count,
        scratch_shapes=[pltpu.SemaphoreType.DMA((count,))],
        compiler_params=pltpu.CompilerParams(vmem_limit_bytes=VMEM_LIMIT),
        name="stage",
    )(*arrays)


def gather_rows(core, x_refs, rows):
    high, depth = x_refs[0].shape[0], rows.shape[2]
    for i, x_ref in enumerate(x_refs):
        for h in range(2):
            rows[core ^ h, i * high : (i + 1) * high, :] = x_ref[:, h * depth : (h + 1) * depth]


def project_mix(order, xs, own, other, slots, kind):
    chips = len(xs)
    streams, depth, chans = own.shape
    high = xs[0].shape[0]
    wide = chans // chips
    half = wide // 2

    def kernel(order, *refs):
        x_refs, (own_ref, other_ref, out_ref, rows) = refs[:chips], refs[chips:]
        core = order[2 * chips]
        gather_rows(core, x_refs, rows)
        for i, slot in enumerate(slots):
            at = columns(order[slot], wide)
            for g in range(1, streams):
                total = jnp.dot(rows[0], own_ref[g, :, at], preferred_element_type=F32)
                total += jnp.dot(rows[1], other_ref[g, :, at], preferred_element_type=F32)
                total = total.astype(kind)
                lanes = slice((g - 1) * half, g * half)
                for h in range(2):
                    out_ref[i, core ^ h, :, lanes] = total[:, h * half : (h + 1) * half]

    shape = (len(slots), 2, chips * high, (streams - 1) * half)
    scratch = [pltpu.VMEM((2, chips * high, depth), BF16)]
    return local(kernel, "project_mix", [(shape, kind)], order, [*xs, own, other], scratch)


def last_rows(order, xs, count):
    high, wide = xs[0].shape

    def kernel(order, *refs):
        for s in range(len(xs)):
            refs[-1][s] = refs[s][high - count :, :]

    return local(kernel, "last_rows", [((len(xs), count, wide), BF16)], order, xs)


def project_query(order, xs, before, own, other, short_filter):
    chips = len(xs)
    _, depth, chans = own.shape
    high = xs[0].shape[0]
    some = before.shape[1]
    step = some + high
    taps = short_filter.shape[0]
    tile = min(chans, 256)

    def kernel(order, *refs):
        x_refs = refs[:chips]
        before_ref, own_ref, other_ref, filt_ref, sent_ref, rest_ref, rows, ends, total = refs[chips:]
        core = order[2 * chips]
        ends[0] = jnp.zeros_like(ends[0])
        for s in range(chips):
            ends[order[chips + s] + 1] = before_ref[s]
        for i, x_ref in enumerate(x_refs):
            end = ends[order[i] + core]
            for h in range(2):
                lanes = slice(h * depth, (h + 1) * depth)
                rows[core ^ h, i * step : i * step + some, :] = end[:, lanes]
                rows[core ^ h, i * step + some : (i + 1) * step, :] = x_ref[:, lanes]
        for at in (slice(i, i + tile) for i in range(0, chans, tile)):
            total[...] = jnp.dot(
                rows[0], own_ref[0, :, at], preferred_element_type=F32
            ) + jnp.dot(rows[1], other_ref[0, :, at], preferred_element_type=F32)
            for i in range(chips):
                first = i * step + some
                value = filt_ref[0, 0:1, at] * total[first : first + high, :]
                for j in range(1, taps):
                    value = value + filt_ref[j, 0:1, at] * total[first - j : first - j + high, :]
                if i < 2:
                    rest_ref[i, :, at] = value
                else:
                    sent_ref[3 - i, :, at] = value.astype(BF16)

    shapes = [((2, high, chans), BF16), ((2, high, chans), F32)]
    scratch = [
        pltpu.VMEM((2, chips * step, depth), BF16),
        pltpu.VMEM((chips + 1, some, 2 * depth), BF16),
        pltpu.VMEM((chips * step, tile), F32),
    ]
    arrays = [*xs, before, own, other, short_filter]
    return local(kernel, "project_query", shapes, order, arrays, scratch)


def second_share(order, rest, both_in, chips):
    shape = (1,) + rest.shape[1:]
    high = rest.shape[2] // chips

    def kernel(order, rest_ref, both_ref, out_ref):
        for h in range(2):
            for s in range(chips):
                here, there = (slice(i * high, (i + 1) * high) for i in (s, s ^ 2))
                term = both_ref[0, h, there, :].astype(F32)
                out_ref[0, h, here, :] = (rest_ref[0, h, here, :] + term).astype(BF16)

    return local(kernel, "second_share", [(shape, BF16)], order, [rest, both_in])


def own_share(order, rest, first_in, second_in, chips):
    _, _, rows, lanes = rest.shape
    high = rows // chips

    def kernel(order, rest_ref, first_ref, second_ref, own_ref, other_ref):
        for h, out_ref in ((1, other_ref), (0, own_ref)):
            for s in range(chips):
                here, first, second = (slice(i * high, (i + 1) * high) for i in (s, s ^ 2, s ^ 1))
                total = rest_ref[1, h, here, :] + first_ref[0, h, first, :].astype(F32)
                total = total + second_ref[0, h, second, :].astype(F32)
                out_ref[here, :] = total.astype(out_ref.dtype)

    shapes = [((rows, lanes), F32), ((rows, lanes), BF16)]
    return local(kernel, "own_share", shapes, order, [rest, first_in, second_in])


def hyena_kernel(
    order, own_ref, swap_ref, filt_ref, decay_ref, residue_ref,
    keep_ref, send_ref, rows, mixed_s, state, enter, edge, *, blocks,
):
    high = rows.shape[1] // blocks
    chans = rows.shape[2]
    modes = decay_ref.shape[0]
    taps = filt_ref.shape[0]
    chips = blocks // 2
    core = order[2 * chips]
    channels = columns(order[2 * chips + 1], chans)

    for s in range(chips):
        here = slice(s * high, (s + 1) * high)
        own_at = columns(2 * order[s] + core, high)
        swap_at = columns(2 * order[chips + s] + 1 - core, high)
        for g in range(2):
            lanes = slice(g * chans, (g + 1) * chans)
            rows[g, own_at, :] = own_ref[here, lanes]
            rows[g, swap_at, :] = swap_ref[here, lanes].astype(F32)

    for k in range(1, taps):
        for g in range(2):
            edge[k - 1, g, 0:1, :] = jnp.zeros((1, chans), F32)
            for b in range(1, blocks):
                edge[k - 1, g, b : b + 1, :] = rows[g, b * high - k : b * high - k + 1, :]

    rate = decay_ref[:, channels]
    taps_of = [filt_ref[j, :, channels] for j in range(taps)]
    decay = [jnp.broadcast_to(rate[n : n + 1, :], (blocks, chans)) for n in range(modes)]
    filt = [
        [jnp.broadcast_to(taps_of[j][g + 1 : g + 2, :], (blocks, chans)) for g in range(2)]
        for j in range(taps)
    ]

    def first_pass(t, carry):
        states, earlier = carry
        now = [rows[g, pl.ds(t, blocks, stride=high), :] for g in range(2)]
        featured = []
        for g in range(2):
            value = filt[0][g] * now[g]
            for k in range(1, taps):
                value = value + filt[k][g] * earlier[k - 1][g]
            featured.append(value)
        mixed = (featured[0] * featured[1]).astype(BF16).astype(F32)
        mixed_s[t] = mixed
        states = tuple(decay[n] * states[n] + mixed for n in range(modes))
        return states, (tuple(now),) + tuple(earlier[:-1])

    zeros = tuple(jnp.zeros((blocks, chans), F32) for _ in range(modes))
    before = tuple(tuple(edge[k, g] for g in range(2)) for k in range(taps - 1))
    states, _ = lax.fori_loop(0, high, first_pass, (zeros, before), unroll=4)
    for n in range(modes):
        state[n * blocks : (n + 1) * blocks, :] = states[n]

    across = jnp.ones_like(rate)
    power, left = rate, high
    while left:
        if left & 1:
            across = across * power
        left >>= 1
        if left:
            power = power * power
    entering = jnp.zeros((modes, chans), F32)
    for b in range(blocks):
        enter[pl.ds(b, modes, stride=blocks), :] = entering
        entering = across * entering + state[pl.ds(b, modes, stride=blocks), :]

    gain = residue_ref[:, channels] * jnp.sqrt(1.0 - rate * rate)
    gains = [jnp.broadcast_to(gain[n : n + 1, :], (blocks, chans)) for n in range(modes)]

    def second_pass(t, states):
        mixed = mixed_s[t]
        states = tuple(decay[n] * states[n] + mixed for n in range(modes))
        terms = [gains[n] * states[n] for n in range(modes)]
        while len(terms) > 1:
            terms = [sum(terms[i : i + 2][1:], terms[i]) for i in range(0, len(terms), 2)]
        rows[0, pl.ds(t, blocks, stride=high), :] = terms[0]
        return states

    begin = tuple(enter[n * blocks : (n + 1) * blocks, :] for n in range(modes))
    lax.fori_loop(0, high, second_pass, begin, unroll=4)
    for s in range(chips):
        keep_ref[s] = rows[0, columns(2 * order[s] + core, high), :].astype(BF16)
        send_ref[s] = rows[0, columns(2 * order[chips + s] + 1 - core, high), :].astype(BF16)


def hyena(order, own, swap, short_filter, mode_decay, residue, blocks):
    rows_count, lanes = own.shape
    chans = lanes // 2
    total = 2 * rows_count
    high = total // blocks
    modes, taps = mode_decay.shape[0], short_filter.shape[0]
    scratch = [
        pltpu.VMEM((2, total, chans), F32),
        pltpu.VMEM((high, blocks, chans), F32),
        pltpu.VMEM((modes * blocks, chans), F32),
        pltpu.VMEM((modes * blocks, chans), F32),
        pltpu.VMEM((taps - 1, 2, blocks, chans), F32),
    ]
    arrays = [own, swap, short_filter, mode_decay, residue]
    kernel = functools.partial(hyena_kernel, blocks=blocks)
    shapes = [((blocks // 2, high, chans), BF16)] * 2
    return local(kernel, "hyena", shapes, order, arrays, scratch)


def pair_up(order, keep, other):
    chips, high, chans = keep.shape

    def kernel(order, keep_ref, other_ref, *out_refs):
        for s, out_ref in enumerate(out_refs):
            out_ref[0] = keep_ref[s]
            out_ref[1] = other_ref[s]

    return local(kernel, "pair_up", [((2, high, chans), BF16)] * chips, order, [keep, other])


def query_second(order, rest, q_in, pieces):
    _, rows, chans = rest.shape
    share = chans // pieces

    def kernel(order, rest_ref, in_ref, *out_refs):
        for i, out_ref in enumerate(out_refs):
            at = slice(i * share, (i + 1) * share)
            out_ref[...] = (rest_ref[1, :, at] + in_ref[0, :, at].astype(F32)).astype(BF16)

    shapes = [((rows, share), BF16)] * pieces
    return local(kernel, "query_second", shapes, order, [rest, q_in])


def gate(scalars, rest, q_in, second_in, long_parts, w_out, groups):
    rows, chans = second_in[0].shape[0], rest.shape[2]
    chips = len(long_parts)
    part = long_parts[0].shape[2]
    wide = w_out.shape[1] // groups
    first_pick = 2 * chips + 2

    def kernel(scalars, rest_ref, in_ref, *refs):
        second_refs = refs[: len(second_in)]
        long_refs = refs[len(second_in) : len(second_in) + chips]
        w_ref, gated_ref, pair_ref, side_ref, query = refs[len(second_in) + chips :]
        core = scalars[2 * chips]
        query[...] = rest_ref[0] + in_ref[1].astype(F32)
        share = second_refs[0].shape[1]
        for i, ref in enumerate(second_refs):
            query[:, i * share : (i + 1) * share] += ref[...].astype(F32)
        for s, ref in enumerate(long_refs):
            for h in range(2):
                at = columns(2 * scalars[s] + (core ^ h), part)
                gated_ref[:, at] = (query[:, at] * ref[h].astype(F32)).astype(BF16)
        for pick, out_ref in enumerate((pair_ref, side_ref)):
            total = jnp.dot(
                gated_ref[...],
                w_ref[:, columns(scalars[first_pick + pick], wide)],
                preferred_element_type=F32,
            )
            out_ref[...] = total.astype(BF16)

    shapes = [((rows, chans), BF16), ((rows, wide), BF16), ((rows, wide), BF16)]
    arrays = [rest, q_in, *second_in, *long_parts, w_out]
    scratch = [pltpu.VMEM((rows, chans), F32)]
    return local(kernel, "gate", shapes, scalars, arrays, scratch)


def out_columns(picks, pick, x, w_out, groups, kind):
    wide = w_out.shape[1] // groups

    def kernel(picks, x_ref, w_ref, out_ref):
        total = jnp.dot(
            x_ref[...], w_ref[:, columns(picks[pick], wide)], preferred_element_type=F32
        )
        out_ref[...] = total.astype(kind)

    return local(kernel, "out_columns", [((x.shape[0], wide), kind)], picks, [x, w_out])


def line_picks():
    z = lax.axis_index("dp")
    table = [[3, 0, 3, 0], [1, 2, 1, 2], [2, 3, 0, 1], [0, 1, 2, 3], [0, 1, 1, 0]]
    return jnp.stack([sum(jnp.where(z == i, v, 0) for i, v in enumerate(row)) for row in table])


def output_over_line(picks, gated, pair, side, w_out, groups):
    pair_in = lax.ppermute(pair, "dp", [(0, 1), (1, 0), (2, 3), (3, 2)])
    far = out_columns(picks, 2, gated, w_out, groups, BF16)
    end_in = lax.ppermute(far, "dp", [(0, 2), (3, 1)])
    middle_in = lax.ppermute(side, "dp", [(1, 2), (2, 1)])
    side_in = lax.ppermute(side, "dp", [(0, 1), (3, 2)])
    own = out_columns(picks, 3, gated, w_out, groups, F32)

    def add(picks, far_ref, pair_ref, out_ref):
        out_ref[...] = (far_ref[...].astype(F32) + pair_ref[...].astype(F32)).astype(BF16)

    both = local(add, "both", [(far.shape, BF16)], picks, [far, pair_in])
    far_in = lax.ppermute(both, "dp", [(1, 3), (2, 0)])

    def total(picks, own_ref, pair_ref, *refs):
        out_ref = refs[-1]
        inner = picks[4] == 1
        value = own_ref[...] + jnp.where(inner, 0.0, pair_ref[...].astype(F32))
        for ref in refs[:-1]:
            value = value + ref[...].astype(F32)
        out_ref[...] = value.astype(BF16)

    arrays = [own, pair_in, middle_in, end_in, side_in, far_in]
    return local(total, "total", [(own.shape, BF16)], picks, arrays)


def on_device_chips(tokens, w_in, short_filter, mode_decay, residue, w_out):
    count, groups = lax.axis_size("ctx"), lax.axis_size("dp")
    chips = count // 2
    me = lax.axis_index("ctx")
    core, chip = me % 2, me // 2

    def across(i, slot):
        high_bit, low_bit = slot >> 1, slot & 1
        step = (high_bit + 2 * low_bit) if i % 2 == 0 else (2 * high_bit + low_bit)
        return i ^ (2 * step)

    def route(slot):
        return [(i, across(i, slot)) for i in range(count)]

    def relative(slot, core):
        high_bit, low_bit = slot >> 1, slot & 1
        return jnp.where(core == 0, high_bit + 2 * low_bit, 2 * high_bit + low_bit)

    slot_chip = [chip ^ relative(s, core) for s in range(chips)]
    slot_other = [chip ^ relative(s, 1 - core) for s in range(chips)]
    order = jnp.stack(slot_chip + slot_other + [core, me]).astype(jnp.int32)
    picks = line_picks().astype(jnp.int32)
    both_scalars = jnp.concatenate([order, picks])
    order, picks, both_scalars = lax.optimization_barrier((order, picks, both_scalars))

    own_w = jnp.transpose(w_in, (1, 0, 2))
    swap = [(i, i ^ 1) for i in range(count)]

    other_w = lax.ppermute(own_w, "ctx", swap)
    xs = cut(order, tokens, chips)
    own_w, w_out, xs = lax.optimization_barrier((own_w, w_out, xs))
    own_w, w_out = stage(own_w, w_out)
    xs = [xs[0]] + [lax.ppermute(xs[s], "ctx", route(s)) for s in (1, 2, 3)]

    both = project_mix(order, xs, own_w, other_w, [3], BF16)
    both_in = lax.ppermute(both, "ctx", route(2))
    xs, both = lax.optimization_barrier((xs, both))
    first = project_mix(order, xs, own_w, other_w, [2], BF16)
    first_in = lax.ppermute(first, "ctx", route(2))
    xs, first = lax.optimization_barrier((xs, first))
    rest = project_mix(order, xs, own_w, other_w, [1, 0], F32)
    second = second_share(order, rest, both_in, chips)
    second_in = lax.ppermute(second, "ctx", route(1))

    xs, second = lax.optimization_barrier((xs, second))
    before = lax.ppermute(last_rows(order, xs, 16), "ctx", swap)
    q_sent, q_rest = project_query(order, xs, before, own_w, other_w, short_filter)
    q_rest, rest = lax.optimization_barrier((q_rest, rest))

    own, other_half = own_share(order, rest, first_in, second_in, chips)
    other_half = lax.ppermute(other_half, "ctx", swap)
    q_sent, own = lax.optimization_barrier((q_sent, own))
    q_in = lax.ppermute(q_sent, "ctx", route(2))
    keep, send = hyena(order, own, other_half, short_filter, mode_decay, residue, count)
    long_parts = pair_up(order, keep, lax.ppermute(send, "ctx", swap))
    q_rest, long_parts = lax.optimization_barrier((q_rest, long_parts))
    q_second = [lax.ppermute(q, "ctx", route(1)) for q in query_second(order, q_rest, q_in, 2)]
    long_parts = [long_parts[0]] + [lax.ppermute(long_parts[s], "ctx", route(s)) for s in (1, 2, 3)]
    gated, pair, side = gate(both_scalars, q_rest, q_in, q_second, long_parts, w_out, groups)
    return output_over_line(picks, gated, pair, side, w_out, groups)


def solution(mesh):
    count, groups = mesh.shape["ctx"], mesh.shape["dp"]

    def on_device(tokens, w_in, *rest):
        lanes = w_in.shape[2] // count
        chips = count == 8 and groups == 4 and w_in.shape[2] % count == 0 and lanes % 128 == 0
        return (on_device_chips if chips else on_device_any)(tokens, w_in, *rest)

    return jax.shard_map(
        on_device,
        mesh=mesh,
        in_specs=(
            P("ctx", None),
            P("ctx", None, "dp"),
            P(None, None, "dp"),
            P(None, "dp"),
            P(None, "dp"),
            P("dp", None),
        ),
        out_specs=P("ctx", "dp"),
        check_vma=False,
    )
```

```python
import functools

import jax
import jax.numpy as jnp
from jax import lax
from jax.experimental import pallas as pl
from jax.experimental.pallas import tpu as pltpu
from jax.sharding import PartitionSpec as P

BLK = 64
F32, BF16 = jnp.float32, jnp.bfloat16
VMEM_LIMIT = 12 * 1024 * 1024


def from_behind(block, axis, distance):
    devices = range(lax.axis_size(axis))
    route = [(i - distance, i) for i in devices if i - distance in devices]
    return lax.ppermute(block, axis, route)


def prefix(value, axis, join, neutral):
    count, mine = (lax.axis_size(axis), lax.axis_index(axis))
    pieces = jax.tree.map(lambda part: lax.all_gather(part, axis), value)
    subtotal = jax.tree.map(
        lambda part, zero: jnp.full_like(part, 0) + jnp.asarray(zero, part.dtype), value, neutral
    )

    def lap(position, subtotal):
        longer = join(subtotal, jax.tree.map(lambda part: part[position], pieces))
        return jax.tree.map(lambda new, old: jnp.where(position < mine, new, old), longer, subtotal)

    return lax.fori_loop(0, count - 1, lap, subtotal)


def on_device_any(tokens, w_in, short_filter, mode_decay, residue, w_out):
    row_count = tokens.shape[0]
    chan_count = w_in.shape[2]
    short_count = short_filter.shape[0]
    mode_count = mode_decay.shape[0]
    earlier_rows = from_behind(tokens[row_count - (short_count - 1) :], "ctx", 1)
    source = jnp.concatenate([earlier_rows, tokens], 0)
    projected = jnp.einsum(
        "td,dgc->tgc",
        source,
        lax.all_gather(w_in, "ctx", axis=0, tiled=True),
        preferred_element_type=jnp.float32,
    )
    featured = jnp.zeros((row_count, 3, chan_count), jnp.float32)
    for j in range(short_count):
        featured = (
            featured
            + short_filter[j] * projected[short_count - 1 - j : short_count - 1 - j + row_count]
        )
    mixed = (featured[:, 1] * featured[:, 2]).astype(jnp.bfloat16)
    medium = mixed.astype(jnp.float32)
    highest = lax.Precision.HIGHEST
    mode_gain = residue * jnp.sqrt(1.0 - mode_decay * mode_decay)
    block_len = BLK
    block_times = jnp.arange(block_len).astype(jnp.float32)
    power_in = jnp.power(mode_decay[None], block_times[:, None, None])
    kernel_head = jnp.sum(mode_gain[None] * power_in, 1)
    lag_index = jnp.arange(block_len)[:, None] - jnp.arange(block_len)[None, :]
    toeplitz = jnp.where(
        (lag_index >= 0)[:, :, None], kernel_head[jnp.clip(lag_index, 0, block_len - 1)], 0.0
    )
    carry_weights = mode_gain[None] * power_in * mode_decay[None]
    state_weights = power_in[::-1]
    decay_block = jnp.power(mode_decay, float(block_len))
    blocks = medium.reshape(row_count // block_len, block_len, chan_count)

    def block_step(carried, block_rows):
        inner = jnp.einsum("tsc,sc->tc", toeplitz, block_rows, precision=highest)
        inner = inner + jnp.einsum("tnc,nc->tc", carry_weights, carried, precision=highest)
        carried = decay_block * carried + jnp.einsum(
            "snc,sc->nc", state_weights, block_rows, precision=highest
        )
        return (carried, inner)

    zero_state = jnp.zeros((mode_count, chan_count), jnp.float32)
    local_end, local_part = lax.scan(block_step, zero_state, blocks)
    local_part = local_part.reshape(row_count, chan_count)
    decay_device = jnp.power(mode_decay, float(row_count))

    def combine_states(earlier, later):
        return (earlier[0] * later[0], later[0] * earlier[1] + later[1])

    identity = (jnp.ones((mode_count, chan_count), jnp.float32), zero_state)
    scanned = prefix((decay_device, local_end), "ctx", combine_states, identity)
    entering = scanned[1]
    row_times = jnp.arange(1, row_count + 1).astype(jnp.float32)
    entry_weights = mode_gain[None] * jnp.power(mode_decay[None], row_times[:, None, None])
    long_part = local_part + jnp.einsum("tnc,nc->tc", entry_weights, entering, precision=highest)
    gated = (featured[:, 0] * long_part).astype(jnp.bfloat16)
    out_term = jnp.dot(gated, w_out, preferred_element_type=jnp.float32)
    return lax.psum_scatter(out_term.astype(jnp.bfloat16), "dp", scatter_dimension=1, tiled=True)


def local(kernel, name, shapes, scalars, arrays, scratch=()):
    whole = pl.BlockSpec(memory_space=pltpu.VMEM)
    out = [jax.ShapeDtypeStruct(*shape) for shape in shapes]
    return pl.pallas_call(
        kernel,
        out_shape=out if len(out) > 1 else out[0],
        in_specs=[pl.BlockSpec(memory_space=pltpu.SMEM)] + [whole] * len(arrays),
        out_specs=[whole] * len(out) if len(out) > 1 else whole,
        scratch_shapes=list(scratch),
        compiler_params=pltpu.CompilerParams(vmem_limit_bytes=VMEM_LIMIT),
        name=name,
    )(scalars, *arrays)


def columns(index, wide):
    return pl.ds(pl.multiple_of(index * wide, wide), wide)


def cut(order, tokens, pieces):
    high, wide = tokens.shape[0], tokens.shape[1] // pieces

    def part(order, tokens_ref, out_ref):
        here = columns(order[2 * pieces + 2], high // 2)
        out_ref[...] = tokens_ref[here, columns(order[pieces - 1], wide)]

    def rest(order, tokens_ref, *out_refs):
        for s, out_ref in enumerate(out_refs):
            out_ref[...] = tokens_ref[:, columns(order[s], wide)]

    last = local(part, "cut_part", [((high // 2, wide), tokens.dtype)], order, [tokens])
    last, tokens = lax.optimization_barrier((last, tokens))
    shapes = [((high, wide), tokens.dtype)] * (pieces - 1)
    return [*local(rest, "cut", shapes, order, [tokens]), last]


def join_rows(order, mine, other):
    half, wide = mine.shape
    at = order.shape[0] - 1

    def kernel(order, mine_ref, other_ref, out_ref):
        out_ref[columns(order[at], half), :] = mine_ref[...]
        out_ref[columns(1 - order[at], half), :] = other_ref[...]

    return local(kernel, "join_rows", [((2 * half, wide), mine.dtype)], order, [mine, other])


def stage(*arrays):
    count = len(arrays)

    def kernel(*refs):
        sems = refs[2 * count]
        copies = [
            pltpu.make_async_copy(refs[i], refs[count + i], sems.at[i]) for i in range(count)
        ]
        for copy in copies:
            copy.start()
        for copy in copies:
            copy.wait()

    return pl.pallas_call(
        kernel,
        out_shape=[jax.ShapeDtypeStruct(x.shape, x.dtype) for x in arrays],
        in_specs=[pl.BlockSpec(memory_space=pl.ANY)] * count,
        out_specs=[pl.BlockSpec(memory_space=pltpu.VMEM)] * count,
        scratch_shapes=[pltpu.SemaphoreType.DMA((count,))],
        compiler_params=pltpu.CompilerParams(vmem_limit_bytes=VMEM_LIMIT),
        name="stage",
    )(*arrays)


def gather_rows(core, x_refs, rows):
    high, depth = x_refs[0].shape[0], rows.shape[2]
    for i, x_ref in enumerate(x_refs):
        for h in range(2):
            rows[core ^ h, i * high : (i + 1) * high, :] = x_ref[:, h * depth : (h + 1) * depth]


def project_mix(order, xs, own, other, slots, kind):
    chips = len(xs)
    streams, depth, chans = own.shape
    high = xs[0].shape[0]
    wide = chans // chips
    half = wide // 2

    def kernel(order, *refs):
        x_refs, (own_ref, other_ref, out_ref, rows) = refs[:chips], refs[chips:]
        core = order[2 * chips]
        gather_rows(core, x_refs, rows)
        for i, slot in enumerate(slots):
            at = columns(order[slot], wide)
            for g in range(1, streams):
                total = jnp.dot(rows[0], own_ref[g, :, at], preferred_element_type=F32)
                total += jnp.dot(rows[1], other_ref[g, :, at], preferred_element_type=F32)
                total = total.astype(kind)
                lanes = slice((g - 1) * half, g * half)
                for h in range(2):
                    out_ref[i, core ^ h, :, lanes] = total[:, h * half : (h + 1) * half]

    shape = (len(slots), 2, chips * high, (streams - 1) * half)
    scratch = [pltpu.VMEM((2, chips * high, depth), BF16)]
    return local(kernel, "project_mix", [(shape, kind)], order, [*xs, own, other], scratch)


def last_rows(order, xs, count):
    high, wide = xs[0].shape

    def kernel(order, *refs):
        for s in range(len(xs)):
            refs[-1][s] = refs[s][high - count :, :]

    return local(kernel, "last_rows", [((len(xs), count, wide), BF16)], order, xs)


def project_query(order, xs, before, own, other, short_filter):
    chips = len(xs)
    _, depth, chans = own.shape
    high = xs[0].shape[0]
    some = before.shape[1]
    step = some + high
    taps = short_filter.shape[0]
    tile = min(chans, 256)

    def kernel(order, *refs):
        x_refs = refs[:chips]
        before_ref, own_ref, other_ref, filt_ref, *out_refs, rows, ends, total = refs[chips:]
        core = order[2 * chips]
        ends[0] = jnp.zeros_like(ends[0])
        for s in range(chips):
            ends[order[chips + s] + 1] = before_ref[s]
        for i, x_ref in enumerate(x_refs):
            end = ends[order[i] + core]
            for h in range(2):
                lanes = slice(h * depth, (h + 1) * depth)
                rows[core ^ h, i * step : i * step + some, :] = end[:, lanes]
                rows[core ^ h, i * step + some : (i + 1) * step, :] = x_ref[:, lanes]
        for at in (slice(i, i + tile) for i in range(0, chans, tile)):
            total[...] = jnp.dot(
                rows[0], own_ref[0, :, at], preferred_element_type=F32
            ) + jnp.dot(rows[1], other_ref[0, :, at], preferred_element_type=F32)
            for i in range(chips):
                first = i * step + some
                value = filt_ref[0, 0:1, at] * total[first : first + high, :]
                for j in range(1, taps):
                    value = value + filt_ref[j, 0:1, at] * total[first - j : first - j + high, :]
                out_refs[i][:, at] = value.astype(out_refs[i].dtype)

    shapes = [((high, chans), F32 if i < 2 else BF16) for i in range(chips)]
    scratch = [
        pltpu.VMEM((2, chips * step, depth), BF16),
        pltpu.VMEM((chips + 1, some, 2 * depth), BF16),
        pltpu.VMEM((chips * step, tile), F32),
    ]
    arrays = [*xs, before, own, other, short_filter]
    return local(kernel, "project_query", shapes, order, arrays, scratch)


def second_share(order, rest, both_in, chips):
    shape = (1,) + rest.shape[1:]
    high = rest.shape[2] // chips

    def kernel(order, rest_ref, both_ref, out_ref):
        for h in range(2):
            for s in range(chips):
                here, there = (slice(i * high, (i + 1) * high) for i in (s, s ^ 2))
                term = both_ref[0, h, there, :].astype(F32)
                out_ref[0, h, here, :] = (rest_ref[0, h, here, :] + term).astype(BF16)

    return local(kernel, "second_share", [(shape, BF16)], order, [rest, both_in])


def own_share(order, rest, first_in, second_in, chips):
    _, _, rows, lanes = rest.shape
    high = rows // chips

    def kernel(order, rest_ref, first_ref, second_ref, own_ref, other_ref):
        for h, out_ref in ((1, other_ref), (0, own_ref)):
            for s in range(chips):
                here, first, second = (slice(i * high, (i + 1) * high) for i in (s, s ^ 2, s ^ 1))
                total = rest_ref[1, h, here, :] + first_ref[0, h, first, :].astype(F32)
                total = total + second_ref[0, h, second, :].astype(F32)
                out_ref[here, :] = total.astype(out_ref.dtype)

    shapes = [((rows, lanes), F32), ((rows, lanes), BF16)]
    return local(kernel, "own_share", shapes, order, [rest, first_in, second_in])


def hyena_kernel(
    order, own_ref, swap_ref, filt_ref, decay_ref, residue_ref,
    keep_ref, send_ref, rows, mixed_s, state, enter, edge, *, blocks,
):
    high = rows.shape[1] // blocks
    chans = rows.shape[2]
    modes = decay_ref.shape[0]
    taps = filt_ref.shape[0]
    chips = blocks // 2
    core = order[2 * chips]
    channels = columns(order[2 * chips + 1], chans)

    for s in range(chips):
        here = slice(s * high, (s + 1) * high)
        own_at = columns(2 * order[s] + core, high)
        swap_at = columns(2 * order[chips + s] + 1 - core, high)
        for g in range(2):
            lanes = slice(g * chans, (g + 1) * chans)
            rows[g, own_at, :] = own_ref[here, lanes]
            rows[g, swap_at, :] = swap_ref[here, lanes].astype(F32)

    for k in range(1, taps):
        for g in range(2):
            edge[k - 1, g, 0:1, :] = jnp.zeros((1, chans), F32)
            for b in range(1, blocks):
                edge[k - 1, g, b : b + 1, :] = rows[g, b * high - k : b * high - k + 1, :]

    rate = decay_ref[:, channels]
    taps_of = [filt_ref[j, :, channels] for j in range(taps)]
    decay = [jnp.broadcast_to(rate[n : n + 1, :], (blocks, chans)) for n in range(modes)]
    filt = [
        [jnp.broadcast_to(taps_of[j][g + 1 : g + 2, :], (blocks, chans)) for g in range(2)]
        for j in range(taps)
    ]

    def first_pass(t, carry):
        states, earlier = carry
        now = [rows[g, pl.ds(t, blocks, stride=high), :] for g in range(2)]
        featured = []
        for g in range(2):
            value = filt[0][g] * now[g]
            for k in range(1, taps):
                value = value + filt[k][g] * earlier[k - 1][g]
            featured.append(value)
        mixed = (featured[0] * featured[1]).astype(BF16).astype(F32)
        mixed_s[t] = mixed
        states = tuple(decay[n] * states[n] + mixed for n in range(modes))
        return states, (tuple(now),) + tuple(earlier[:-1])

    zeros = tuple(jnp.zeros((blocks, chans), F32) for _ in range(modes))
    before = tuple(tuple(edge[k, g] for g in range(2)) for k in range(taps - 1))
    states, _ = lax.fori_loop(0, high, first_pass, (zeros, before), unroll=4)
    for n in range(modes):
        state[n * blocks : (n + 1) * blocks, :] = states[n]

    across = jnp.ones_like(rate)
    power, left = rate, high
    while left:
        if left & 1:
            across = across * power
        left >>= 1
        if left:
            power = power * power
    entering = jnp.zeros((modes, chans), F32)
    for b in range(blocks):
        enter[pl.ds(b, modes, stride=blocks), :] = entering
        entering = across * entering + state[pl.ds(b, modes, stride=blocks), :]

    gain = residue_ref[:, channels] * jnp.sqrt(1.0 - rate * rate)
    gains = [jnp.broadcast_to(gain[n : n + 1, :], (blocks, chans)) for n in range(modes)]

    def second_pass(t, states):
        mixed = mixed_s[t]
        states = tuple(decay[n] * states[n] + mixed for n in range(modes))
        terms = [gains[n] * states[n] for n in range(modes)]
        while len(terms) > 1:
            terms = [sum(terms[i : i + 2][1:], terms[i]) for i in range(0, len(terms), 2)]
        rows[0, pl.ds(t, blocks, stride=high), :] = terms[0]
        return states

    begin = tuple(enter[n * blocks : (n + 1) * blocks, :] for n in range(modes))
    lax.fori_loop(0, high, second_pass, begin, unroll=4)
    for s in range(chips):
        keep_ref[s] = rows[0, columns(2 * order[s] + core, high), :].astype(BF16)
        send_ref[s] = rows[0, columns(2 * order[chips + s] + 1 - core, high), :].astype(BF16)


def hyena(order, own, swap, short_filter, mode_decay, residue, blocks):
    rows_count, lanes = own.shape
    chans = lanes // 2
    total = 2 * rows_count
    high = total // blocks
    modes, taps = mode_decay.shape[0], short_filter.shape[0]
    scratch = [
        pltpu.VMEM((2, total, chans), F32),
        pltpu.VMEM((high, blocks, chans), F32),
        pltpu.VMEM((modes * blocks, chans), F32),
        pltpu.VMEM((modes * blocks, chans), F32),
        pltpu.VMEM((taps - 1, 2, blocks, chans), F32),
    ]
    arrays = [own, swap, short_filter, mode_decay, residue]
    kernel = functools.partial(hyena_kernel, blocks=blocks)
    shapes = [((blocks // 2, high, chans), BF16)] * 2
    return local(kernel, "hyena", shapes, order, arrays, scratch)


def pair_up(order, keep, other):
    chips, high, chans = keep.shape

    def kernel(order, keep_ref, other_ref, *out_refs):
        for s, out_ref in enumerate(out_refs):
            out_ref[0] = keep_ref[s]
            out_ref[1] = other_ref[s]

    return local(kernel, "pair_up", [((2, high, chans), BF16)] * chips, order, [keep, other])


def query_second(order, rest, q_in):
    def kernel(order, rest_ref, in_ref, out_ref):
        out_ref[...] = (rest_ref[...] + in_ref[...].astype(F32)).astype(BF16)

    return local(kernel, "query_second", [(rest.shape, BF16)], order, [rest, q_in])


def gate(scalars, queries, long_parts, w_out, groups):
    rows, chans = queries[0].shape
    chips = len(long_parts)
    part = long_parts[0].shape[2]
    wide = w_out.shape[1] // groups
    first_pick = 2 * chips + 3

    def kernel(scalars, *refs):
        query_refs, long_refs = refs[: len(queries)], refs[len(queries) : len(queries) + chips]
        w_ref, gated_ref, pair_ref, side_ref, query = refs[len(queries) + chips :]
        core = scalars[2 * chips]
        query[...] = sum(ref[...].astype(F32) for ref in query_refs)
        for s, ref in enumerate(long_refs):
            for h in range(2):
                at = columns(2 * scalars[s] + (core ^ h), part)
                gated_ref[:, at] = (query[:, at] * ref[h].astype(F32)).astype(BF16)
        for pick, out_ref in enumerate((pair_ref, side_ref)):
            total = jnp.dot(
                gated_ref[...],
                w_ref[:, columns(scalars[first_pick + pick], wide)],
                preferred_element_type=F32,
            )
            out_ref[...] = total.astype(BF16)

    shapes = [((rows, chans), BF16), ((rows, wide), BF16), ((rows, wide), BF16)]
    arrays = [*queries, *long_parts, w_out]
    scratch = [pltpu.VMEM((rows, chans), F32)]
    return local(kernel, "gate", shapes, scalars, arrays, scratch)


def out_columns(picks, pick, x, w_out, groups, kind):
    wide = w_out.shape[1] // groups

    def kernel(picks, x_ref, w_ref, out_ref):
        total = jnp.dot(
            x_ref[...], w_ref[:, columns(picks[pick], wide)], preferred_element_type=F32
        )
        out_ref[...] = total.astype(kind)

    return local(kernel, "out_columns", [((x.shape[0], wide), kind)], picks, [x, w_out])


def line_picks():
    z = lax.axis_index("dp")
    table = [[3, 0, 3, 0], [1, 2, 1, 2], [2, 3, 0, 1], [0, 1, 2, 3], [0, 1, 1, 0]]
    return jnp.stack([sum(jnp.where(z == i, v, 0) for i, v in enumerate(row)) for row in table])


def output_over_line(picks, gated, pair, side, w_out, groups):
    pair_in = lax.ppermute(pair, "dp", [(0, 1), (1, 0), (2, 3), (3, 2)])
    far = out_columns(picks, 2, gated, w_out, groups, BF16)
    middle_in = lax.ppermute(side, "dp", [(1, 2), (2, 1)])
    side, far = lax.optimization_barrier((side, far))
    end_in = lax.ppermute(far, "dp", [(0, 2), (3, 1)])
    side_in = lax.ppermute(side, "dp", [(0, 1), (3, 2)])
    own = out_columns(picks, 3, gated, w_out, groups, F32)

    def add(picks, far_ref, pair_ref, out_ref):
        out_ref[...] = (far_ref[...].astype(F32) + pair_ref[...].astype(F32)).astype(BF16)

    both = local(add, "both", [(far.shape, BF16)], picks, [far, pair_in])
    far_in = lax.ppermute(both, "dp", [(1, 3), (2, 0)])

    def total(picks, own_ref, pair_ref, *refs):
        out_ref = refs[-1]
        inner = picks[4] == 1
        value = own_ref[...] + jnp.where(inner, 0.0, pair_ref[...].astype(F32))
        for ref in refs[:-1]:
            value = value + ref[...].astype(F32)
        out_ref[...] = value.astype(BF16)

    arrays = [own, pair_in, middle_in, end_in, side_in, far_in]
    return local(total, "total", [(own.shape, BF16)], picks, arrays)


def on_device_chips(tokens, w_in, short_filter, mode_decay, residue, w_out):
    count, groups = lax.axis_size("ctx"), lax.axis_size("dp")
    chips = count // 2
    me = lax.axis_index("ctx")
    core, chip = me % 2, me // 2

    def across(i, slot):
        high_bit, low_bit = slot >> 1, slot & 1
        step = (high_bit + 2 * low_bit) if i % 2 == 0 else (2 * high_bit + low_bit)
        return i ^ (2 * step)

    def route(slot):
        return [(i, across(i, slot)) for i in range(count)]

    def relative(slot, core):
        high_bit, low_bit = slot >> 1, slot & 1
        return jnp.where(core == 0, high_bit + 2 * low_bit, 2 * high_bit + low_bit)

    slot_chip = [chip ^ relative(s, core) for s in range(chips)]
    slot_other = [chip ^ relative(s, 1 - core) for s in range(chips)]
    order = jnp.stack(slot_chip + slot_other + [core, me, lax.axis_index("dp") % 2]).astype(jnp.int32)
    picks = line_picks().astype(jnp.int32)
    both_scalars = jnp.concatenate([order, picks])
    order, picks, both_scalars = lax.optimization_barrier((order, picks, both_scalars))

    own_w = jnp.transpose(w_in, (1, 0, 2))
    swap = [(i, i ^ 1) for i in range(count)]

    other_w = lax.ppermute(own_w, "ctx", swap)
    xs = cut(order, tokens, chips)
    own_w, w_out, xs = lax.optimization_barrier((own_w, w_out, xs))
    own_w, w_out = stage(own_w, w_out)
    half = lax.ppermute(xs[3], "ctx", route(3))
    other = lax.ppermute(half, "dp", [(i, i ^ 1) for i in range(groups)])
    xs = [xs[0]] + [lax.ppermute(xs[s], "ctx", route(s)) for s in (1, 2)]
    xs.append(join_rows(order, half, other))

    both = project_mix(order, xs, own_w, other_w, [3], BF16)
    both_in = lax.ppermute(both, "ctx", route(2))
    xs, both = lax.optimization_barrier((xs, both))
    first = project_mix(order, xs, own_w, other_w, [2], BF16)
    first_in = lax.ppermute(first, "ctx", route(2))
    xs, first = lax.optimization_barrier((xs, first))
    rest = project_mix(order, xs, own_w, other_w, [1, 0], F32)
    second = second_share(order, rest, both_in, chips)
    second_in = lax.ppermute(second, "ctx", route(1))

    xs, second = lax.optimization_barrier((xs, second))
    before = lax.ppermute(last_rows(order, xs, 16), "ctx", swap)
    q_own, q_next, q_first, q_both = project_query(order, xs, before, own_w, other_w, short_filter)
    q_own, rest = lax.optimization_barrier((q_own, rest))

    own, other_half = own_share(order, rest, first_in, second_in, chips)
    other_half = lax.ppermute(other_half, "ctx", swap)
    q_both, q_first, own = lax.optimization_barrier((q_both, q_first, own))
    q_both = lax.ppermute(q_both, "ctx", route(2))
    q_first = lax.ppermute(q_first, "ctx", route(2))
    keep, send = hyena(order, own, other_half, short_filter, mode_decay, residue, count)
    q_next, keep, send = lax.optimization_barrier((q_next, keep, send))
    q_second = query_second(order, q_next, q_both)
    long_parts = pair_up(order, keep, lax.ppermute(send, "ctx", swap))
    q_second = lax.ppermute(q_second, "ctx", route(1))
    long_parts = [long_parts[0]] + [lax.ppermute(long_parts[s], "ctx", route(s)) for s in (1, 2, 3)]
    queries = [q_own, q_first, q_second]
    gated, pair, side = gate(both_scalars, queries, long_parts, w_out, groups)
    return output_over_line(picks, gated, pair, side, w_out, groups)


def solution(mesh):
    count, groups = mesh.shape["ctx"], mesh.shape["dp"]

    def on_device(tokens, w_in, *rest):
        lanes = w_in.shape[2] // count
        chips = count == 8 and groups == 4 and w_in.shape[2] % count == 0 and lanes % 128 == 0
        return (on_device_chips if chips else on_device_any)(tokens, w_in, *rest)

    return jax.shard_map(
        on_device,
        mesh=mesh,
        in_specs=(
            P("ctx", None),
            P("ctx", None, "dp"),
            P(None, None, "dp"),
            P(None, "dp"),
            P(None, "dp"),
            P("dp", None),
        ),
        out_specs=P("ctx", "dp"),
        check_vma=False,
    )
```

```python
import functools

import jax
import jax.numpy as jnp
from jax import lax
from jax.experimental import pallas as pl
from jax.experimental.pallas import tpu as pltpu
from jax.sharding import PartitionSpec as P

BLK = 64
F32, BF16 = jnp.float32, jnp.bfloat16
VMEM_LIMIT = 12 * 1024 * 1024


def from_behind(block, axis, distance):
    devices = range(lax.axis_size(axis))
    route = [(i - distance, i) for i in devices if i - distance in devices]
    return lax.ppermute(block, axis, route)


def prefix(value, axis, join, neutral):
    count, mine = (lax.axis_size(axis), lax.axis_index(axis))
    pieces = jax.tree.map(lambda part: lax.all_gather(part, axis), value)
    subtotal = jax.tree.map(
        lambda part, zero: jnp.full_like(part, 0) + jnp.asarray(zero, part.dtype), value, neutral
    )

    def lap(position, subtotal):
        longer = join(subtotal, jax.tree.map(lambda part: part[position], pieces))
        return jax.tree.map(lambda new, old: jnp.where(position < mine, new, old), longer, subtotal)

    return lax.fori_loop(0, count - 1, lap, subtotal)


def on_device_any(tokens, w_in, short_filter, mode_decay, residue, w_out):
    row_count = tokens.shape[0]
    chan_count = w_in.shape[2]
    short_count = short_filter.shape[0]
    mode_count = mode_decay.shape[0]
    earlier_rows = from_behind(tokens[row_count - (short_count - 1) :], "ctx", 1)
    source = jnp.concatenate([earlier_rows, tokens], 0)
    projected = jnp.einsum(
        "td,dgc->tgc",
        source,
        lax.all_gather(w_in, "ctx", axis=0, tiled=True),
        preferred_element_type=jnp.float32,
    )
    featured = jnp.zeros((row_count, 3, chan_count), jnp.float32)
    for j in range(short_count):
        featured = (
            featured
            + short_filter[j] * projected[short_count - 1 - j : short_count - 1 - j + row_count]
        )
    mixed = (featured[:, 1] * featured[:, 2]).astype(jnp.bfloat16)
    medium = mixed.astype(jnp.float32)
    highest = lax.Precision.HIGHEST
    mode_gain = residue * jnp.sqrt(1.0 - mode_decay * mode_decay)
    block_len = BLK
    block_times = jnp.arange(block_len).astype(jnp.float32)
    power_in = jnp.power(mode_decay[None], block_times[:, None, None])
    kernel_head = jnp.sum(mode_gain[None] * power_in, 1)
    lag_index = jnp.arange(block_len)[:, None] - jnp.arange(block_len)[None, :]
    toeplitz = jnp.where(
        (lag_index >= 0)[:, :, None], kernel_head[jnp.clip(lag_index, 0, block_len - 1)], 0.0
    )
    carry_weights = mode_gain[None] * power_in * mode_decay[None]
    state_weights = power_in[::-1]
    decay_block = jnp.power(mode_decay, float(block_len))
    blocks = medium.reshape(row_count // block_len, block_len, chan_count)

    def block_step(carried, block_rows):
        inner = jnp.einsum("tsc,sc->tc", toeplitz, block_rows, precision=highest)
        inner = inner + jnp.einsum("tnc,nc->tc", carry_weights, carried, precision=highest)
        carried = decay_block * carried + jnp.einsum(
            "snc,sc->nc", state_weights, block_rows, precision=highest
        )
        return (carried, inner)

    zero_state = jnp.zeros((mode_count, chan_count), jnp.float32)
    local_end, local_part = lax.scan(block_step, zero_state, blocks)
    local_part = local_part.reshape(row_count, chan_count)
    decay_device = jnp.power(mode_decay, float(row_count))

    def combine_states(earlier, later):
        return (earlier[0] * later[0], later[0] * earlier[1] + later[1])

    identity = (jnp.ones((mode_count, chan_count), jnp.float32), zero_state)
    scanned = prefix((decay_device, local_end), "ctx", combine_states, identity)
    entering = scanned[1]
    row_times = jnp.arange(1, row_count + 1).astype(jnp.float32)
    entry_weights = mode_gain[None] * jnp.power(mode_decay[None], row_times[:, None, None])
    long_part = local_part + jnp.einsum("tnc,nc->tc", entry_weights, entering, precision=highest)
    gated = (featured[:, 0] * long_part).astype(jnp.bfloat16)
    out_term = jnp.dot(gated, w_out, preferred_element_type=jnp.float32)
    return lax.psum_scatter(out_term.astype(jnp.bfloat16), "dp", scatter_dimension=1, tiled=True)


def local(kernel, name, shapes, scalars, arrays, scratch=()):
    whole = pl.BlockSpec(memory_space=pltpu.VMEM)
    out = [jax.ShapeDtypeStruct(*shape) for shape in shapes]
    return pl.pallas_call(
        kernel,
        out_shape=out if len(out) > 1 else out[0],
        in_specs=[pl.BlockSpec(memory_space=pltpu.SMEM)] + [whole] * len(arrays),
        out_specs=[whole] * len(out) if len(out) > 1 else whole,
        scratch_shapes=list(scratch),
        compiler_params=pltpu.CompilerParams(vmem_limit_bytes=VMEM_LIMIT),
        name=name,
    )(scalars, *arrays)


def columns(index, wide):
    return pl.ds(pl.multiple_of(index * wide, wide), wide)


def cut(order, tokens, pieces):
    high, wide = tokens.shape[0], tokens.shape[1] // pieces

    def kernel(order, tokens_ref, *out_refs):
        here = columns(order[2 * pieces + 2], high // 2)
        out_refs[pieces - 1][...] = tokens_ref[here, columns(order[pieces - 1], wide)]
        for s, out_ref in enumerate(out_refs[: pieces - 1]):
            out_ref[...] = tokens_ref[:, columns(order[s], wide)]

    shapes = [((high, wide), tokens.dtype)] * (pieces - 1) + [((high // 2, wide), tokens.dtype)]
    return local(kernel, "cut", shapes, order, [tokens])


def join_rows(order, mine, other):
    half, wide = mine.shape
    at = order.shape[0] - 1

    def kernel(order, mine_ref, other_ref, out_ref):
        out_ref[columns(order[at], half), :] = mine_ref[...]
        out_ref[columns(1 - order[at], half), :] = other_ref[...]

    return local(kernel, "join_rows", [((2 * half, wide), mine.dtype)], order, [mine, other])


def stage(*arrays):
    count = len(arrays)

    def kernel(*refs):
        sems = refs[2 * count]
        copies = [
            pltpu.make_async_copy(refs[i], refs[count + i], sems.at[i]) for i in range(count)
        ]
        for copy in copies:
            copy.start()
        for copy in copies:
            copy.wait()

    return pl.pallas_call(
        kernel,
        out_shape=[jax.ShapeDtypeStruct(x.shape, x.dtype) for x in arrays],
        in_specs=[pl.BlockSpec(memory_space=pl.ANY)] * count,
        out_specs=[pl.BlockSpec(memory_space=pltpu.VMEM)] * count,
        scratch_shapes=[pltpu.SemaphoreType.DMA((count,))],
        compiler_params=pltpu.CompilerParams(vmem_limit_bytes=VMEM_LIMIT),
        name="stage",
    )(*arrays)


def gather_rows(core, x_refs, rows):
    high, depth = x_refs[0].shape[0], rows.shape[2]
    for i, x_ref in enumerate(x_refs):
        for h in range(2):
            rows[core ^ h, i * high : (i + 1) * high, :] = x_ref[:, h * depth : (h + 1) * depth]


def project_mix(order, xs, own, other, slots, kind):
    chips = len(xs)
    streams, depth, chans = own.shape
    high = xs[0].shape[0]
    wide = chans // chips
    half = wide // 2

    def kernel(order, *refs):
        x_refs, (own_ref, other_ref, out_ref, rows) = refs[:chips], refs[chips:]
        core = order[2 * chips]
        gather_rows(core, x_refs, rows)
        for i, slot in enumerate(slots):
            at = columns(order[slot], wide)
            for g in range(1, streams):
                total = jnp.dot(rows[0], own_ref[g, :, at], preferred_element_type=F32)
                total += jnp.dot(rows[1], other_ref[g, :, at], preferred_element_type=F32)
                total = total.astype(kind)
                lanes = slice((g - 1) * half, g * half)
                for h in range(2):
                    out_ref[i, core ^ h, :, lanes] = total[:, h * half : (h + 1) * half]

    shape = (len(slots), 2, chips * high, (streams - 1) * half)
    scratch = [pltpu.VMEM((2, chips * high, depth), BF16)]
    return local(kernel, "project_mix", [(shape, kind)], order, [*xs, own, other], scratch)


def last_rows(order, xs, count):
    high, wide = xs[0].shape

    def kernel(order, *refs):
        for s in range(len(xs)):
            refs[-1][s] = refs[s][high - count :, :]

    return local(kernel, "last_rows", [((len(xs), count, wide), BF16)], order, xs)


def project_query(order, xs, before, own, other, short_filter):
    chips = len(xs)
    _, depth, chans = own.shape
    high = xs[0].shape[0]
    some = before.shape[1]
    step = some + high
    taps = short_filter.shape[0]
    tile = min(chans, 256)
    extra = tile if chans > tile else 0

    def kernel(order, *refs):
        x_refs = refs[:chips]
        before_ref, own_ref, other_ref, filt_ref, *out_refs, rows, ends, total = refs[chips:]
        core = order[2 * chips]
        ends[0] = jnp.zeros_like(ends[0])
        for s in range(chips):
            ends[order[chips + s] + 1] = before_ref[s]
        for i, x_ref in enumerate(x_refs):
            end = ends[order[i] + core]
            for h in range(2):
                lanes = slice(h * depth, (h + 1) * depth)
                rows[core ^ h, i * step : i * step + some, :] = end[:, lanes]
                rows[core ^ h, i * step + some : (i + 1) * step, :] = x_ref[:, lanes]
        for at in (slice(i, i + tile) for i in range(0, chans, tile)):
            total[...] = jnp.dot(
                rows[0], own_ref[0, :, at], preferred_element_type=F32
            ) + jnp.dot(rows[1], other_ref[0, :, at], preferred_element_type=F32)
            for i in range(chips):
                first = i * step + some
                value = filt_ref[0, 0:1, at] * total[first : first + high, :]
                for j in range(1, taps):
                    value = value + filt_ref[j, 0:1, at] * total[first - j : first - j + high, :]
                if i < 2:
                    out_refs[i][:, at] = value
                elif i == 3:
                    out_refs[3][:, at] = value.astype(BF16)
                elif at.start < extra:
                    out_refs[3][:, chans + at.start : chans + at.stop] = value.astype(BF16)
                else:
                    out_refs[2][:, at.start - extra : at.stop - extra] = value.astype(BF16)

    shapes = [((high, chans), F32)] * 2
    shapes += [((high, chans - extra), BF16), ((high, chans + extra), BF16)]
    scratch = [
        pltpu.VMEM((2, chips * step, depth), BF16),
        pltpu.VMEM((chips + 1, some, 2 * depth), BF16),
        pltpu.VMEM((chips * step, tile), F32),
    ]
    arrays = [*xs, before, own, other, short_filter]
    return local(kernel, "project_query", shapes, order, arrays, scratch)


def second_share(order, rest, both_in, chips):
    _, _, rows, lanes = rest.shape
    high = rows // chips

    def kernel(order, rest_ref, both_ref, *out_refs):
        for h, out_ref in enumerate(out_refs):
            for s in range(chips):
                here, there = (slice(i * high, (i + 1) * high) for i in (s, s ^ 2))
                term = both_ref[0, h, there, :].astype(F32)
                out_ref[here, :] = (rest_ref[0, h, here, :] + term).astype(BF16)

    shapes = [((rows, lanes), BF16)] * 2
    return local(kernel, "second_share", shapes, order, [rest, both_in])


def first_share(order, rest, first_in, chips):
    _, _, rows, lanes = rest.shape
    high = rows // chips

    def kernel(order, rest_ref, first_ref, own_ref, other_ref):
        for h, out_ref in ((1, other_ref), (0, own_ref)):
            for s in range(chips):
                here, first = (slice(i * high, (i + 1) * high) for i in (s, s ^ 2))
                total = rest_ref[1, h, here, :] + first_ref[0, h, first, :].astype(F32)
                out_ref[here, :] = total.astype(out_ref.dtype)

    shapes = [((rows, lanes), F32), ((rows, lanes), BF16)]
    return local(kernel, "first_share", shapes, order, [rest, first_in])


def hyena_kernel(
    order, own_ref, swap_ref, second_ref, swap_second_ref, filt_ref, decay_ref, residue_ref,
    keep_ref, send_ref, rows, mixed_s, state, enter, edge, *, blocks,
):
    high = rows.shape[1] // blocks
    chans = rows.shape[2]
    modes = decay_ref.shape[0]
    taps = filt_ref.shape[0]
    chips = blocks // 2
    core = order[2 * chips]
    channels = columns(order[2 * chips + 1], chans)

    for s in range(chips):
        here, second = (slice(i * high, (i + 1) * high) for i in (s, s ^ 1))
        own_at = columns(2 * order[s] + core, high)
        swap_at = columns(2 * order[chips + s] + 1 - core, high)
        for g in range(2):
            lanes = slice(g * chans, (g + 1) * chans)
            rows[g, own_at, :] = own_ref[here, lanes] + second_ref[second, lanes].astype(F32)
            rows[g, swap_at, :] = swap_ref[here, lanes].astype(F32) + swap_second_ref[
                second, lanes
            ].astype(F32)

    for k in range(1, taps):
        for g in range(2):
            edge[k - 1, g, 0:1, :] = jnp.zeros((1, chans), F32)
            for b in range(1, blocks):
                edge[k - 1, g, b : b + 1, :] = rows[g, b * high - k : b * high - k + 1, :]

    rate = decay_ref[:, channels]
    taps_of = [filt_ref[j, :, channels] for j in range(taps)]
    decay = [jnp.broadcast_to(rate[n : n + 1, :], (blocks, chans)) for n in range(modes)]
    filt = [
        [jnp.broadcast_to(taps_of[j][g + 1 : g + 2, :], (blocks, chans)) for g in range(2)]
        for j in range(taps)
    ]

    def first_pass(t, carry):
        states, earlier = carry
        now = [rows[g, pl.ds(t, blocks, stride=high), :] for g in range(2)]
        featured = []
        for g in range(2):
            value = filt[0][g] * now[g]
            for k in range(1, taps):
                value = value + filt[k][g] * earlier[k - 1][g]
            featured.append(value)
        mixed = (featured[0] * featured[1]).astype(BF16).astype(F32)
        mixed_s[t] = mixed
        states = tuple(decay[n] * states[n] + mixed for n in range(modes))
        return states, (tuple(now),) + tuple(earlier[:-1])

    zeros = tuple(jnp.zeros((blocks, chans), F32) for _ in range(modes))
    before = tuple(tuple(edge[k, g] for g in range(2)) for k in range(taps - 1))
    states, _ = lax.fori_loop(0, high, first_pass, (zeros, before), unroll=16)
    for n in range(modes):
        state[n * blocks : (n + 1) * blocks, :] = states[n]

    across = jnp.ones_like(rate)
    power, left = rate, high
    while left:
        if left & 1:
            across = across * power
        left >>= 1
        if left:
            power = power * power
    entering = jnp.zeros((modes, chans), F32)
    for b in range(blocks):
        enter[pl.ds(b, modes, stride=blocks), :] = entering
        entering = across * entering + state[pl.ds(b, modes, stride=blocks), :]

    gain = residue_ref[:, channels] * jnp.sqrt(1.0 - rate * rate)
    gains = [jnp.broadcast_to(gain[n : n + 1, :], (blocks, chans)) for n in range(modes)]

    def second_pass(t, states):
        mixed = mixed_s[t]
        states = tuple(decay[n] * states[n] + mixed for n in range(modes))
        terms = [gains[n] * states[n] for n in range(modes)]
        while len(terms) > 1:
            terms = [sum(terms[i : i + 2][1:], terms[i]) for i in range(0, len(terms), 2)]
        rows[0, pl.ds(t, blocks, stride=high), :] = terms[0]
        return states

    begin = tuple(enter[n * blocks : (n + 1) * blocks, :] for n in range(modes))
    lax.fori_loop(0, high, second_pass, begin, unroll=16)
    for s in range(chips):
        keep_ref[s] = rows[0, columns(2 * order[s] + core, high), :].astype(BF16)
        send_ref[s] = rows[0, columns(2 * order[chips + s] + 1 - core, high), :].astype(BF16)


def hyena(order, parts, short_filter, mode_decay, residue, blocks):
    rows_count, lanes = parts[0].shape
    chans = lanes // 2
    total = 2 * rows_count
    high = total // blocks
    modes, taps = mode_decay.shape[0], short_filter.shape[0]
    scratch = [
        pltpu.VMEM((2, total, chans), F32),
        pltpu.VMEM((high, blocks, chans), F32),
        pltpu.VMEM((modes * blocks, chans), F32),
        pltpu.VMEM((modes * blocks, chans), F32),
        pltpu.VMEM((taps - 1, 2, blocks, chans), F32),
    ]
    arrays = [*parts, short_filter, mode_decay, residue]
    kernel = functools.partial(hyena_kernel, blocks=blocks)
    shapes = [((blocks // 2, high, chans), BF16)] * 2
    return local(kernel, "hyena", shapes, order, arrays, scratch)


def payloads(order, q_next, q_in, keep, other):
    chips, high, _ = keep.shape
    chans = q_next.shape[1]

    def kernel(order, next_ref, in_ref, keep_ref, other_ref, second_ref, *out_refs):
        second_ref[...] = (next_ref[...] + in_ref[:, :chans].astype(F32)).astype(BF16)
        for s, out_ref in enumerate(out_refs):
            out_ref[0] = keep_ref[s]
            out_ref[1] = other_ref[s]

    shapes = [(q_next.shape, BF16)] + [((2, high, keep.shape[2]), BF16)] * chips
    return local(kernel, "payloads", shapes, order, [q_next, q_in, keep, other])


def gate(scalars, queries, long_parts, w_out, groups):
    rows, chans = queries[0].shape
    chips = len(long_parts)
    part = long_parts[0].shape[2]
    wide = w_out.shape[1] // groups
    first_pick = 2 * chips + 3

    def kernel(scalars, *refs):
        query_refs, long_refs = refs[: len(queries)], refs[len(queries) : len(queries) + chips]
        w_ref, gated_ref, pair_ref, side_ref, query = refs[len(queries) + chips :]
        core = scalars[2 * chips]
        own_ref, second_ref, both_ref, first_ref = query_refs
        extra = both_ref.shape[1] - chans
        query[...] = own_ref[...] + second_ref[...].astype(F32)
        query[:, :extra] += both_ref[:, chans:].astype(F32)
        query[:, extra:] += first_ref[...].astype(F32)
        for s, ref in enumerate(long_refs):
            for h in range(2):
                at = columns(2 * scalars[s] + (core ^ h), part)
                gated_ref[:, at] = (query[:, at] * ref[h].astype(F32)).astype(BF16)
        for pick, out_ref in enumerate((pair_ref, side_ref)):
            total = jnp.dot(
                gated_ref[...],
                w_ref[:, columns(scalars[first_pick + pick], wide)],
                preferred_element_type=F32,
            )
            out_ref[...] = total.astype(BF16)

    shapes = [((rows, chans), BF16), ((rows, wide), BF16), ((rows, wide), BF16)]
    arrays = [*queries, *long_parts, w_out]
    scratch = [pltpu.VMEM((rows, chans), F32)]
    return local(kernel, "gate", shapes, scalars, arrays, scratch)


def out_columns(picks, pick, x, w_out, groups, kind):
    wide = w_out.shape[1] // groups

    def kernel(picks, x_ref, w_ref, out_ref):
        total = jnp.dot(
            x_ref[...], w_ref[:, columns(picks[pick], wide)], preferred_element_type=F32
        )
        out_ref[...] = total.astype(kind)

    return local(kernel, "out_columns", [((x.shape[0], wide), kind)], picks, [x, w_out])


def line_picks():
    z = lax.axis_index("dp")
    table = [[3, 0, 3, 0], [1, 2, 1, 2], [2, 3, 0, 1], [0, 1, 2, 3], [0, 1, 1, 0]]
    return jnp.stack([sum(jnp.where(z == i, v, 0) for i, v in enumerate(row)) for row in table])


def output_over_line(picks, gated, pair, side, w_out, groups):
    pair_in = lax.ppermute(pair, "dp", [(0, 1), (1, 0), (2, 3), (3, 2)])
    far = out_columns(picks, 2, gated, w_out, groups, BF16)
    middle_in = lax.ppermute(side, "dp", [(1, 2), (2, 1)])
    side, far = lax.optimization_barrier((side, far))
    end_in = lax.ppermute(far, "dp", [(0, 2), (3, 1)])
    side_in = lax.ppermute(side, "dp", [(0, 1), (3, 2)])
    own = out_columns(picks, 3, gated, w_out, groups, F32)

    def add(picks, far_ref, pair_ref, out_ref):
        out_ref[...] = (far_ref[...].astype(F32) + pair_ref[...].astype(F32)).astype(BF16)

    both = local(add, "both", [(far.shape, BF16)], picks, [far, pair_in])
    far_in = lax.ppermute(both, "dp", [(1, 3), (2, 0)])

    def early(picks, own_ref, pair_ref, *refs):
        inner = picks[4] == 1
        value = own_ref[...] + jnp.where(inner, 0.0, pair_ref[...].astype(F32))
        for ref in refs[:-1]:
            value = value + ref[...].astype(F32)
        refs[-1][...] = value

    def total(picks, early_ref, far_ref, out_ref):
        out_ref[...] = (early_ref[...] + far_ref[...].astype(F32)).astype(BF16)

    arrays = [own, pair_in, middle_in, end_in, side_in]
    own = local(early, "early", [(own.shape, F32)], picks, arrays)
    return local(total, "total", [(own.shape, BF16)], picks, [own, far_in])


def on_device_chips(tokens, w_in, short_filter, mode_decay, residue, w_out):
    count, groups = lax.axis_size("ctx"), lax.axis_size("dp")
    chips = count // 2
    me = lax.axis_index("ctx")
    core, chip = me % 2, me // 2

    def across(i, slot):
        high_bit, low_bit = slot >> 1, slot & 1
        step = (high_bit + 2 * low_bit) if i % 2 == 0 else (2 * high_bit + low_bit)
        return i ^ (2 * step)

    def route(slot):
        return [(i, across(i, slot)) for i in range(count)]

    def relative(slot, core):
        high_bit, low_bit = slot >> 1, slot & 1
        return jnp.where(core == 0, high_bit + 2 * low_bit, 2 * high_bit + low_bit)

    slot_chip = [chip ^ relative(s, core) for s in range(chips)]
    slot_other = [chip ^ relative(s, 1 - core) for s in range(chips)]
    order = jnp.stack(slot_chip + slot_other + [core, me, lax.axis_index("dp") % 2]).astype(jnp.int32)
    picks = line_picks().astype(jnp.int32)
    both_scalars = jnp.concatenate([order, picks])
    order, picks, both_scalars = lax.optimization_barrier((order, picks, both_scalars))

    own_w = jnp.transpose(w_in, (1, 0, 2))
    swap = [(i, i ^ 1) for i in range(count)]

    other_w = lax.ppermute(own_w, "ctx", swap)
    xs = cut(order, tokens, chips)
    own_w, w_out, xs = lax.optimization_barrier((own_w, w_out, xs))
    own_w, w_out = stage(own_w, w_out)
    half = lax.ppermute(xs[3], "ctx", route(3))
    other = lax.ppermute(half, "dp", [(i, i ^ 1) for i in range(groups)])
    xs = [xs[0]] + [lax.ppermute(xs[s], "ctx", route(s)) for s in (1, 2)]
    xs.append(join_rows(order, half, other))

    both = project_mix(order, xs, own_w, other_w, [3], BF16)
    both_in = lax.ppermute(both, "ctx", route(2))
    xs, both = lax.optimization_barrier((xs, both))
    first = project_mix(order, xs, own_w, other_w, [2], BF16)
    first_in = lax.ppermute(first, "ctx", route(2))
    xs, first = lax.optimization_barrier((xs, first))
    rest = project_mix(order, xs, own_w, other_w, [1, 0], F32)
    second, swap_second = second_share(order, rest, both_in, chips)
    second_in = lax.ppermute(second, "ctx", route(1))
    swap_second = lax.ppermute(swap_second, "ctx", [(i, j ^ 1) for i, j in route(1)])

    xs, second = lax.optimization_barrier((xs, second))
    before = lax.ppermute(last_rows(order, xs, 16), "ctx", swap)
    q_own, q_next, q_first, q_both = project_query(order, xs, before, own_w, other_w, short_filter)
    q_own, rest = lax.optimization_barrier((q_own, rest))

    own, other_half = first_share(order, rest, first_in, chips)
    other_half = lax.ppermute(other_half, "ctx", swap)
    q_both, q_first, own = lax.optimization_barrier((q_both, q_first, own))
    q_both = lax.ppermute(q_both, "ctx", route(2))
    q_first = lax.ppermute(q_first, "ctx", route(2))
    parts = [own, other_half, second_in, swap_second]
    keep, send = hyena(order, parts, short_filter, mode_decay, residue, count)
    other_long = lax.ppermute(send, "ctx", swap)
    q_second, *long_parts = payloads(order, q_next, q_both, keep, other_long)
    q_second = lax.ppermute(q_second, "ctx", route(1))
    long_parts = [long_parts[0]] + [lax.ppermute(long_parts[s], "ctx", route(s)) for s in (1, 2, 3)]
    queries = [q_own, q_second, q_both, q_first]
    gated, pair, side = gate(both_scalars, queries, long_parts, w_out, groups)
    return output_over_line(picks, gated, pair, side, w_out, groups)


def solution(mesh):
    count, groups = mesh.shape["ctx"], mesh.shape["dp"]

    def on_device(tokens, w_in, *rest):
        lanes = w_in.shape[2] // count
        chips = count == 8 and groups == 4 and w_in.shape[2] % count == 0 and lanes % 128 == 0
        return (on_device_chips if chips else on_device_any)(tokens, w_in, *rest)

    return jax.shard_map(
        on_device,
        mesh=mesh,
        in_specs=(
            P("ctx", None),
            P("ctx", None, "dp"),
            P(None, None, "dp"),
            P(None, "dp"),
            P(None, "dp"),
            P("dp", None),
        ),
        out_specs=P("ctx", "dp"),
        check_vma=False,
    )
```

```python
import functools

import jax
import jax.numpy as jnp
from jax import lax
from jax.experimental import pallas as pl
from jax.experimental.pallas import tpu as pltpu
from jax.sharding import PartitionSpec as P

BLK = 64
F32, BF16 = jnp.float32, jnp.bfloat16
VMEM_LIMIT = 12 * 1024 * 1024


def from_behind(block, axis, distance):
    devices = range(lax.axis_size(axis))
    route = [(i - distance, i) for i in devices if i - distance in devices]
    return lax.ppermute(block, axis, route)


def prefix(value, axis, join, neutral):
    count, mine = (lax.axis_size(axis), lax.axis_index(axis))
    pieces = jax.tree.map(lambda part: lax.all_gather(part, axis), value)
    subtotal = jax.tree.map(
        lambda part, zero: jnp.full_like(part, 0) + jnp.asarray(zero, part.dtype), value, neutral
    )

    def lap(position, subtotal):
        longer = join(subtotal, jax.tree.map(lambda part: part[position], pieces))
        return jax.tree.map(lambda new, old: jnp.where(position < mine, new, old), longer, subtotal)

    return lax.fori_loop(0, count - 1, lap, subtotal)


def on_device_any(tokens, w_in, short_filter, mode_decay, residue, w_out):
    row_count = tokens.shape[0]
    chan_count = w_in.shape[2]
    short_count = short_filter.shape[0]
    mode_count = mode_decay.shape[0]
    earlier_rows = from_behind(tokens[row_count - (short_count - 1) :], "ctx", 1)
    source = jnp.concatenate([earlier_rows, tokens], 0)
    projected = jnp.einsum(
        "td,dgc->tgc",
        source,
        lax.all_gather(w_in, "ctx", axis=0, tiled=True),
        preferred_element_type=jnp.float32,
    )
    featured = jnp.zeros((row_count, 3, chan_count), jnp.float32)
    for j in range(short_count):
        featured = (
            featured
            + short_filter[j] * projected[short_count - 1 - j : short_count - 1 - j + row_count]
        )
    mixed = (featured[:, 1] * featured[:, 2]).astype(jnp.bfloat16)
    medium = mixed.astype(jnp.float32)
    highest = lax.Precision.HIGHEST
    mode_gain = residue * jnp.sqrt(1.0 - mode_decay * mode_decay)
    block_len = BLK
    block_times = jnp.arange(block_len).astype(jnp.float32)
    power_in = jnp.power(mode_decay[None], block_times[:, None, None])
    kernel_head = jnp.sum(mode_gain[None] * power_in, 1)
    lag_index = jnp.arange(block_len)[:, None] - jnp.arange(block_len)[None, :]
    toeplitz = jnp.where(
        (lag_index >= 0)[:, :, None], kernel_head[jnp.clip(lag_index, 0, block_len - 1)], 0.0
    )
    carry_weights = mode_gain[None] * power_in * mode_decay[None]
    state_weights = power_in[::-1]
    decay_block = jnp.power(mode_decay, float(block_len))
    blocks = medium.reshape(row_count // block_len, block_len, chan_count)

    def block_step(carried, block_rows):
        inner = jnp.einsum("tsc,sc->tc", toeplitz, block_rows, precision=highest)
        inner = inner + jnp.einsum("tnc,nc->tc", carry_weights, carried, precision=highest)
        carried = decay_block * carried + jnp.einsum(
            "snc,sc->nc", state_weights, block_rows, precision=highest
        )
        return (carried, inner)

    zero_state = jnp.zeros((mode_count, chan_count), jnp.float32)
    local_end, local_part = lax.scan(block_step, zero_state, blocks)
    local_part = local_part.reshape(row_count, chan_count)
    decay_device = jnp.power(mode_decay, float(row_count))

    def combine_states(earlier, later):
        return (earlier[0] * later[0], later[0] * earlier[1] + later[1])

    identity = (jnp.ones((mode_count, chan_count), jnp.float32), zero_state)
    scanned = prefix((decay_device, local_end), "ctx", combine_states, identity)
    entering = scanned[1]
    row_times = jnp.arange(1, row_count + 1).astype(jnp.float32)
    entry_weights = mode_gain[None] * jnp.power(mode_decay[None], row_times[:, None, None])
    long_part = local_part + jnp.einsum("tnc,nc->tc", entry_weights, entering, precision=highest)
    gated = (featured[:, 0] * long_part).astype(jnp.bfloat16)
    out_term = jnp.dot(gated, w_out, preferred_element_type=jnp.float32)
    return lax.psum_scatter(out_term.astype(jnp.bfloat16), "dp", scatter_dimension=1, tiled=True)


def local(kernel, name, shapes, scalars, arrays, scratch=()):
    whole = pl.BlockSpec(memory_space=pltpu.VMEM)
    out = [jax.ShapeDtypeStruct(*shape) for shape in shapes]
    return pl.pallas_call(
        kernel,
        out_shape=out if len(out) > 1 else out[0],
        in_specs=[pl.BlockSpec(memory_space=pltpu.SMEM)] + [whole] * len(arrays),
        out_specs=[whole] * len(out) if len(out) > 1 else whole,
        scratch_shapes=list(scratch),
        compiler_params=pltpu.CompilerParams(vmem_limit_bytes=VMEM_LIMIT),
        name=name,
    )(scalars, *arrays)


def columns(index, wide):
    return pl.ds(pl.multiple_of(index * wide, wide), wide)


def cut(order, tokens, pieces):
    high, wide = tokens.shape[0], tokens.shape[1] // pieces

    def kernel(order, tokens_ref, *out_refs):
        here = columns(order[2 * pieces + 2], high // 2)
        out_refs[pieces - 1][...] = tokens_ref[here, columns(order[pieces - 1], wide)]
        for s, out_ref in enumerate(out_refs[: pieces - 1]):
            out_ref[...] = tokens_ref[:, columns(order[s], wide)]

    shapes = [((high, wide), tokens.dtype)] * (pieces - 1) + [((high // 2, wide), tokens.dtype)]
    return local(kernel, "cut", shapes, order, [tokens])


def join_rows(order, mine, other):
    half, wide = mine.shape
    at = order.shape[0] - 1

    def kernel(order, mine_ref, other_ref, out_ref):
        out_ref[columns(order[at], half), :] = mine_ref[...]
        out_ref[columns(1 - order[at], half), :] = other_ref[...]

    return local(kernel, "join_rows", [((2 * half, wide), mine.dtype)], order, [mine, other])


def stage(array):
    def kernel(array_ref, out_ref, sem):
        copy = pltpu.make_async_copy(array_ref, out_ref, sem)
        copy.start()
        copy.wait()

    return pl.pallas_call(
        kernel,
        out_shape=jax.ShapeDtypeStruct(array.shape, array.dtype),
        in_specs=[pl.BlockSpec(memory_space=pl.ANY)],
        out_specs=pl.BlockSpec(memory_space=pltpu.VMEM),
        scratch_shapes=[pltpu.SemaphoreType.DMA],
        compiler_params=pltpu.CompilerParams(vmem_limit_bytes=VMEM_LIMIT),
        name="stage",
    )(array)


def gather_rows(core, x_refs, rows):
    high, depth = x_refs[0].shape[0], rows.shape[2]
    for i, x_ref in enumerate(x_refs):
        for h in range(2):
            rows[core ^ h, i * high : (i + 1) * high, :] = x_ref[:, h * depth : (h + 1) * depth]


def project_mix(order, xs, own, other, slots, kind, ends=0):
    chips = len(xs)
    streams, depth, chans = own.shape
    high = xs[0].shape[0]
    wide = chans // chips
    half = wide // 2

    def kernel(order, *refs):
        x_refs, (own_ref, other_ref, out_ref, *end_refs, rows) = refs[:chips], refs[chips:]
        core = order[2 * chips]
        gather_rows(core, x_refs, rows)
        for end_ref in end_refs:
            for s in range(chips):
                end_ref[s] = x_refs[s][high - ends :, :]
        for i, slot in enumerate(slots):
            at = columns(order[slot], wide)
            for g in range(1, streams):
                total = jnp.dot(rows[0], own_ref[g, :, at], preferred_element_type=F32)
                total += jnp.dot(rows[1], other_ref[g, :, at], preferred_element_type=F32)
                total = total.astype(kind)
                lanes = slice((g - 1) * half, g * half)
                for h in range(2):
                    out_ref[i, core ^ h, :, lanes] = total[:, h * half : (h + 1) * half]

    shape = (len(slots), 2, chips * high, (streams - 1) * half)
    scratch = [pltpu.VMEM((2, chips * high, depth), BF16)]
    shapes = [(shape, kind)] + ([((chips, ends, 2 * depth), BF16)] if ends else [])
    return local(kernel, "project_mix", shapes, order, [*xs, own, other], scratch)


def project_query(order, xs, before, own, other, short_filter):
    chips = len(xs)
    _, depth, chans = own.shape
    high = xs[0].shape[0]
    some = before.shape[1]
    step = some + high
    taps = short_filter.shape[0]
    tile = min(chans, 256)

    def kernel(order, *refs):
        x_refs = refs[:chips]
        before_ref, own_ref, other_ref, filt_ref, *out_refs, rows, ends, total = refs[chips:]
        core = order[2 * chips]
        ends[0] = jnp.zeros_like(ends[0])
        for s in range(chips):
            ends[order[chips + s] + 1] = before_ref[s]
        for i, x_ref in enumerate(x_refs):
            end = ends[order[i] + core]
            for h in range(2):
                lanes = slice(h * depth, (h + 1) * depth)
                rows[core ^ h, i * step : i * step + some, :] = end[:, lanes]
                rows[core ^ h, i * step + some : (i + 1) * step, :] = x_ref[:, lanes]
        for at in (slice(i, i + tile) for i in range(0, chans, tile)):
            total[...] = jnp.dot(
                rows[0], own_ref[0, :, at], preferred_element_type=F32
            ) + jnp.dot(rows[1], other_ref[0, :, at], preferred_element_type=F32)
            for i in range(chips):
                first = i * step + some
                value = filt_ref[0, 0:1, at] * total[first : first + high, :]
                for j in range(1, taps):
                    value = value + filt_ref[j, 0:1, at] * total[first - j : first - j + high, :]
                out_refs[i][:, at] = value.astype(out_refs[i].dtype)

    shapes = [((high, chans), F32 if i < 2 else BF16) for i in range(chips)]
    scratch = [
        pltpu.VMEM((2, chips * step, depth), BF16),
        pltpu.VMEM((chips + 1, some, 2 * depth), BF16),
        pltpu.VMEM((chips * step, tile), F32),
    ]
    arrays = [*xs, before, own, other, short_filter]
    return local(kernel, "project_query", shapes, order, arrays, scratch)


def second_share(order, rest, both_in, chips):
    _, _, rows, lanes = rest.shape
    high = rows // chips

    def kernel(order, rest_ref, both_ref, *out_refs):
        for h, out_ref in enumerate(out_refs):
            for s in range(chips):
                here, there = (slice(i * high, (i + 1) * high) for i in (s, s ^ 2))
                term = both_ref[0, h, there, :].astype(F32)
                out_ref[here, :] = (rest_ref[0, h, here, :] + term).astype(BF16)

    shapes = [((rows, lanes), BF16)] * 2
    return local(kernel, "second_share", shapes, order, [rest, both_in])


def first_share(order, rest, first_in, chips):
    _, _, rows, lanes = rest.shape
    high = rows // chips

    def kernel(order, rest_ref, first_ref, own_ref, other_ref):
        for h, out_ref in ((1, other_ref), (0, own_ref)):
            for s in range(chips):
                here, first = (slice(i * high, (i + 1) * high) for i in (s, s ^ 2))
                total = rest_ref[1, h, here, :] + first_ref[0, h, first, :].astype(F32)
                out_ref[here, :] = total.astype(out_ref.dtype)

    shapes = [((rows, lanes), F32), ((rows, lanes), BF16)]
    return local(kernel, "first_share", shapes, order, [rest, first_in])


def hyena_kernel(
    order, own_ref, swap_ref, second_ref, swap_second_ref, filt_ref, decay_ref, residue_ref,
    keep_ref, send_ref, rows, mixed_s, state, enter, edge, *, blocks,
):
    high = rows.shape[1] // blocks
    chans = rows.shape[2]
    modes = decay_ref.shape[0]
    taps = filt_ref.shape[0]
    chips = blocks // 2
    core = order[2 * chips]
    channels = columns(order[2 * chips + 1], chans)

    for s in range(chips):
        here, second = (slice(i * high, (i + 1) * high) for i in (s, s ^ 1))
        own_at = columns(2 * order[s] + core, high)
        swap_at = columns(2 * order[chips + s] + 1 - core, high)
        for g in range(2):
            lanes = slice(g * chans, (g + 1) * chans)
            rows[g, own_at, :] = own_ref[here, lanes] + second_ref[second, lanes].astype(F32)
            rows[g, swap_at, :] = swap_ref[here, lanes].astype(F32) + swap_second_ref[
                second, lanes
            ].astype(F32)

    for k in range(1, taps):
        for g in range(2):
            edge[k - 1, g, 0:1, :] = jnp.zeros((1, chans), F32)
            for b in range(1, blocks):
                edge[k - 1, g, b : b + 1, :] = rows[g, b * high - k : b * high - k + 1, :]

    rate = decay_ref[:, channels]
    taps_of = [filt_ref[j, :, channels] for j in range(taps)]
    decay = [jnp.broadcast_to(rate[n : n + 1, :], (blocks, chans)) for n in range(modes)]
    filt = [
        [jnp.broadcast_to(taps_of[j][g + 1 : g + 2, :], (blocks, chans)) for g in range(2)]
        for j in range(taps)
    ]

    def first_pass(t, carry):
        states, earlier = carry
        now = [rows[g, pl.ds(t, blocks, stride=high), :] for g in range(2)]
        featured = []
        for g in range(2):
            value = filt[0][g] * now[g]
            for k in range(1, taps):
                value = value + filt[k][g] * earlier[k - 1][g]
            featured.append(value)
        mixed = (featured[0] * featured[1]).astype(BF16).astype(F32)
        mixed_s[t] = mixed
        states = tuple(decay[n] * states[n] + mixed for n in range(modes))
        return states, (tuple(now),) + tuple(earlier[:-1])

    zeros = tuple(jnp.zeros((blocks, chans), F32) for _ in range(modes))
    before = tuple(tuple(edge[k, g] for g in range(2)) for k in range(taps - 1))
    states, _ = lax.fori_loop(0, high, first_pass, (zeros, before), unroll=16)
    for n in range(modes):
        state[n * blocks : (n + 1) * blocks, :] = states[n]

    across = jnp.ones_like(rate)
    power, left = rate, high
    while left:
        if left & 1:
            across = across * power
        left >>= 1
        if left:
            power = power * power
    entering = jnp.zeros((modes, chans), F32)
    for b in range(blocks):
        enter[pl.ds(b, modes, stride=blocks), :] = entering
        entering = across * entering + state[pl.ds(b, modes, stride=blocks), :]

    gain = residue_ref[:, channels] * jnp.sqrt(1.0 - rate * rate)
    gains = [jnp.broadcast_to(gain[n : n + 1, :], (blocks, chans)) for n in range(modes)]

    def second_pass(t, states):
        mixed = mixed_s[t]
        states = tuple(decay[n] * states[n] + mixed for n in range(modes))
        terms = [gains[n] * states[n] for n in range(modes)]
        while len(terms) > 1:
            terms = [sum(terms[i : i + 2][1:], terms[i]) for i in range(0, len(terms), 2)]
        rows[0, pl.ds(t, blocks, stride=high), :] = terms[0]
        return states

    begin = tuple(enter[n * blocks : (n + 1) * blocks, :] for n in range(modes))
    lax.fori_loop(0, high, second_pass, begin, unroll=16)
    for s in range(chips):
        keep_ref[s] = rows[0, columns(2 * order[s] + core, high), :].astype(BF16)
        send_ref[s] = rows[0, columns(2 * order[chips + s] + 1 - core, high), :].astype(BF16)


def hyena(order, parts, short_filter, mode_decay, residue, blocks):
    rows_count, lanes = parts[0].shape
    chans = lanes // 2
    total = 2 * rows_count
    high = total // blocks
    modes, taps = mode_decay.shape[0], short_filter.shape[0]
    scratch = [
        pltpu.VMEM((2, total, chans), F32),
        pltpu.VMEM((high, blocks, chans), F32),
        pltpu.VMEM((modes * blocks, chans), F32),
        pltpu.VMEM((modes * blocks, chans), F32),
        pltpu.VMEM((taps - 1, 2, blocks, chans), F32),
    ]
    arrays = [*parts, short_filter, mode_decay, residue]
    kernel = functools.partial(hyena_kernel, blocks=blocks)
    shapes = [((blocks // 2, high, chans), BF16)] * 2
    return local(kernel, "hyena", shapes, order, arrays, scratch)


def payloads(order, q_next, q_in, keep, other):
    chips, high, _ = keep.shape
    chans = q_next.shape[1]

    def kernel(order, next_ref, in_ref, keep_ref, other_ref, second_ref, *out_refs):
        second_ref[...] = (next_ref[...] + in_ref[:, :chans].astype(F32)).astype(BF16)
        for s, out_ref in enumerate(out_refs):
            out_ref[0] = keep_ref[s]
            out_ref[1] = other_ref[s]

    shapes = [(q_next.shape, BF16)] + [((2, high, keep.shape[2]), BF16)] * chips
    return local(kernel, "payloads", shapes, order, [q_next, q_in, keep, other])


def gate(scalars, queries, long_parts, w_out, groups):
    rows, chans = queries[0].shape
    chips = len(long_parts)
    part = long_parts[0].shape[2]
    wide = w_out.shape[1] // groups
    first_pick = 2 * chips + 3

    def kernel(scalars, *refs):
        query_refs, long_refs = refs[: len(queries)], refs[len(queries) : len(queries) + chips]
        w_ref, gated_ref, pair_ref, side_ref, query = refs[len(queries) + chips :]
        core = scalars[2 * chips]
        own_ref, second_ref, first_ref = query_refs
        query[...] = own_ref[...] + second_ref[...].astype(F32) + first_ref[...].astype(F32)
        for s, ref in enumerate(long_refs):
            for h in range(2):
                at = columns(2 * scalars[s] + (core ^ h), part)
                gated_ref[:, at] = (query[:, at] * ref[h].astype(F32)).astype(BF16)
        for pick, out_ref in enumerate((pair_ref, side_ref)):
            total = jnp.dot(
                gated_ref[...],
                w_ref[:, columns(scalars[first_pick + pick], wide)],
                preferred_element_type=F32,
            )
            out_ref[...] = total.astype(BF16)

    shapes = [((rows, chans), BF16), ((rows, wide), BF16), ((rows, wide), BF16)]
    arrays = [*queries, *long_parts, w_out]
    scratch = [pltpu.VMEM((rows, chans), F32)]
    return local(kernel, "gate", shapes, scalars, arrays, scratch)


def out_columns(picks, pick, x, w_out, groups, kind):
    wide = w_out.shape[1] // groups

    def kernel(picks, x_ref, w_ref, out_ref):
        total = jnp.dot(
            x_ref[...], w_ref[:, columns(picks[pick], wide)], preferred_element_type=F32
        )
        out_ref[...] = total.astype(kind)

    return local(kernel, "out_columns", [((x.shape[0], wide), kind)], picks, [x, w_out])


def line_picks():
    z = lax.axis_index("dp")
    table = [[3, 0, 3, 0], [1, 2, 1, 2], [2, 3, 0, 1], [0, 1, 2, 3], [0, 1, 1, 0]]
    return jnp.stack([sum(jnp.where(z == i, v, 0) for i, v in enumerate(row)) for row in table])


def output_over_line(picks, gated, pair, side, w_out, groups):
    pair_in = lax.ppermute(pair, "dp", [(0, 1), (1, 0), (2, 3), (3, 2)])
    far = out_columns(picks, 2, gated, w_out, groups, BF16)
    middle_in = lax.ppermute(side, "dp", [(1, 2), (2, 1)])
    side, far = lax.optimization_barrier((side, far))
    end_in = lax.ppermute(far, "dp", [(0, 2), (3, 1)])

    def add(picks, far_ref, pair_ref, side_ref, out_ref):
        value = far_ref[...].astype(F32) + pair_ref[...].astype(F32)
        out_ref[...] = jnp.where(picks[4] == 1, value.astype(BF16), side_ref[...])

    last = local(add, "last_step", [(far.shape, BF16)], picks, [far, pair_in, side])
    gated, last = lax.optimization_barrier((gated, last))
    last_in = lax.ppermute(last, "dp", [(0, 1), (1, 3), (2, 0), (3, 2)])
    own = out_columns(picks, 3, gated, w_out, groups, F32)

    def early(picks, own_ref, pair_ref, *refs):
        inner = picks[4] == 1
        value = own_ref[...] + jnp.where(inner, 0.0, pair_ref[...].astype(F32))
        for ref in refs[:-1]:
            value = value + ref[...].astype(F32)
        refs[-1][...] = value

    def total(picks, early_ref, last_ref, out_ref):
        out_ref[...] = (early_ref[...] + last_ref[...].astype(F32)).astype(BF16)

    own = local(early, "early", [(own.shape, F32)], picks, [own, pair_in, middle_in, end_in])
    return local(total, "total", [(own.shape, BF16)], picks, [own, last_in])


def on_device_chips(tokens, w_in, short_filter, mode_decay, residue, w_out):
    count, groups = lax.axis_size("ctx"), lax.axis_size("dp")
    chips = count // 2
    me = lax.axis_index("ctx")
    core, chip = me % 2, me // 2

    def across(i, slot):
        high_bit, low_bit = slot >> 1, slot & 1
        step = (high_bit + 2 * low_bit) if i % 2 == 0 else (2 * high_bit + low_bit)
        return i ^ (2 * step)

    def route(slot):
        return [(i, across(i, slot)) for i in range(count)]

    def relative(slot, core):
        high_bit, low_bit = slot >> 1, slot & 1
        return jnp.where(core == 0, high_bit + 2 * low_bit, 2 * high_bit + low_bit)

    slot_chip = [chip ^ relative(s, core) for s in range(chips)]
    slot_other = [chip ^ relative(s, 1 - core) for s in range(chips)]
    order = jnp.stack(slot_chip + slot_other + [core, me, lax.axis_index("dp") % 2]).astype(jnp.int32)
    picks = line_picks().astype(jnp.int32)
    both_scalars = jnp.concatenate([order, picks])
    order, picks, both_scalars = lax.optimization_barrier((order, picks, both_scalars))

    own_w = jnp.transpose(w_in, (1, 0, 2))
    swap = [(i, i ^ 1) for i in range(count)]

    other_w = lax.ppermute(own_w, "ctx", swap)
    xs = cut(order, tokens, chips)
    own_w, xs = lax.optimization_barrier((own_w, xs))
    own_w = stage(own_w)
    half = lax.ppermute(xs[3], "ctx", route(3))
    other = lax.ppermute(half, "dp", [(i, i ^ 1) for i in range(groups)])
    xs = [xs[0]] + [lax.ppermute(xs[s], "ctx", route(s)) for s in (1, 2)]
    xs.append(join_rows(order, half, other))

    both = project_mix(order, xs, own_w, other_w, [3], BF16)
    both_in = lax.ppermute(both, "ctx", route(2))
    xs, both = lax.optimization_barrier((xs, both))
    first = project_mix(order, xs, own_w, other_w, [2], BF16)
    first_in = lax.ppermute(first, "ctx", route(2))
    xs, first = lax.optimization_barrier((xs, first))
    rest, ends = project_mix(order, xs, own_w, other_w, [1, 0], F32, 16)
    second, swap_second = second_share(order, rest, both_in, chips)
    second_in = lax.ppermute(second, "ctx", route(1))
    swap_second = lax.ppermute(swap_second, "ctx", [(i, j ^ 1) for i, j in route(1)])

    xs, ends, second = lax.optimization_barrier((xs, ends, second))
    before = lax.ppermute(ends, "ctx", swap)
    q_own, q_next, q_first, q_both = project_query(order, xs, before, own_w, other_w, short_filter)
    q_own, w_out = lax.optimization_barrier((q_own, w_out))
    w_out = stage(w_out)
    q_own, w_out, rest = lax.optimization_barrier((q_own, w_out, rest))

    own, other_half = first_share(order, rest, first_in, chips)
    other_half = lax.ppermute(other_half, "ctx", swap)
    q_both, q_first, own = lax.optimization_barrier((q_both, q_first, own))
    q_both = lax.ppermute(q_both, "ctx", route(2))
    q_first = lax.ppermute(q_first, "ctx", route(2))
    parts = [own, other_half, second_in, swap_second]
    keep, send = hyena(order, parts, short_filter, mode_decay, residue, count)
    other_long = lax.ppermute(send, "ctx", swap)
    q_second, *long_parts = payloads(order, q_next, q_both, keep, other_long)
    q_second = lax.ppermute(q_second, "ctx", route(1))
    long_parts = [long_parts[0]] + [lax.ppermute(long_parts[s], "ctx", route(s)) for s in (1, 2, 3)]
    queries = [q_own, q_second, q_first]
    gated, pair, side = gate(both_scalars, queries, long_parts, w_out, groups)
    return output_over_line(picks, gated, pair, side, w_out, groups)


def solution(mesh):
    count, groups = mesh.shape["ctx"], mesh.shape["dp"]

    def on_device(tokens, w_in, *rest):
        lanes = w_in.shape[2] // count
        chips = count == 8 and groups == 4 and w_in.shape[2] % count == 0 and lanes % 128 == 0
        return (on_device_chips if chips else on_device_any)(tokens, w_in, *rest)

    return jax.shard_map(
        on_device,
        mesh=mesh,
        in_specs=(
            P("ctx", None),
            P("ctx", None, "dp"),
            P(None, None, "dp"),
            P(None, "dp"),
            P(None, "dp"),
            P("dp", None),
        ),
        out_specs=P("ctx", "dp"),
        check_vma=False,
    )
```

```python
import functools

import jax
import jax.numpy as jnp
from jax import lax
from jax.experimental import pallas as pl
from jax.experimental.pallas import tpu as pltpu
from jax.sharding import PartitionSpec as P

BLK = 64
F32, BF16 = jnp.float32, jnp.bfloat16
VMEM_LIMIT = 12 * 1024 * 1024


def from_behind(block, axis, distance):
    devices = range(lax.axis_size(axis))
    route = [(i - distance, i) for i in devices if i - distance in devices]
    return lax.ppermute(block, axis, route)


def prefix(value, axis, join, neutral):
    count, mine = (lax.axis_size(axis), lax.axis_index(axis))
    pieces = jax.tree.map(lambda part: lax.all_gather(part, axis), value)
    subtotal = jax.tree.map(
        lambda part, zero: jnp.full_like(part, 0) + jnp.asarray(zero, part.dtype), value, neutral
    )

    def lap(position, subtotal):
        longer = join(subtotal, jax.tree.map(lambda part: part[position], pieces))
        return jax.tree.map(lambda new, old: jnp.where(position < mine, new, old), longer, subtotal)

    return lax.fori_loop(0, count - 1, lap, subtotal)


def on_device_any(tokens, w_in, short_filter, mode_decay, residue, w_out):
    row_count = tokens.shape[0]
    chan_count = w_in.shape[2]
    short_count = short_filter.shape[0]
    mode_count = mode_decay.shape[0]
    earlier_rows = from_behind(tokens[row_count - (short_count - 1) :], "ctx", 1)
    source = jnp.concatenate([earlier_rows, tokens], 0)
    projected = jnp.einsum(
        "td,dgc->tgc",
        source,
        lax.all_gather(w_in, "ctx", axis=0, tiled=True),
        preferred_element_type=jnp.float32,
    )
    featured = jnp.zeros((row_count, 3, chan_count), jnp.float32)
    for j in range(short_count):
        featured = (
            featured
            + short_filter[j] * projected[short_count - 1 - j : short_count - 1 - j + row_count]
        )
    mixed = (featured[:, 1] * featured[:, 2]).astype(jnp.bfloat16)
    medium = mixed.astype(jnp.float32)
    highest = lax.Precision.HIGHEST
    mode_gain = residue * jnp.sqrt(1.0 - mode_decay * mode_decay)
    block_len = BLK
    block_times = jnp.arange(block_len).astype(jnp.float32)
    power_in = jnp.power(mode_decay[None], block_times[:, None, None])
    kernel_head = jnp.sum(mode_gain[None] * power_in, 1)
    lag_index = jnp.arange(block_len)[:, None] - jnp.arange(block_len)[None, :]
    toeplitz = jnp.where(
        (lag_index >= 0)[:, :, None], kernel_head[jnp.clip(lag_index, 0, block_len - 1)], 0.0
    )
    carry_weights = mode_gain[None] * power_in * mode_decay[None]
    state_weights = power_in[::-1]
    decay_block = jnp.power(mode_decay, float(block_len))
    blocks = medium.reshape(row_count // block_len, block_len, chan_count)

    def block_step(carried, block_rows):
        inner = jnp.einsum("tsc,sc->tc", toeplitz, block_rows, precision=highest)
        inner = inner + jnp.einsum("tnc,nc->tc", carry_weights, carried, precision=highest)
        carried = decay_block * carried + jnp.einsum(
            "snc,sc->nc", state_weights, block_rows, precision=highest
        )
        return (carried, inner)

    zero_state = jnp.zeros((mode_count, chan_count), jnp.float32)
    local_end, local_part = lax.scan(block_step, zero_state, blocks)
    local_part = local_part.reshape(row_count, chan_count)
    decay_device = jnp.power(mode_decay, float(row_count))

    def combine_states(earlier, later):
        return (earlier[0] * later[0], later[0] * earlier[1] + later[1])

    identity = (jnp.ones((mode_count, chan_count), jnp.float32), zero_state)
    scanned = prefix((decay_device, local_end), "ctx", combine_states, identity)
    entering = scanned[1]
    row_times = jnp.arange(1, row_count + 1).astype(jnp.float32)
    entry_weights = mode_gain[None] * jnp.power(mode_decay[None], row_times[:, None, None])
    long_part = local_part + jnp.einsum("tnc,nc->tc", entry_weights, entering, precision=highest)
    gated = (featured[:, 0] * long_part).astype(jnp.bfloat16)
    out_term = jnp.dot(gated, w_out, preferred_element_type=jnp.float32)
    return lax.psum_scatter(out_term.astype(jnp.bfloat16), "dp", scatter_dimension=1, tiled=True)


def local(kernel, name, shapes, scalars, arrays, scratch=()):
    whole = pl.BlockSpec(memory_space=pltpu.VMEM)
    out = [jax.ShapeDtypeStruct(*shape) for shape in shapes]
    return pl.pallas_call(
        kernel,
        out_shape=out if len(out) > 1 else out[0],
        in_specs=[pl.BlockSpec(memory_space=pltpu.SMEM)] + [whole] * len(arrays),
        out_specs=[whole] * len(out) if len(out) > 1 else whole,
        scratch_shapes=list(scratch),
        compiler_params=pltpu.CompilerParams(vmem_limit_bytes=VMEM_LIMIT),
        name=name,
    )(scalars, *arrays)


def columns(index, wide):
    return pl.ds(pl.multiple_of(index * wide, wide), wide)


def cut(order, tokens, pieces):
    high, wide = tokens.shape[0], tokens.shape[1] // pieces

    def kernel(order, tokens_ref, *out_refs):
        here = columns(order[2 * pieces + 2], high // 2)
        out_refs[pieces - 1][...] = tokens_ref[here, columns(order[pieces - 1], wide)]
        for s, out_ref in enumerate(out_refs[: pieces - 1]):
            out_ref[...] = tokens_ref[:, columns(order[s], wide)]

    shapes = [((high, wide), tokens.dtype)] * (pieces - 1) + [((high // 2, wide), tokens.dtype)]
    return local(kernel, "cut", shapes, order, [tokens])


def stage(array):
    def kernel(array_ref, out_ref, sem):
        copy = pltpu.make_async_copy(array_ref, out_ref, sem)
        copy.start()
        copy.wait()

    return pl.pallas_call(
        kernel,
        out_shape=jax.ShapeDtypeStruct(array.shape, array.dtype),
        in_specs=[pl.BlockSpec(memory_space=pl.ANY)],
        out_specs=pl.BlockSpec(memory_space=pltpu.VMEM),
        scratch_shapes=[pltpu.SemaphoreType.DMA],
        compiler_params=pltpu.CompilerParams(vmem_limit_bytes=VMEM_LIMIT),
        name="stage",
    )(array)


def gather_rows(core, x_refs, rows):
    high, depth = x_refs[0].shape[0], rows.shape[2]
    for i, x_ref in enumerate(x_refs):
        for h in range(2):
            rows[core ^ h, i * high : (i + 1) * high, :] = x_ref[:, h * depth : (h + 1) * depth]


def project_mix(order, xs, own, other, slots, kind, ends=0):
    chips = len(xs)
    streams, depth, chans = own.shape
    high = xs[0].shape[0]
    wide = chans // chips
    half = wide // 2

    def kernel(order, *refs):
        x_refs, (own_ref, other_ref, out_ref, *end_refs, rows) = refs[:chips], refs[chips:]
        core = order[2 * chips]
        gather_rows(core, x_refs, rows)
        for end_ref in end_refs:
            for s in range(chips):
                end_ref[s] = x_refs[s][high - ends :, :]
        for i, slot in enumerate(slots):
            at = columns(order[slot], wide)
            for g in range(1, streams):
                total = jnp.dot(rows[0], own_ref[g, :, at], preferred_element_type=F32)
                total += jnp.dot(rows[1], other_ref[g, :, at], preferred_element_type=F32)
                total = total.astype(kind)
                lanes = slice((g - 1) * half, g * half)
                for h in range(2):
                    out_ref[i, core ^ h, :, lanes] = total[:, h * half : (h + 1) * half]

    shape = (len(slots), 2, chips * high, (streams - 1) * half)
    scratch = [pltpu.VMEM((2, chips * high, depth), BF16)]
    shapes = [(shape, kind)] + ([((chips, ends, 2 * depth), BF16)] if ends else [])
    return local(kernel, "project_mix", shapes, order, [*xs, own, other], scratch)


def early_share(order, own_rows, mine, other_rows, own, other, slot, chips):
    half, wide_x = mine.shape
    high = 2 * half
    streams, depth, chans = own.shape
    wide = chans // chips
    lanes = wide // 2
    place = order.shape[0] - 1

    def kernel(order, own_rows_ref, mine_ref, there_ref, own_ref, other_ref, joined_ref, out_ref, rows):
        core = order[2 * chips]
        joined_ref[columns(order[place], half), :] = mine_ref[...]
        joined_ref[columns(1 - order[place], half), :] = there_ref[...]
        gather_rows(core, (own_rows_ref, joined_ref), rows)
        at = columns(order[slot], wide)
        for g in range(1, streams):
            total = jnp.dot(rows[0], own_ref[g, :, at], preferred_element_type=F32)
            total += jnp.dot(rows[1], other_ref[g, :, at], preferred_element_type=F32)
            for h in range(2):
                to = slice((g - 1) * lanes, g * lanes)
                out_ref[core ^ h, :, to] = total[:, h * lanes : (h + 1) * lanes].astype(BF16)

    shapes = [((high, wide_x), BF16), ((2, 2 * high, (streams - 1) * lanes), BF16)]
    scratch = [pltpu.VMEM((2, 2 * high, depth), BF16)]
    arrays = [own_rows, mine, other_rows, own, other]
    return local(kernel, "early_share", shapes, order, arrays, scratch)


def rest_share(order, xs, early, own, other, slot, chips):
    high = xs[0].shape[0]
    streams, depth, chans = own.shape
    wide = chans // chips
    lanes = wide // 2

    def kernel(order, first_ref, second_ref, early_ref, own_ref, other_ref, out_ref, rows):
        core = order[2 * chips]
        gather_rows(core, (first_ref, second_ref), rows)
        at = columns(order[slot], wide)
        for h in range(2):
            out_ref[0, h, :high, :] = early_ref[h, :high, :]
            out_ref[0, h, 3 * high :, :] = early_ref[h, high:, :]
        for g in range(1, streams):
            total = jnp.dot(rows[0], own_ref[g, :, at], preferred_element_type=F32)
            total += jnp.dot(rows[1], other_ref[g, :, at], preferred_element_type=F32)
            for h in range(2):
                to = slice((g - 1) * lanes, g * lanes)
                out_ref[0, core ^ h, high : 3 * high, to] = total[
                    :, h * lanes : (h + 1) * lanes
                ].astype(BF16)

    shapes = [((1, 2, chips * high, (streams - 1) * lanes), BF16)]
    scratch = [pltpu.VMEM((2, 2 * high, depth), BF16)]
    return local(kernel, "rest_share", shapes, order, [*xs, early, own, other], scratch)


def project_query(order, xs, before, own, other, short_filter):
    chips = len(xs)
    _, depth, chans = own.shape
    high = xs[0].shape[0]
    some = before.shape[1]
    step = some + high
    taps = short_filter.shape[0]
    tile = min(chans, 256)

    def kernel(order, *refs):
        x_refs = refs[:chips]
        before_ref, own_ref, other_ref, filt_ref, *out_refs, rows, ends, total = refs[chips:]
        core = order[2 * chips]
        ends[0] = jnp.zeros_like(ends[0])
        for s in range(chips):
            ends[order[chips + s] + 1] = before_ref[s]
        for i, x_ref in enumerate(x_refs):
            end = ends[order[i] + core]
            for h in range(2):
                lanes = slice(h * depth, (h + 1) * depth)
                rows[core ^ h, i * step : i * step + some, :] = end[:, lanes]
                rows[core ^ h, i * step + some : (i + 1) * step, :] = x_ref[:, lanes]
        for at in (slice(i, i + tile) for i in range(0, chans, tile)):
            total[...] = jnp.dot(
                rows[0], own_ref[0, :, at], preferred_element_type=F32
            ) + jnp.dot(rows[1], other_ref[0, :, at], preferred_element_type=F32)
            for i in range(chips):
                first = i * step + some
                value = filt_ref[0, 0:1, at] * total[first : first + high, :]
                for j in range(1, taps):
                    value = value + filt_ref[j, 0:1, at] * total[first - j : first - j + high, :]
                out_refs[i][:, at] = value.astype(out_refs[i].dtype)

    shapes = [((high, chans), F32 if i < 2 else BF16) for i in range(chips)]
    scratch = [
        pltpu.VMEM((2, chips * step, depth), BF16),
        pltpu.VMEM((chips + 1, some, 2 * depth), BF16),
        pltpu.VMEM((chips * step, tile), F32),
    ]
    arrays = [*xs, before, own, other, short_filter]
    return local(kernel, "project_query", shapes, order, arrays, scratch)


def second_share(order, rest, both_in, chips):
    _, _, rows, lanes = rest.shape
    high = rows // chips

    def kernel(order, rest_ref, both_ref, *out_refs):
        for h, out_ref in enumerate(out_refs):
            for s in range(chips):
                here, there = (slice(i * high, (i + 1) * high) for i in (s, s ^ 2))
                term = both_ref[0, h, there, :].astype(F32)
                out_ref[here, :] = (rest_ref[0, h, here, :] + term).astype(BF16)

    shapes = [((rows, lanes), BF16)] * 2
    return local(kernel, "second_share", shapes, order, [rest, both_in])


def first_share(order, rest, first_in, chips):
    _, _, rows, lanes = rest.shape
    high = rows // chips

    def kernel(order, rest_ref, first_ref, own_ref, other_ref):
        for h, out_ref in ((1, other_ref), (0, own_ref)):
            for s in range(chips):
                here, first = (slice(i * high, (i + 1) * high) for i in (s, s ^ 2))
                total = rest_ref[1, h, here, :] + first_ref[0, h, first, :].astype(F32)
                out_ref[here, :] = total.astype(out_ref.dtype)

    shapes = [((rows, lanes), F32), ((rows, lanes), BF16)]
    return local(kernel, "first_share", shapes, order, [rest, first_in])


def hyena_kernel(
    order, own_ref, swap_ref, second_ref, swap_second_ref, filt_ref, decay_ref, residue_ref,
    keep_ref, send_ref, rows, mixed_s, state, enter, edge, *, blocks,
):
    high = rows.shape[1] // blocks
    chans = rows.shape[2]
    modes = decay_ref.shape[0]
    taps = filt_ref.shape[0]
    chips = blocks // 2
    core = order[2 * chips]
    channels = columns(order[2 * chips + 1], chans)

    for s in range(chips):
        here, second = (slice(i * high, (i + 1) * high) for i in (s, s ^ 1))
        own_at = columns(2 * order[s] + core, high)
        swap_at = columns(2 * order[chips + s] + 1 - core, high)
        for g in range(2):
            lanes = slice(g * chans, (g + 1) * chans)
            rows[g, own_at, :] = own_ref[here, lanes] + second_ref[second, lanes].astype(F32)
            rows[g, swap_at, :] = swap_ref[here, lanes].astype(F32) + swap_second_ref[
                second, lanes
            ].astype(F32)

    for k in range(1, taps):
        for g in range(2):
            edge[k - 1, g, 0:1, :] = jnp.zeros((1, chans), F32)
            for b in range(1, blocks):
                edge[k - 1, g, b : b + 1, :] = rows[g, b * high - k : b * high - k + 1, :]

    rate = decay_ref[:, channels]
    taps_of = [filt_ref[j, :, channels] for j in range(taps)]
    decay = [jnp.broadcast_to(rate[n : n + 1, :], (blocks, chans)) for n in range(modes)]
    filt = [
        [jnp.broadcast_to(taps_of[j][g + 1 : g + 2, :], (blocks, chans)) for g in range(2)]
        for j in range(taps)
    ]

    def first_pass(t, carry):
        states, earlier = carry
        now = [rows[g, pl.ds(t, blocks, stride=high), :] for g in range(2)]
        featured = []
        for g in range(2):
            value = filt[0][g] * now[g]
            for k in range(1, taps):
                value = value + filt[k][g] * earlier[k - 1][g]
            featured.append(value)
        mixed = (featured[0] * featured[1]).astype(BF16).astype(F32)
        mixed_s[t] = mixed
        states = tuple(decay[n] * states[n] + mixed for n in range(modes))
        return states, (tuple(now),) + tuple(earlier[:-1])

    zeros = tuple(jnp.zeros((blocks, chans), F32) for _ in range(modes))
    before = tuple(tuple(edge[k, g] for g in range(2)) for k in range(taps - 1))
    states, _ = lax.fori_loop(0, high, first_pass, (zeros, before), unroll=16)
    for n in range(modes):
        state[n * blocks : (n + 1) * blocks, :] = states[n]

    across = jnp.ones_like(rate)
    power, left = rate, high
    while left:
        if left & 1:
            across = across * power
        left >>= 1
        if left:
            power = power * power
    entering = jnp.zeros((modes, chans), F32)
    for b in range(blocks):
        enter[pl.ds(b, modes, stride=blocks), :] = entering
        entering = across * entering + state[pl.ds(b, modes, stride=blocks), :]

    gain = residue_ref[:, channels] * jnp.sqrt(1.0 - rate * rate)
    gains = [jnp.broadcast_to(gain[n : n + 1, :], (blocks, chans)) for n in range(modes)]

    def second_pass(t, states):
        mixed = mixed_s[t]
        states = tuple(decay[n] * states[n] + mixed for n in range(modes))
        terms = [gains[n] * states[n] for n in range(modes)]
        while len(terms) > 1:
            terms = [sum(terms[i : i + 2][1:], terms[i]) for i in range(0, len(terms), 2)]
        rows[0, pl.ds(t, blocks, stride=high), :] = terms[0]
        return states

    begin = tuple(enter[n * blocks : (n + 1) * blocks, :] for n in range(modes))
    lax.fori_loop(0, high, second_pass, begin, unroll=16)
    for s in range(chips):
        keep_ref[s] = rows[0, columns(2 * order[s] + core, high), :].astype(BF16)
        send_ref[s] = rows[0, columns(2 * order[chips + s] + 1 - core, high), :].astype(BF16)


def hyena(order, parts, short_filter, mode_decay, residue, blocks):
    rows_count, lanes = parts[0].shape
    chans = lanes // 2
    total = 2 * rows_count
    high = total // blocks
    modes, taps = mode_decay.shape[0], short_filter.shape[0]
    scratch = [
        pltpu.VMEM((2, total, chans), F32),
        pltpu.VMEM((high, blocks, chans), F32),
        pltpu.VMEM((modes * blocks, chans), F32),
        pltpu.VMEM((modes * blocks, chans), F32),
        pltpu.VMEM((taps - 1, 2, blocks, chans), F32),
    ]
    arrays = [*parts, short_filter, mode_decay, residue]
    kernel = functools.partial(hyena_kernel, blocks=blocks)
    shapes = [((blocks // 2, high, chans), BF16)] * 2
    return local(kernel, "hyena", shapes, order, arrays, scratch)


def payloads(order, q_next, q_in, keep, other):
    chips, high, _ = keep.shape
    chans = q_next.shape[1]

    def kernel(order, next_ref, in_ref, keep_ref, other_ref, second_ref, *out_refs):
        second_ref[...] = (next_ref[...] + in_ref[:, :chans].astype(F32)).astype(BF16)
        for s, out_ref in enumerate(out_refs):
            out_ref[0] = keep_ref[s]
            out_ref[1] = other_ref[s]

    shapes = [(q_next.shape, BF16)] + [((2, high, keep.shape[2]), BF16)] * chips
    return local(kernel, "payloads", shapes, order, [q_next, q_in, keep, other])


def gate(scalars, queries, long_parts, w_out, groups):
    rows, chans = queries[0].shape
    chips = len(long_parts)
    part = long_parts[0].shape[2]
    wide = w_out.shape[1] // groups
    first_pick = 2 * chips + 3

    def kernel(scalars, *refs):
        query_refs, long_refs = refs[: len(queries)], refs[len(queries) : len(queries) + chips]
        w_ref, gated_ref, pair_ref, side_ref, query = refs[len(queries) + chips :]
        core = scalars[2 * chips]
        own_ref, second_ref, first_ref = query_refs
        query[...] = own_ref[...] + second_ref[...].astype(F32) + first_ref[...].astype(F32)
        for s, ref in enumerate(long_refs):
            for h in range(2):
                at = columns(2 * scalars[s] + (core ^ h), part)
                gated_ref[:, at] = (query[:, at] * ref[h].astype(F32)).astype(BF16)
        for pick, out_ref in enumerate((pair_ref, side_ref)):
            total = jnp.dot(
                gated_ref[...],
                w_ref[:, columns(scalars[first_pick + pick], wide)],
                preferred_element_type=F32,
            )
            out_ref[...] = total.astype(BF16)

    shapes = [((rows, chans), BF16), ((rows, wide), BF16), ((rows, wide), BF16)]
    arrays = [*queries, *long_parts, w_out]
    scratch = [pltpu.VMEM((rows, chans), F32)]
    return local(kernel, "gate", shapes, scalars, arrays, scratch)


def out_columns(picks, pick, x, w_out, groups, kind):
    wide = w_out.shape[1] // groups

    def kernel(picks, x_ref, w_ref, out_ref):
        total = jnp.dot(
            x_ref[...], w_ref[:, columns(picks[pick], wide)], preferred_element_type=F32
        )
        out_ref[...] = total.astype(kind)

    return local(kernel, "out_columns", [((x.shape[0], wide), kind)], picks, [x, w_out])


def line_picks():
    z = lax.axis_index("dp")
    table = [[3, 0, 3, 0], [1, 2, 1, 2], [2, 3, 0, 1], [0, 1, 2, 3], [0, 1, 1, 0]]
    return jnp.stack([sum(jnp.where(z == i, v, 0) for i, v in enumerate(row)) for row in table])


def output_over_line(picks, gated, pair, side, w_out, groups):
    pair_in = lax.ppermute(pair, "dp", [(0, 1), (1, 0), (2, 3), (3, 2)])
    far = out_columns(picks, 2, gated, w_out, groups, BF16)
    middle_in = lax.ppermute(side, "dp", [(1, 2), (2, 1)])
    side, far = lax.optimization_barrier((side, far))
    end_in = lax.ppermute(far, "dp", [(0, 2), (3, 1)])

    def add(picks, far_ref, pair_ref, side_ref, out_ref):
        value = far_ref[...].astype(F32) + pair_ref[...].astype(F32)
        out_ref[...] = jnp.where(picks[4] == 1, value.astype(BF16), side_ref[...])

    last = local(add, "last_step", [(far.shape, BF16)], picks, [far, pair_in, side])
    gated, last = lax.optimization_barrier((gated, last))
    last_in = lax.ppermute(last, "dp", [(0, 1), (1, 3), (2, 0), (3, 2)])
    own = out_columns(picks, 3, gated, w_out, groups, F32)

    def early(picks, own_ref, pair_ref, *refs):
        inner = picks[4] == 1
        value = own_ref[...] + jnp.where(inner, 0.0, pair_ref[...].astype(F32))
        for ref in refs[:-1]:
            value = value + ref[...].astype(F32)
        refs[-1][...] = value

    def total(picks, early_ref, last_ref, out_ref):
        out_ref[...] = (early_ref[...] + last_ref[...].astype(F32)).astype(BF16)

    own = local(early, "early", [(own.shape, F32)], picks, [own, pair_in, middle_in, end_in])
    return local(total, "total", [(own.shape, BF16)], picks, [own, last_in])


def on_device_chips(tokens, w_in, short_filter, mode_decay, residue, w_out):
    count, groups = lax.axis_size("ctx"), lax.axis_size("dp")
    chips = count // 2
    me = lax.axis_index("ctx")
    core, chip = me % 2, me // 2

    def across(i, slot):
        high_bit, low_bit = slot >> 1, slot & 1
        step = (high_bit + 2 * low_bit) if i % 2 == 0 else (2 * high_bit + low_bit)
        return i ^ (2 * step)

    def route(slot):
        return [(i, across(i, slot)) for i in range(count)]

    def relative(slot, core):
        high_bit, low_bit = slot >> 1, slot & 1
        return jnp.where(core == 0, high_bit + 2 * low_bit, 2 * high_bit + low_bit)

    slot_chip = [chip ^ relative(s, core) for s in range(chips)]
    slot_other = [chip ^ relative(s, 1 - core) for s in range(chips)]
    order = jnp.stack(slot_chip + slot_other + [core, me, lax.axis_index("dp") % 2]).astype(jnp.int32)
    picks = line_picks().astype(jnp.int32)
    both_scalars = jnp.concatenate([order, picks])
    order, picks, both_scalars = lax.optimization_barrier((order, picks, both_scalars))

    own_w = jnp.transpose(w_in, (1, 0, 2))
    swap = [(i, i ^ 1) for i in range(count)]

    other_w = lax.ppermute(own_w, "ctx", swap)
    xs = cut(order, tokens, chips)
    own_w, xs = lax.optimization_barrier((own_w, xs))
    own_w = stage(own_w)
    half = lax.ppermute(xs[3], "ctx", route(3))
    other = lax.ppermute(half, "dp", [(i, i ^ 1) for i in range(groups)])
    xs = [xs[0]] + [lax.ppermute(xs[s], "ctx", route(s)) for s in (1, 2)]
    joined, early = early_share(order, xs[0], half, other, own_w, other_w, 3, chips)
    xs.append(joined)

    both = rest_share(order, xs[1:3], early, own_w, other_w, 3, chips)
    both_in = lax.ppermute(both, "ctx", route(2))
    xs, both = lax.optimization_barrier((xs, both))
    first = project_mix(order, xs, own_w, other_w, [2], BF16)
    first_in = lax.ppermute(first, "ctx", route(2))
    xs, first = lax.optimization_barrier((xs, first))
    rest, ends = project_mix(order, xs, own_w, other_w, [1, 0], F32, 16)
    second, swap_second = second_share(order, rest, both_in, chips)
    second_in = lax.ppermute(second, "ctx", route(1))
    swap_second = lax.ppermute(swap_second, "ctx", [(i, j ^ 1) for i, j in route(1)])

    xs, ends, second = lax.optimization_barrier((xs, ends, second))
    before = lax.ppermute(ends, "ctx", swap)
    q_own, q_next, q_first, q_both = project_query(order, xs, before, own_w, other_w, short_filter)
    q_own, w_out = lax.optimization_barrier((q_own, w_out))
    w_out = stage(w_out)
    q_own, w_out, rest = lax.optimization_barrier((q_own, w_out, rest))

    own, other_half = first_share(order, rest, first_in, chips)
    other_half = lax.ppermute(other_half, "ctx", swap)
    q_both, q_first, own = lax.optimization_barrier((q_both, q_first, own))
    q_both = lax.ppermute(q_both, "ctx", route(2))
    q_first = lax.ppermute(q_first, "ctx", route(2))
    parts = [own, other_half, second_in, swap_second]
    keep, send = hyena(order, parts, short_filter, mode_decay, residue, count)
    other_long = lax.ppermute(send, "ctx", swap)
    q_second, *long_parts = payloads(order, q_next, q_both, keep, other_long)
    q_second = lax.ppermute(q_second, "ctx", route(1))
    long_parts = [long_parts[0]] + [lax.ppermute(long_parts[s], "ctx", route(s)) for s in (1, 2, 3)]
    queries = [q_own, q_second, q_first]
    gated, pair, side = gate(both_scalars, queries, long_parts, w_out, groups)
    return output_over_line(picks, gated, pair, side, w_out, groups)


def solution(mesh):
    count, groups = mesh.shape["ctx"], mesh.shape["dp"]

    def on_device(tokens, w_in, *rest):
        lanes = w_in.shape[2] // count
        chips = count == 8 and groups == 4 and w_in.shape[2] % count == 0 and lanes % 128 == 0
        return (on_device_chips if chips else on_device_any)(tokens, w_in, *rest)

    return jax.shard_map(
        on_device,
        mesh=mesh,
        in_specs=(
            P("ctx", None),
            P("ctx", None, "dp"),
            P(None, None, "dp"),
            P(None, "dp"),
            P(None, "dp"),
            P("dp", None),
        ),
        out_specs=P("ctx", "dp"),
        check_vma=False,
    )
```

```python
import functools

import jax
import jax.numpy as jnp
from jax import lax
from jax.experimental import pallas as pl
from jax.experimental.pallas import tpu as pltpu
from jax.sharding import PartitionSpec as P

BLK = 64
F32, BF16 = jnp.float32, jnp.bfloat16
VMEM_LIMIT = 12 * 1024 * 1024


def from_behind(block, axis, distance):
    devices = range(lax.axis_size(axis))
    route = [(i - distance, i) for i in devices if i - distance in devices]
    return lax.ppermute(block, axis, route)


def prefix(value, axis, join, neutral):
    count, mine = (lax.axis_size(axis), lax.axis_index(axis))
    pieces = jax.tree.map(lambda part: lax.all_gather(part, axis), value)
    subtotal = jax.tree.map(
        lambda part, zero: jnp.full_like(part, 0) + jnp.asarray(zero, part.dtype), value, neutral
    )

    def lap(position, subtotal):
        longer = join(subtotal, jax.tree.map(lambda part: part[position], pieces))
        return jax.tree.map(lambda new, old: jnp.where(position < mine, new, old), longer, subtotal)

    return lax.fori_loop(0, count - 1, lap, subtotal)


def on_device_any(tokens, w_in, short_filter, mode_decay, residue, w_out):
    row_count = tokens.shape[0]
    chan_count = w_in.shape[2]
    short_count = short_filter.shape[0]
    mode_count = mode_decay.shape[0]
    earlier_rows = from_behind(tokens[row_count - (short_count - 1) :], "ctx", 1)
    source = jnp.concatenate([earlier_rows, tokens], 0)
    projected = jnp.einsum(
        "td,dgc->tgc",
        source,
        lax.all_gather(w_in, "ctx", axis=0, tiled=True),
        preferred_element_type=jnp.float32,
    )
    featured = jnp.zeros((row_count, 3, chan_count), jnp.float32)
    for j in range(short_count):
        featured = (
            featured
            + short_filter[j] * projected[short_count - 1 - j : short_count - 1 - j + row_count]
        )
    mixed = (featured[:, 1] * featured[:, 2]).astype(jnp.bfloat16)
    medium = mixed.astype(jnp.float32)
    highest = lax.Precision.HIGHEST
    mode_gain = residue * jnp.sqrt(1.0 - mode_decay * mode_decay)
    block_len = BLK
    block_times = jnp.arange(block_len).astype(jnp.float32)
    power_in = jnp.power(mode_decay[None], block_times[:, None, None])
    kernel_head = jnp.sum(mode_gain[None] * power_in, 1)
    lag_index = jnp.arange(block_len)[:, None] - jnp.arange(block_len)[None, :]
    toeplitz = jnp.where(
        (lag_index >= 0)[:, :, None], kernel_head[jnp.clip(lag_index, 0, block_len - 1)], 0.0
    )
    carry_weights = mode_gain[None] * power_in * mode_decay[None]
    state_weights = power_in[::-1]
    decay_block = jnp.power(mode_decay, float(block_len))
    blocks = medium.reshape(row_count // block_len, block_len, chan_count)

    def block_step(carried, block_rows):
        inner = jnp.einsum("tsc,sc->tc", toeplitz, block_rows, precision=highest)
        inner = inner + jnp.einsum("tnc,nc->tc", carry_weights, carried, precision=highest)
        carried = decay_block * carried + jnp.einsum(
            "snc,sc->nc", state_weights, block_rows, precision=highest
        )
        return (carried, inner)

    zero_state = jnp.zeros((mode_count, chan_count), jnp.float32)
    local_end, local_part = lax.scan(block_step, zero_state, blocks)
    local_part = local_part.reshape(row_count, chan_count)
    decay_device = jnp.power(mode_decay, float(row_count))

    def combine_states(earlier, later):
        return (earlier[0] * later[0], later[0] * earlier[1] + later[1])

    identity = (jnp.ones((mode_count, chan_count), jnp.float32), zero_state)
    scanned = prefix((decay_device, local_end), "ctx", combine_states, identity)
    entering = scanned[1]
    row_times = jnp.arange(1, row_count + 1).astype(jnp.float32)
    entry_weights = mode_gain[None] * jnp.power(mode_decay[None], row_times[:, None, None])
    long_part = local_part + jnp.einsum("tnc,nc->tc", entry_weights, entering, precision=highest)
    gated = (featured[:, 0] * long_part).astype(jnp.bfloat16)
    out_term = jnp.dot(gated, w_out, preferred_element_type=jnp.float32)
    return lax.psum_scatter(out_term.astype(jnp.bfloat16), "dp", scatter_dimension=1, tiled=True)


def local(kernel, name, shapes, scalars, arrays, scratch=()):
    whole = pl.BlockSpec(memory_space=pltpu.VMEM)
    out = [jax.ShapeDtypeStruct(*shape) for shape in shapes]
    return pl.pallas_call(
        kernel,
        out_shape=out if len(out) > 1 else out[0],
        in_specs=[pl.BlockSpec(memory_space=pltpu.SMEM)] + [whole] * len(arrays),
        out_specs=[whole] * len(out) if len(out) > 1 else whole,
        scratch_shapes=list(scratch),
        compiler_params=pltpu.CompilerParams(vmem_limit_bytes=VMEM_LIMIT),
        name=name,
    )(scalars, *arrays)


def columns(index, wide):
    return pl.ds(pl.multiple_of(index * wide, wide), wide)


def cut(order, tokens, pieces):
    high, wide = tokens.shape[0], tokens.shape[1] // pieces

    def kernel(order, tokens_ref, *out_refs):
        here = columns(order[2 * pieces + 2], high // 2)
        out_refs[pieces - 1][...] = tokens_ref[here, columns(order[pieces - 1], wide)]
        for s, out_ref in enumerate(out_refs[: pieces - 1]):
            out_ref[...] = tokens_ref[:, columns(order[s], wide)]

    shapes = [((high, wide), tokens.dtype)] * (pieces - 1) + [((high // 2, wide), tokens.dtype)]
    return local(kernel, "cut", shapes, order, [tokens])


def stage(array):
    def kernel(array_ref, out_ref, sem):
        copy = pltpu.make_async_copy(array_ref, out_ref, sem)
        copy.start()
        copy.wait()

    return pl.pallas_call(
        kernel,
        out_shape=jax.ShapeDtypeStruct(array.shape, array.dtype),
        in_specs=[pl.BlockSpec(memory_space=pl.ANY)],
        out_specs=pl.BlockSpec(memory_space=pltpu.VMEM),
        scratch_shapes=[pltpu.SemaphoreType.DMA],
        compiler_params=pltpu.CompilerParams(vmem_limit_bytes=VMEM_LIMIT),
        name="stage",
    )(array)


def gather_rows(core, x_refs, rows):
    high, depth = x_refs[0].shape[0], rows.shape[2]
    for i, x_ref in enumerate(x_refs):
        for h in range(2):
            rows[core ^ h, i * high : (i + 1) * high, :] = x_ref[:, h * depth : (h + 1) * depth]


def project_mix(order, xs, own, other, slots, kind, ends=0):
    chips = len(xs)
    streams, depth, chans = own.shape
    high = xs[0].shape[0]
    wide = chans // chips
    half = wide // 2

    def kernel(order, *refs):
        x_refs, (own_ref, other_ref, out_ref, *end_refs, rows) = refs[:chips], refs[chips:]
        core = order[2 * chips]
        gather_rows(core, x_refs, rows)
        for end_ref in end_refs:
            for s in range(chips):
                end_ref[s] = x_refs[s][high - ends :, :]
        for i, slot in enumerate(slots):
            at = columns(order[slot], wide)
            for g in range(1, streams):
                total = jnp.dot(rows[0], own_ref[g, :, at], preferred_element_type=F32)
                total += jnp.dot(rows[1], other_ref[g, :, at], preferred_element_type=F32)
                total = total.astype(kind)
                lanes = slice((g - 1) * half, g * half)
                for h in range(2):
                    out_ref[i, core ^ h, :, lanes] = total[:, h * half : (h + 1) * half]

    shape = (len(slots), 2, chips * high, (streams - 1) * half)
    scratch = [pltpu.VMEM((2, chips * high, depth), BF16)]
    shapes = [(shape, kind)] + ([((chips, ends, 2 * depth), BF16)] if ends else [])
    return local(kernel, "project_mix", shapes, order, [*xs, own, other], scratch)


def early_share(order, own_rows, mine, other_rows, own, other, slot, chips):
    half, wide_x = mine.shape
    high = 2 * half
    streams, depth, chans = own.shape
    wide = chans // chips
    lanes = wide // 2
    place = order.shape[0] - 1

    def kernel(order, own_rows_ref, mine_ref, there_ref, own_ref, other_ref, joined_ref, out_ref, rows):
        core = order[2 * chips]
        joined_ref[columns(order[place], half), :] = mine_ref[...]
        joined_ref[columns(1 - order[place], half), :] = there_ref[...]
        gather_rows(core, (own_rows_ref, joined_ref), rows)
        at = columns(order[slot], wide)
        for g in range(1, streams):
            total = jnp.dot(rows[0], own_ref[g, :, at], preferred_element_type=F32)
            total += jnp.dot(rows[1], other_ref[g, :, at], preferred_element_type=F32)
            for h in range(2):
                to = slice((g - 1) * lanes, g * lanes)
                out_ref[core ^ h, :, to] = total[:, h * lanes : (h + 1) * lanes].astype(BF16)

    shapes = [((high, wide_x), BF16), ((2, 2 * high, (streams - 1) * lanes), BF16)]
    scratch = [pltpu.VMEM((2, 2 * high, depth), BF16)]
    arrays = [own_rows, mine, other_rows, own, other]
    return local(kernel, "early_share", shapes, order, arrays, scratch)


def rest_share(order, xs, early, own, other, slot, chips):
    high = xs[0].shape[0]
    streams, depth, chans = own.shape
    wide = chans // chips
    lanes = wide // 2

    def kernel(order, first_ref, second_ref, early_ref, own_ref, other_ref, out_ref, rows):
        core = order[2 * chips]
        gather_rows(core, (first_ref, second_ref), rows)
        at = columns(order[slot], wide)
        for h in range(2):
            out_ref[0, h, :high, :] = early_ref[h, :high, :]
            out_ref[0, h, 3 * high :, :] = early_ref[h, high:, :]
        for g in range(1, streams):
            total = jnp.dot(rows[0], own_ref[g, :, at], preferred_element_type=F32)
            total += jnp.dot(rows[1], other_ref[g, :, at], preferred_element_type=F32)
            for h in range(2):
                to = slice((g - 1) * lanes, g * lanes)
                out_ref[0, core ^ h, high : 3 * high, to] = total[
                    :, h * lanes : (h + 1) * lanes
                ].astype(BF16)

    shapes = [((1, 2, chips * high, (streams - 1) * lanes), BF16)]
    scratch = [pltpu.VMEM((2, 2 * high, depth), BF16)]
    return local(kernel, "rest_share", shapes, order, [*xs, early, own, other], scratch)


def project_query(order, xs, before, own, other, short_filter):
    chips = len(xs)
    _, depth, chans = own.shape
    high = xs[0].shape[0]
    some = before.shape[1]
    step = some + high
    taps = short_filter.shape[0]
    tile = min(chans, 256)

    def kernel(order, *refs):
        x_refs = refs[:chips]
        before_ref, own_ref, other_ref, filt_ref, *out_refs, rows, ends, total = refs[chips:]
        core = order[2 * chips]
        ends[0] = jnp.zeros_like(ends[0])
        for s in range(chips):
            ends[order[chips + s] + 1] = before_ref[s]
        for i, x_ref in enumerate(x_refs):
            end = ends[order[i] + core]
            for h in range(2):
                lanes = slice(h * depth, (h + 1) * depth)
                rows[core ^ h, i * step : i * step + some, :] = end[:, lanes]
                rows[core ^ h, i * step + some : (i + 1) * step, :] = x_ref[:, lanes]
        for at in (slice(i, i + tile) for i in range(0, chans, tile)):
            total[...] = jnp.dot(
                rows[0], own_ref[0, :, at], preferred_element_type=F32
            ) + jnp.dot(rows[1], other_ref[0, :, at], preferred_element_type=F32)
            for i in range(chips):
                first = i * step + some
                value = filt_ref[0, 0:1, at] * total[first : first + high, :]
                for j in range(1, taps):
                    value = value + filt_ref[j, 0:1, at] * total[first - j : first - j + high, :]
                out_refs[i][:, at] = value.astype(out_refs[i].dtype)

    shapes = [((high, chans), F32 if i < 2 else BF16) for i in range(chips)]
    scratch = [
        pltpu.VMEM((2, chips * step, depth), BF16),
        pltpu.VMEM((chips + 1, some, 2 * depth), BF16),
        pltpu.VMEM((chips * step, tile), F32),
    ]
    arrays = [*xs, before, own, other, short_filter]
    return local(kernel, "project_query", shapes, order, arrays, scratch)


def second_share(order, rest, both_in, chips):
    _, _, rows, lanes = rest.shape
    high = rows // chips

    def kernel(order, rest_ref, both_ref, *out_refs):
        for h, out_ref in enumerate(out_refs):
            for s in range(chips):
                here, there = (slice(i * high, (i + 1) * high) for i in (s, s ^ 2))
                term = both_ref[0, h, there, :].astype(F32)
                out_ref[here, :] = (rest_ref[0, h, here, :] + term).astype(BF16)

    shapes = [((rows, lanes), BF16)] * 2
    return local(kernel, "second_share", shapes, order, [rest, both_in])


def first_share(order, rest, first_in, chips):
    _, _, rows, lanes = rest.shape
    high = rows // chips

    def kernel(order, rest_ref, first_ref, own_ref, other_ref):
        for h, out_ref in ((1, other_ref), (0, own_ref)):
            for s in range(chips):
                here, first = (slice(i * high, (i + 1) * high) for i in (s, s ^ 2))
                total = rest_ref[1, h, here, :] + first_ref[0, h, first, :].astype(F32)
                out_ref[here, :] = total.astype(out_ref.dtype)

    shapes = [((rows, lanes), F32), ((rows, lanes), BF16)]
    return local(kernel, "first_share", shapes, order, [rest, first_in])


def hyena_kernel(
    order, own_ref, swap_ref, second_ref, swap_second_ref, filt_ref, decay_ref, residue_ref,
    keep_ref, send_ref, rows, mixed_s, state, enter, edge, *, blocks,
):
    high = rows.shape[1] // blocks
    chans = rows.shape[2]
    modes = decay_ref.shape[0]
    taps = filt_ref.shape[0]
    chips = blocks // 2
    core = order[2 * chips]
    channels = columns(order[2 * chips + 1], chans)

    for s in range(chips):
        here, second = (slice(i * high, (i + 1) * high) for i in (s, s ^ 1))
        own_at = columns(2 * order[s] + core, high)
        swap_at = columns(2 * order[chips + s] + 1 - core, high)
        for g in range(2):
            lanes = slice(g * chans, (g + 1) * chans)
            rows[g, own_at, :] = own_ref[here, lanes] + second_ref[second, lanes].astype(F32)
            rows[g, swap_at, :] = swap_ref[here, lanes].astype(F32) + swap_second_ref[
                second, lanes
            ].astype(F32)

    for k in range(1, taps):
        for g in range(2):
            edge[k - 1, g, 0:1, :] = jnp.zeros((1, chans), F32)
            for b in range(1, blocks):
                edge[k - 1, g, b : b + 1, :] = rows[g, b * high - k : b * high - k + 1, :]

    rate = decay_ref[:, channels]
    taps_of = [filt_ref[j, :, channels] for j in range(taps)]
    decay = [jnp.broadcast_to(rate[n : n + 1, :], (blocks, chans)) for n in range(modes)]
    filt = [
        [jnp.broadcast_to(taps_of[j][g + 1 : g + 2, :], (blocks, chans)) for g in range(2)]
        for j in range(taps)
    ]

    def first_pass(t, carry):
        states, earlier = carry
        now = [rows[g, pl.ds(t, blocks, stride=high), :] for g in range(2)]
        featured = []
        for g in range(2):
            value = filt[0][g] * now[g]
            for k in range(1, taps):
                value = value + filt[k][g] * earlier[k - 1][g]
            featured.append(value)
        mixed = (featured[0] * featured[1]).astype(BF16).astype(F32)
        mixed_s[t] = mixed
        states = tuple(decay[n] * states[n] + mixed for n in range(modes))
        return states, (tuple(now),) + tuple(earlier[:-1])

    zeros = tuple(jnp.zeros((blocks, chans), F32) for _ in range(modes))
    before = tuple(tuple(edge[k, g] for g in range(2)) for k in range(taps - 1))
    states, _ = lax.fori_loop(0, high, first_pass, (zeros, before), unroll=16)
    for n in range(modes):
        state[n * blocks : (n + 1) * blocks, :] = states[n]

    across = jnp.ones_like(rate)
    power, left = rate, high
    while left:
        if left & 1:
            across = across * power
        left >>= 1
        if left:
            power = power * power
    entering = jnp.zeros((modes, chans), F32)
    for b in range(blocks):
        enter[pl.ds(b, modes, stride=blocks), :] = entering
        entering = across * entering + state[pl.ds(b, modes, stride=blocks), :]

    gain = residue_ref[:, channels] * jnp.sqrt(1.0 - rate * rate)
    gains = [jnp.broadcast_to(gain[n : n + 1, :], (blocks, chans)) for n in range(modes)]

    def second_pass(t, states):
        mixed = mixed_s[t]
        states = tuple(decay[n] * states[n] + mixed for n in range(modes))
        terms = [gains[n] * states[n] for n in range(modes)]
        while len(terms) > 1:
            terms = [sum(terms[i : i + 2][1:], terms[i]) for i in range(0, len(terms), 2)]
        rows[0, pl.ds(t, blocks, stride=high), :] = terms[0]
        return states

    begin = tuple(enter[n * blocks : (n + 1) * blocks, :] for n in range(modes))
    lax.fori_loop(0, high, second_pass, begin, unroll=16)
    for s in range(chips):
        keep_ref[s] = rows[0, columns(2 * order[s] + core, high), :].astype(BF16)
        send_ref[s] = rows[0, columns(2 * order[chips + s] + 1 - core, high), :].astype(BF16)


def hyena(order, parts, short_filter, mode_decay, residue, blocks):
    rows_count, lanes = parts[0].shape
    chans = lanes // 2
    total = 2 * rows_count
    high = total // blocks
    modes, taps = mode_decay.shape[0], short_filter.shape[0]
    scratch = [
        pltpu.VMEM((2, total, chans), F32),
        pltpu.VMEM((high, blocks, chans), F32),
        pltpu.VMEM((modes * blocks, chans), F32),
        pltpu.VMEM((modes * blocks, chans), F32),
        pltpu.VMEM((taps - 1, 2, blocks, chans), F32),
    ]
    arrays = [*parts, short_filter, mode_decay, residue]
    kernel = functools.partial(hyena_kernel, blocks=blocks)
    shapes = [((blocks // 2, high, chans), BF16)] * 2
    return local(kernel, "hyena", shapes, order, arrays, scratch)


def payloads(order, q_next, q_in, keep, other):
    chips, high, _ = keep.shape
    chans = q_next.shape[1]

    def kernel(order, next_ref, in_ref, keep_ref, other_ref, second_ref, *out_refs):
        second_ref[...] = (next_ref[...] + in_ref[:, :chans].astype(F32)).astype(BF16)
        for s, out_ref in enumerate(out_refs):
            out_ref[0] = keep_ref[s]
            out_ref[1] = other_ref[s]

    shapes = [(q_next.shape, BF16)] + [((2, high, keep.shape[2]), BF16)] * chips
    return local(kernel, "payloads", shapes, order, [q_next, q_in, keep, other])


def gate(scalars, queries, long_parts, w_out, groups):
    rows, chans = queries[0].shape
    chips = len(long_parts)
    part = long_parts[0].shape[2]
    wide = w_out.shape[1] // groups
    first_pick = 2 * chips + 3

    def kernel(scalars, *refs):
        query_refs, long_refs = refs[: len(queries)], refs[len(queries) : len(queries) + chips]
        w_ref, gated_ref, pair_ref, side_ref, query = refs[len(queries) + chips :]
        core = scalars[2 * chips]
        own_ref, second_ref, first_ref = query_refs
        query[...] = own_ref[...] + second_ref[...].astype(F32) + first_ref[...].astype(F32)
        for s, ref in enumerate(long_refs):
            for h in range(2):
                at = columns(2 * scalars[s] + (core ^ h), part)
                gated_ref[:, at] = (query[:, at] * ref[h].astype(F32)).astype(BF16)
        for pick, out_ref in enumerate((pair_ref, side_ref)):
            total = jnp.dot(
                gated_ref[...],
                w_ref[:, columns(scalars[first_pick + pick], wide)],
                preferred_element_type=F32,
            )
            out_ref[...] = total.astype(BF16)

    shapes = [((rows, chans), BF16), ((rows, wide), BF16), ((rows, wide), BF16)]
    arrays = [*queries, *long_parts, w_out]
    scratch = [pltpu.VMEM((rows, chans), F32)]
    return local(kernel, "gate", shapes, scalars, arrays, scratch)


def out_columns(picks, pick, x, w_out, groups, kind):
    wide = w_out.shape[1] // groups

    def kernel(picks, x_ref, w_ref, out_ref):
        total = jnp.dot(
            x_ref[...], w_ref[:, columns(picks[pick], wide)], preferred_element_type=F32
        )
        out_ref[...] = total.astype(kind)

    return local(kernel, "out_columns", [((x.shape[0], wide), kind)], picks, [x, w_out])


def line_picks():
    z = lax.axis_index("dp")
    table = [[3, 0, 3, 0], [1, 2, 1, 2], [2, 3, 0, 1], [0, 1, 2, 3], [0, 1, 1, 0]]
    return jnp.stack([sum(jnp.where(z == i, v, 0) for i, v in enumerate(row)) for row in table])


def output_over_line(picks, gated, pair, side, w_out, groups):
    pair_in = lax.ppermute(pair, "dp", [(0, 1), (1, 0), (2, 3), (3, 2)])
    far = out_columns(picks, 2, gated, w_out, groups, BF16)
    middle_in = lax.ppermute(side, "dp", [(1, 2), (2, 1)])
    side, far = lax.optimization_barrier((side, far))
    end_in = lax.ppermute(far, "dp", [(0, 2), (3, 1)])

    def add(picks, far_ref, pair_ref, side_ref, out_ref):
        value = far_ref[...].astype(F32) + pair_ref[...].astype(F32)
        out_ref[...] = jnp.where(picks[4] == 1, value.astype(BF16), side_ref[...])

    last = local(add, "last_step", [(far.shape, BF16)], picks, [far, pair_in, side])
    gated, last = lax.optimization_barrier((gated, last))
    last_in = lax.ppermute(last, "dp", [(0, 1), (1, 3), (2, 0), (3, 2)])
    own = out_columns(picks, 3, gated, w_out, groups, F32)

    def early(picks, own_ref, pair_ref, *refs):
        inner = picks[4] == 1
        value = own_ref[...] + jnp.where(inner, 0.0, pair_ref[...].astype(F32))
        for ref in refs[:-1]:
            value = value + ref[...].astype(F32)
        refs[-1][...] = value

    own = local(early, "early", [(own.shape, F32)], picks, [own, pair_in, middle_in, end_in])
    return (own + last_in.astype(F32)).astype(BF16)


def on_device_chips(tokens, w_in, short_filter, mode_decay, residue, w_out):
    count, groups = lax.axis_size("ctx"), lax.axis_size("dp")
    chips = count // 2
    me = lax.axis_index("ctx")
    core, chip = me % 2, me // 2

    def across(i, slot):
        high_bit, low_bit = slot >> 1, slot & 1
        step = (high_bit + 2 * low_bit) if i % 2 == 0 else (2 * high_bit + low_bit)
        return i ^ (2 * step)

    def route(slot):
        return [(i, across(i, slot)) for i in range(count)]

    def relative(slot, core):
        high_bit, low_bit = slot >> 1, slot & 1
        return jnp.where(core == 0, high_bit + 2 * low_bit, 2 * high_bit + low_bit)

    slot_chip = [chip ^ relative(s, core) for s in range(chips)]
    slot_other = [chip ^ relative(s, 1 - core) for s in range(chips)]
    order = jnp.stack(slot_chip + slot_other + [core, me, lax.axis_index("dp") % 2]).astype(jnp.int32)
    picks = line_picks().astype(jnp.int32)
    both_scalars = jnp.concatenate([order, picks])
    order, picks, both_scalars = lax.optimization_barrier((order, picks, both_scalars))

    own_w = jnp.transpose(w_in, (1, 0, 2))
    swap = [(i, i ^ 1) for i in range(count)]

    other_w = lax.ppermute(own_w, "ctx", swap)
    xs = cut(order, tokens, chips)
    own_w, xs = lax.optimization_barrier((own_w, xs))
    own_w = stage(own_w)
    half = lax.ppermute(xs[3], "ctx", route(3))
    other = lax.ppermute(half, "dp", [(i, i ^ 1) for i in range(groups)])
    xs = [xs[0]] + [lax.ppermute(xs[s], "ctx", route(s)) for s in (1, 2)]
    joined, early = early_share(order, xs[0], half, other, own_w, other_w, 3, chips)
    xs.append(joined)

    both = rest_share(order, xs[1:3], early, own_w, other_w, 3, chips)
    both_in = lax.ppermute(both, "ctx", route(2))
    xs, both = lax.optimization_barrier((xs, both))
    first = project_mix(order, xs, own_w, other_w, [2], BF16)
    first_in = lax.ppermute(first, "ctx", route(2))
    xs, first = lax.optimization_barrier((xs, first))
    rest, ends = project_mix(order, xs, own_w, other_w, [1, 0], F32, 16)
    second, swap_second = second_share(order, rest, both_in, chips)
    second_in = lax.ppermute(second, "ctx", route(1))
    swap_second = lax.ppermute(swap_second, "ctx", [(i, j ^ 1) for i, j in route(1)])

    xs, ends, second = lax.optimization_barrier((xs, ends, second))
    before = lax.ppermute(ends, "ctx", swap)
    q_own, q_next, q_first, q_both = project_query(order, xs, before, own_w, other_w, short_filter)
    q_own, w_out = lax.optimization_barrier((q_own, w_out))
    w_out = stage(w_out)
    q_own, w_out, rest = lax.optimization_barrier((q_own, w_out, rest))

    own, other_half = first_share(order, rest, first_in, chips)
    other_half = lax.ppermute(other_half, "ctx", swap)
    q_both, q_first, own = lax.optimization_barrier((q_both, q_first, own))
    q_both = lax.ppermute(q_both, "ctx", route(2))
    q_first = lax.ppermute(q_first, "ctx", route(2))
    parts = [own, other_half, second_in, swap_second]
    keep, send = hyena(order, parts, short_filter, mode_decay, residue, count)
    other_long = lax.ppermute(send, "ctx", swap)
    q_second, *long_parts = payloads(order, q_next, q_both, keep, other_long)
    q_second = lax.ppermute(q_second, "ctx", route(1))
    long_parts = [long_parts[0]] + [lax.ppermute(long_parts[s], "ctx", route(s)) for s in (1, 2, 3)]
    queries = [q_own, q_second, q_first]
    gated, pair, side = gate(both_scalars, queries, long_parts, w_out, groups)
    return output_over_line(picks, gated, pair, side, w_out, groups)


def solution(mesh):
    count, groups = mesh.shape["ctx"], mesh.shape["dp"]

    def on_device(tokens, w_in, *rest):
        lanes = w_in.shape[2] // count
        chips = count == 8 and groups == 4 and w_in.shape[2] % count == 0 and lanes % 128 == 0
        return (on_device_chips if chips else on_device_any)(tokens, w_in, *rest)

    return jax.shard_map(
        on_device,
        mesh=mesh,
        in_specs=(
            P("ctx", None),
            P("ctx", None, "dp"),
            P(None, None, "dp"),
            P(None, "dp"),
            P(None, "dp"),
            P("dp", None),
        ),
        out_specs=P("ctx", "dp"),
        check_vma=False,
    )
```

```python
import functools

import jax
import jax.numpy as jnp
from jax import lax
from jax.experimental import pallas as pl
from jax.experimental.pallas import tpu as pltpu
from jax.sharding import PartitionSpec as P

BLK = 64
F32, BF16 = jnp.float32, jnp.bfloat16
VMEM_LIMIT = 12 * 1024 * 1024


def from_behind(block, axis, distance):
    devices = range(lax.axis_size(axis))
    route = [(i - distance, i) for i in devices if i - distance in devices]
    return lax.ppermute(block, axis, route)


def prefix(value, axis, join, neutral):
    count, mine = (lax.axis_size(axis), lax.axis_index(axis))
    pieces = jax.tree.map(lambda part: lax.all_gather(part, axis), value)
    subtotal = jax.tree.map(
        lambda part, zero: jnp.full_like(part, 0) + jnp.asarray(zero, part.dtype), value, neutral
    )

    def lap(position, subtotal):
        longer = join(subtotal, jax.tree.map(lambda part: part[position], pieces))
        return jax.tree.map(lambda new, old: jnp.where(position < mine, new, old), longer, subtotal)

    return lax.fori_loop(0, count - 1, lap, subtotal)


def on_device_any(tokens, w_in, short_filter, mode_decay, residue, w_out):
    row_count = tokens.shape[0]
    chan_count = w_in.shape[2]
    short_count = short_filter.shape[0]
    mode_count = mode_decay.shape[0]
    earlier_rows = from_behind(tokens[row_count - (short_count - 1) :], "ctx", 1)
    source = jnp.concatenate([earlier_rows, tokens], 0)
    projected = jnp.einsum(
        "td,dgc->tgc",
        source,
        lax.all_gather(w_in, "ctx", axis=0, tiled=True),
        preferred_element_type=jnp.float32,
    )
    featured = jnp.zeros((row_count, 3, chan_count), jnp.float32)
    for j in range(short_count):
        featured = (
            featured
            + short_filter[j] * projected[short_count - 1 - j : short_count - 1 - j + row_count]
        )
    mixed = (featured[:, 1] * featured[:, 2]).astype(jnp.bfloat16)
    medium = mixed.astype(jnp.float32)
    highest = lax.Precision.HIGHEST
    mode_gain = residue * jnp.sqrt(1.0 - mode_decay * mode_decay)
    block_len = BLK
    block_times = jnp.arange(block_len).astype(jnp.float32)
    power_in = jnp.power(mode_decay[None], block_times[:, None, None])
    kernel_head = jnp.sum(mode_gain[None] * power_in, 1)
    lag_index = jnp.arange(block_len)[:, None] - jnp.arange(block_len)[None, :]
    toeplitz = jnp.where(
        (lag_index >= 0)[:, :, None], kernel_head[jnp.clip(lag_index, 0, block_len - 1)], 0.0
    )
    carry_weights = mode_gain[None] * power_in * mode_decay[None]
    state_weights = power_in[::-1]
    decay_block = jnp.power(mode_decay, float(block_len))
    blocks = medium.reshape(row_count // block_len, block_len, chan_count)

    def block_step(carried, block_rows):
        inner = jnp.einsum("tsc,sc->tc", toeplitz, block_rows, precision=highest)
        inner = inner + jnp.einsum("tnc,nc->tc", carry_weights, carried, precision=highest)
        carried = decay_block * carried + jnp.einsum(
            "snc,sc->nc", state_weights, block_rows, precision=highest
        )
        return (carried, inner)

    zero_state = jnp.zeros((mode_count, chan_count), jnp.float32)
    local_end, local_part = lax.scan(block_step, zero_state, blocks)
    local_part = local_part.reshape(row_count, chan_count)
    decay_device = jnp.power(mode_decay, float(row_count))

    def combine_states(earlier, later):
        return (earlier[0] * later[0], later[0] * earlier[1] + later[1])

    identity = (jnp.ones((mode_count, chan_count), jnp.float32), zero_state)
    scanned = prefix((decay_device, local_end), "ctx", combine_states, identity)
    entering = scanned[1]
    row_times = jnp.arange(1, row_count + 1).astype(jnp.float32)
    entry_weights = mode_gain[None] * jnp.power(mode_decay[None], row_times[:, None, None])
    long_part = local_part + jnp.einsum("tnc,nc->tc", entry_weights, entering, precision=highest)
    gated = (featured[:, 0] * long_part).astype(jnp.bfloat16)
    out_term = jnp.dot(gated, w_out, preferred_element_type=jnp.float32)
    return lax.psum_scatter(out_term.astype(jnp.bfloat16), "dp", scatter_dimension=1, tiled=True)


def local(kernel, name, shapes, scalars, arrays, scratch=()):
    whole = pl.BlockSpec(memory_space=pltpu.VMEM)
    out = [jax.ShapeDtypeStruct(*shape) for shape in shapes]

    def placed(*refs):
        kernel(scalars() if scalars else None, *refs)

    return pl.pallas_call(
        placed,
        out_shape=out if len(out) > 1 else out[0],
        in_specs=[whole] * len(arrays),
        out_specs=[whole] * len(out) if len(out) > 1 else whole,
        scratch_shapes=list(scratch),
        compiler_params=pltpu.CompilerParams(vmem_limit_bytes=VMEM_LIMIT),
        name=name,
    )(*arrays)


def slot_order(chips):
    me, line = lax.axis_index("ctx"), lax.axis_index("dp")
    core, chip = lax.rem(me, 2), lax.div(me, 2)

    def chip_of(slot, core):
        high_bit, low_bit = slot >> 1, slot & 1
        one, two = high_bit + 2 * low_bit, 2 * high_bit + low_bit
        return chip ^ (one + (two - one) * core)

    mine = [chip_of(s, core) for s in range(chips)]
    other = [chip_of(s, 1 - core) for s in range(chips)]
    return mine + other + [core, me, lax.rem(line, 2)]


def columns(index, wide):
    return pl.ds(pl.multiple_of(index * wide, wide), wide)


def cut(order, tokens, pieces):
    high, wide = tokens.shape[0], tokens.shape[1] // pieces

    def kernel(order, tokens_ref, *out_refs):
        here = columns(order[2 * pieces + 2], high // 2)
        out_refs[pieces - 1][...] = tokens_ref[here, columns(order[pieces - 1], wide)]
        for s, out_ref in enumerate(out_refs[: pieces - 1]):
            out_ref[...] = tokens_ref[:, columns(order[s], wide)]

    shapes = [((high, wide), tokens.dtype)] * (pieces - 1) + [((high // 2, wide), tokens.dtype)]
    return local(kernel, "cut", shapes, order, [tokens])


def stage(array):
    def kernel(array_ref, out_ref, sem):
        copy = pltpu.make_async_copy(array_ref, out_ref, sem)
        copy.start()
        copy.wait()

    return pl.pallas_call(
        kernel,
        out_shape=jax.ShapeDtypeStruct(array.shape, array.dtype),
        in_specs=[pl.BlockSpec(memory_space=pl.ANY)],
        out_specs=pl.BlockSpec(memory_space=pltpu.VMEM),
        scratch_shapes=[pltpu.SemaphoreType.DMA],
        compiler_params=pltpu.CompilerParams(vmem_limit_bytes=VMEM_LIMIT),
        name="stage",
    )(array)


def gather_rows(core, x_refs, rows):
    high, depth = x_refs[0].shape[0], rows.shape[2]
    for i, x_ref in enumerate(x_refs):
        for h in range(2):
            rows[core ^ h, i * high : (i + 1) * high, :] = x_ref[:, h * depth : (h + 1) * depth]


def project_mix(order, xs, own, other, slots, kind, ends=0):
    chips = len(xs)
    streams, depth, chans = own.shape
    high = xs[0].shape[0]
    wide = chans // chips
    half = wide // 2

    def kernel(order, *refs):
        x_refs, (own_ref, other_ref, out_ref, *end_refs, rows) = refs[:chips], refs[chips:]
        core = order[2 * chips]
        gather_rows(core, x_refs, rows)
        for end_ref in end_refs:
            for s in range(chips):
                end_ref[s] = x_refs[s][high - ends :, :]
        for i, slot in enumerate(slots):
            at = columns(order[slot], wide)
            for g in range(1, streams):
                total = jnp.dot(rows[0], own_ref[g, :, at], preferred_element_type=F32)
                total += jnp.dot(rows[1], other_ref[g, :, at], preferred_element_type=F32)
                total = total.astype(kind)
                lanes = slice((g - 1) * half, g * half)
                for h in range(2):
                    out_ref[i, core ^ h, :, lanes] = total[:, h * half : (h + 1) * half]

    shape = (len(slots), 2, chips * high, (streams - 1) * half)
    scratch = [pltpu.VMEM((2, chips * high, depth), BF16)]
    shapes = [(shape, kind)] + ([((chips, ends, 2 * depth), BF16)] if ends else [])
    return local(kernel, "project_mix", shapes, order, [*xs, own, other], scratch)


def early_share(order, own_rows, mine, other_rows, own, other, slot, chips):
    half, wide_x = mine.shape
    high = 2 * half
    streams, depth, chans = own.shape
    wide = chans // chips
    lanes = wide // 2
    place = 2 * chips + 2

    def kernel(order, own_rows_ref, mine_ref, there_ref, own_ref, other_ref, joined_ref, out_ref, rows):
        core = order[2 * chips]
        joined_ref[columns(order[place], half), :] = mine_ref[...]
        joined_ref[columns(1 - order[place], half), :] = there_ref[...]
        gather_rows(core, (own_rows_ref, joined_ref), rows)
        at = columns(order[slot], wide)
        for g in range(1, streams):
            total = jnp.dot(rows[0], own_ref[g, :, at], preferred_element_type=F32)
            total += jnp.dot(rows[1], other_ref[g, :, at], preferred_element_type=F32)
            for h in range(2):
                to = slice((g - 1) * lanes, g * lanes)
                out_ref[core ^ h, :, to] = total[:, h * lanes : (h + 1) * lanes].astype(BF16)

    shapes = [((high, wide_x), BF16), ((2, 2 * high, (streams - 1) * lanes), BF16)]
    scratch = [pltpu.VMEM((2, 2 * high, depth), BF16)]
    arrays = [own_rows, mine, other_rows, own, other]
    return local(kernel, "early_share", shapes, order, arrays, scratch)


def rest_share(order, xs, early, own, other, slot, chips):
    high = xs[0].shape[0]
    streams, depth, chans = own.shape
    wide = chans // chips
    lanes = wide // 2

    def kernel(order, first_ref, second_ref, early_ref, own_ref, other_ref, out_ref, rows):
        core = order[2 * chips]
        gather_rows(core, (first_ref, second_ref), rows)
        at = columns(order[slot], wide)
        for h in range(2):
            out_ref[0, h, :high, :] = early_ref[h, :high, :]
            out_ref[0, h, 3 * high :, :] = early_ref[h, high:, :]
        for g in range(1, streams):
            total = jnp.dot(rows[0], own_ref[g, :, at], preferred_element_type=F32)
            total += jnp.dot(rows[1], other_ref[g, :, at], preferred_element_type=F32)
            for h in range(2):
                to = slice((g - 1) * lanes, g * lanes)
                out_ref[0, core ^ h, high : 3 * high, to] = total[
                    :, h * lanes : (h + 1) * lanes
                ].astype(BF16)

    shapes = [((1, 2, chips * high, (streams - 1) * lanes), BF16)]
    scratch = [pltpu.VMEM((2, 2 * high, depth), BF16)]
    return local(kernel, "rest_share", shapes, order, [*xs, early, own, other], scratch)


def project_query(order, xs, before, own, other, short_filter):
    chips = len(xs)
    _, depth, chans = own.shape
    high = xs[0].shape[0]
    some = before.shape[1]
    step = some + high
    taps = short_filter.shape[0]
    tile = min(chans, 256)

    def kernel(order, *refs):
        x_refs = refs[:chips]
        before_ref, own_ref, other_ref, filt_ref, *out_refs, rows, ends, total = refs[chips:]
        core = order[2 * chips]
        ends[0] = jnp.zeros_like(ends[0])
        for s in range(chips):
            ends[order[chips + s] + 1] = before_ref[s]
        for i, x_ref in enumerate(x_refs):
            end = ends[order[i] + core]
            for h in range(2):
                lanes = slice(h * depth, (h + 1) * depth)
                rows[core ^ h, i * step : i * step + some, :] = end[:, lanes]
                rows[core ^ h, i * step + some : (i + 1) * step, :] = x_ref[:, lanes]
        for at in (slice(i, i + tile) for i in range(0, chans, tile)):
            total[...] = jnp.dot(
                rows[0], own_ref[0, :, at], preferred_element_type=F32
            ) + jnp.dot(rows[1], other_ref[0, :, at], preferred_element_type=F32)
            for i in range(chips):
                first = i * step + some
                value = filt_ref[0, 0:1, at] * total[first : first + high, :]
                for j in range(1, taps):
                    value = value + filt_ref[j, 0:1, at] * total[first - j : first - j + high, :]
                out_refs[i][:, at] = value.astype(out_refs[i].dtype)

    shapes = [((high, chans), F32 if i < 2 else BF16) for i in range(chips)]
    scratch = [
        pltpu.VMEM((2, chips * step, depth), BF16),
        pltpu.VMEM((chips + 1, some, 2 * depth), BF16),
        pltpu.VMEM((chips * step, tile), F32),
    ]
    arrays = [*xs, before, own, other, short_filter]
    return local(kernel, "project_query", shapes, order, arrays, scratch)


def second_share(order, rest, both_in, chips):
    _, _, rows, lanes = rest.shape
    high = rows // chips

    def kernel(order, rest_ref, both_ref, *out_refs):
        for h, out_ref in enumerate(out_refs):
            for s in range(chips):
                here, there = (slice(i * high, (i + 1) * high) for i in (s, s ^ 2))
                term = both_ref[0, h, there, :].astype(F32)
                out_ref[here, :] = (rest_ref[0, h, here, :] + term).astype(BF16)

    shapes = [((rows, lanes), BF16)] * 2
    return local(kernel, "second_share", shapes, None, [rest, both_in])


def first_share(order, rest, first_in, chips):
    _, _, rows, lanes = rest.shape
    high = rows // chips

    def kernel(order, rest_ref, first_ref, own_ref, other_ref):
        for h, out_ref in ((1, other_ref), (0, own_ref)):
            for s in range(chips):
                here, first = (slice(i * high, (i + 1) * high) for i in (s, s ^ 2))
                total = rest_ref[1, h, here, :] + first_ref[0, h, first, :].astype(F32)
                out_ref[here, :] = total.astype(out_ref.dtype)

    shapes = [((rows, lanes), F32), ((rows, lanes), BF16)]
    return local(kernel, "first_share", shapes, None, [rest, first_in])


def hyena_kernel(
    order, own_ref, swap_ref, second_ref, swap_second_ref, filt_ref, decay_ref, residue_ref,
    keep_ref, send_ref, rows, mixed_s, state, enter, edge, *, blocks,
):
    high = rows.shape[1] // blocks
    chans = rows.shape[2]
    modes = decay_ref.shape[0]
    taps = filt_ref.shape[0]
    chips = blocks // 2
    core = order[2 * chips]
    channels = columns(order[2 * chips + 1], chans)

    for s in range(chips):
        here, second = (slice(i * high, (i + 1) * high) for i in (s, s ^ 1))
        own_at = columns(2 * order[s] + core, high)
        swap_at = columns(2 * order[chips + s] + 1 - core, high)
        for g in range(2):
            lanes = slice(g * chans, (g + 1) * chans)
            rows[g, own_at, :] = own_ref[here, lanes] + second_ref[second, lanes].astype(F32)
            rows[g, swap_at, :] = swap_ref[here, lanes].astype(F32) + swap_second_ref[
                second, lanes
            ].astype(F32)

    for k in range(1, taps):
        for g in range(2):
            edge[k - 1, g, 0:1, :] = jnp.zeros((1, chans), F32)
            for b in range(1, blocks):
                edge[k - 1, g, b : b + 1, :] = rows[g, b * high - k : b * high - k + 1, :]

    rate = decay_ref[:, channels]
    taps_of = [filt_ref[j, :, channels] for j in range(taps)]
    decay = [jnp.broadcast_to(rate[n : n + 1, :], (blocks, chans)) for n in range(modes)]
    filt = [
        [jnp.broadcast_to(taps_of[j][g + 1 : g + 2, :], (blocks, chans)) for g in range(2)]
        for j in range(taps)
    ]

    def first_pass(t, carry):
        states, earlier = carry
        now = [rows[g, pl.ds(t, blocks, stride=high), :] for g in range(2)]
        featured = []
        for g in range(2):
            value = filt[0][g] * now[g]
            for k in range(1, taps):
                value = value + filt[k][g] * earlier[k - 1][g]
            featured.append(value)
        mixed = (featured[0] * featured[1]).astype(BF16).astype(F32)
        mixed_s[t] = mixed
        states = tuple(decay[n] * states[n] + mixed for n in range(modes))
        return states, (tuple(now),) + tuple(earlier[:-1])

    zeros = tuple(jnp.zeros((blocks, chans), F32) for _ in range(modes))
    before = tuple(tuple(edge[k, g] for g in range(2)) for k in range(taps - 1))
    states, _ = lax.fori_loop(0, high, first_pass, (zeros, before), unroll=16)
    for n in range(modes):
        state[n * blocks : (n + 1) * blocks, :] = states[n]

    across = jnp.ones_like(rate)
    power, left = rate, high
    while left:
        if left & 1:
            across = across * power
        left >>= 1
        if left:
            power = power * power
    entering = jnp.zeros((modes, chans), F32)
    for b in range(blocks):
        enter[pl.ds(b, modes, stride=blocks), :] = entering
        entering = across * entering + state[pl.ds(b, modes, stride=blocks), :]

    gain = residue_ref[:, channels] * jnp.sqrt(1.0 - rate * rate)
    gains = [jnp.broadcast_to(gain[n : n + 1, :], (blocks, chans)) for n in range(modes)]

    def second_pass(t, states):
        mixed = mixed_s[t]
        states = tuple(decay[n] * states[n] + mixed for n in range(modes))
        terms = [gains[n] * states[n] for n in range(modes)]
        while len(terms) > 1:
            terms = [sum(terms[i : i + 2][1:], terms[i]) for i in range(0, len(terms), 2)]
        rows[0, pl.ds(t, blocks, stride=high), :] = terms[0]
        return states

    begin = tuple(enter[n * blocks : (n + 1) * blocks, :] for n in range(modes))
    lax.fori_loop(0, high, second_pass, begin, unroll=16)
    for s in range(chips):
        keep_ref[s] = rows[0, columns(2 * order[s] + core, high), :].astype(BF16)
        send_ref[s] = rows[0, columns(2 * order[chips + s] + 1 - core, high), :].astype(BF16)


def hyena(order, parts, short_filter, mode_decay, residue, blocks):
    rows_count, lanes = parts[0].shape
    chans = lanes // 2
    total = 2 * rows_count
    high = total // blocks
    modes, taps = mode_decay.shape[0], short_filter.shape[0]
    scratch = [
        pltpu.VMEM((2, total, chans), F32),
        pltpu.VMEM((high, blocks, chans), F32),
        pltpu.VMEM((modes * blocks, chans), F32),
        pltpu.VMEM((modes * blocks, chans), F32),
        pltpu.VMEM((taps - 1, 2, blocks, chans), F32),
    ]
    arrays = [*parts, short_filter, mode_decay, residue]
    kernel = functools.partial(hyena_kernel, blocks=blocks)
    shapes = [((blocks // 2, high, chans), BF16)] * 2
    return local(kernel, "hyena", shapes, order, arrays, scratch)


def payloads(order, q_next, q_in, keep, other):
    chips, high, _ = keep.shape
    chans = q_next.shape[1]

    def kernel(order, next_ref, in_ref, keep_ref, other_ref, second_ref, *out_refs):
        second_ref[...] = (next_ref[...] + in_ref[:, :chans].astype(F32)).astype(BF16)
        for s, out_ref in enumerate(out_refs):
            out_ref[0] = keep_ref[s]
            out_ref[1] = other_ref[s]

    shapes = [(q_next.shape, BF16)] + [((2, high, keep.shape[2]), BF16)] * chips
    return local(kernel, "payloads", shapes, None, [q_next, q_in, keep, other])


def gate(scalars, queries, long_parts, w_out, groups):
    rows, chans = queries[0].shape
    chips = len(long_parts)
    part = long_parts[0].shape[2]
    wide = w_out.shape[1] // groups
    first_pick = 2 * chips + 3

    def kernel(scalars, *refs):
        query_refs, long_refs = refs[: len(queries)], refs[len(queries) : len(queries) + chips]
        w_ref, gated_ref, pair_ref, side_ref, query = refs[len(queries) + chips :]
        core = scalars[2 * chips]
        own_ref, second_ref, first_ref = query_refs
        query[...] = own_ref[...] + second_ref[...].astype(F32) + first_ref[...].astype(F32)
        for s, ref in enumerate(long_refs):
            for h in range(2):
                at = columns(2 * scalars[s] + (core ^ h), part)
                gated_ref[:, at] = (query[:, at] * ref[h].astype(F32)).astype(BF16)
        for pick, out_ref in enumerate((pair_ref, side_ref)):
            total = jnp.dot(
                gated_ref[...],
                w_ref[:, columns(scalars[first_pick + pick], wide)],
                preferred_element_type=F32,
            )
            out_ref[...] = total.astype(BF16)

    shapes = [((rows, chans), BF16), ((rows, wide), BF16), ((rows, wide), BF16)]
    arrays = [*queries, *long_parts, w_out]
    scratch = [pltpu.VMEM((rows, chans), F32)]
    return local(kernel, "gate", shapes, scalars, arrays, scratch)


def out_columns(picks, pick, x, w_out, groups, kind):
    wide = w_out.shape[1] // groups

    def kernel(picks, x_ref, w_ref, out_ref):
        total = jnp.dot(
            x_ref[...], w_ref[:, columns(picks[pick], wide)], preferred_element_type=F32
        )
        out_ref[...] = total.astype(kind)

    return local(kernel, "out_columns", [((x.shape[0], wide), kind)], picks, [x, w_out])


def line_picks():
    z = lax.axis_index("dp")
    table = [[3, 0, 3, 0], [1, 2, 1, 2], [2, 3, 0, 1], [0, 1, 2, 3], [0, 1, 1, 0]]
    return [sum(jnp.where(z == i, v, 0) for i, v in enumerate(row)) for row in table]


def output_over_line(picks, gated, pair, side, w_out, groups):
    pair_in = lax.ppermute(pair, "dp", [(0, 1), (1, 0), (2, 3), (3, 2)])
    far = out_columns(picks, 2, gated, w_out, groups, BF16)
    middle_in = lax.ppermute(side, "dp", [(1, 2), (2, 1)])
    side, far = lax.optimization_barrier((side, far))
    end_in = lax.ppermute(far, "dp", [(0, 2), (3, 1)])

    def add(picks, far_ref, pair_ref, side_ref, out_ref):
        value = far_ref[...].astype(F32) + pair_ref[...].astype(F32)
        out_ref[...] = jnp.where(picks[4] == 1, value.astype(BF16), side_ref[...])

    last = local(add, "last_step", [(far.shape, BF16)], picks, [far, pair_in, side])
    gated, last = lax.optimization_barrier((gated, last))
    last_in = lax.ppermute(last, "dp", [(0, 1), (1, 3), (2, 0), (3, 2)])
    own = out_columns(picks, 3, gated, w_out, groups, F32)

    def early(picks, own_ref, pair_ref, *refs):
        inner = picks[4] == 1
        value = own_ref[...] + jnp.where(inner, 0.0, pair_ref[...].astype(F32))
        for ref in refs[:-1]:
            value = value + ref[...].astype(F32)
        refs[-1][...] = value

    own = local(early, "early", [(own.shape, F32)], picks, [own, pair_in, middle_in, end_in])
    return (own + last_in.astype(F32)).astype(BF16)


def on_device_chips(tokens, w_in, short_filter, mode_decay, residue, w_out):
    count, groups = lax.axis_size("ctx"), lax.axis_size("dp")
    chips = count // 2

    def across(i, slot):
        high_bit, low_bit = slot >> 1, slot & 1
        step = (high_bit + 2 * low_bit) if i % 2 == 0 else (2 * high_bit + low_bit)
        return i ^ (2 * step)

    def route(slot):
        return [(i, across(i, slot)) for i in range(count)]

    order, picks = functools.partial(slot_order, chips), line_picks

    def both_scalars():
        return order() + picks()

    own_w = jnp.transpose(w_in, (1, 0, 2))
    swap = [(i, i ^ 1) for i in range(count)]

    other_w = lax.ppermute(own_w, "ctx", swap)
    xs = cut(order, tokens, chips)
    own_w, xs = lax.optimization_barrier((own_w, xs))
    own_w = stage(own_w)
    half = lax.ppermute(xs[3], "ctx", route(3))
    other = lax.ppermute(half, "dp", [(i, i ^ 1) for i in range(groups)])
    xs = [xs[0]] + [lax.ppermute(xs[s], "ctx", route(s)) for s in (1, 2)]
    joined, early = early_share(order, xs[0], half, other, own_w, other_w, 3, chips)
    xs.append(joined)

    both = rest_share(order, xs[1:3], early, own_w, other_w, 3, chips)
    both_in = lax.ppermute(both, "ctx", route(2))
    xs, both = lax.optimization_barrier((xs, both))
    first = project_mix(order, xs, own_w, other_w, [2], BF16)
    first_in = lax.ppermute(first, "ctx", route(2))
    xs, first = lax.optimization_barrier((xs, first))
    rest, ends = project_mix(order, xs, own_w, other_w, [1, 0], F32, 16)
    second, swap_second = second_share(order, rest, both_in, chips)
    second_in = lax.ppermute(second, "ctx", route(1))
    swap_second = lax.ppermute(swap_second, "ctx", [(i, j ^ 1) for i, j in route(1)])

    xs, ends, second = lax.optimization_barrier((xs, ends, second))
    before = lax.ppermute(ends, "ctx", swap)
    q_own, q_next, q_first, q_both = project_query(order, xs, before, own_w, other_w, short_filter)
    q_own, w_out = lax.optimization_barrier((q_own, w_out))
    w_out = stage(w_out)
    q_own, w_out, rest = lax.optimization_barrier((q_own, w_out, rest))

    own, other_half = first_share(order, rest, first_in, chips)
    other_half = lax.ppermute(other_half, "ctx", swap)
    q_both, q_first, own = lax.optimization_barrier((q_both, q_first, own))
    q_both = lax.ppermute(q_both, "ctx", route(2))
    q_first = lax.ppermute(q_first, "ctx", route(2))
    parts = [own, other_half, second_in, swap_second]
    keep, send = hyena(order, parts, short_filter, mode_decay, residue, count)
    other_long = lax.ppermute(send, "ctx", swap)
    q_second, *long_parts = payloads(order, q_next, q_both, keep, other_long)
    q_second = lax.ppermute(q_second, "ctx", route(1))
    long_parts = [long_parts[0]] + [lax.ppermute(long_parts[s], "ctx", route(s)) for s in (1, 2, 3)]
    queries = [q_own, q_second, q_first]
    gated, pair, side = gate(both_scalars, queries, long_parts, w_out, groups)
    return output_over_line(picks, gated, pair, side, w_out, groups)


def solution(mesh):
    count, groups = mesh.shape["ctx"], mesh.shape["dp"]

    def on_device(tokens, w_in, *rest):
        lanes = w_in.shape[2] // count
        chips = count == 8 and groups == 4 and w_in.shape[2] % count == 0 and lanes % 128 == 0
        return (on_device_chips if chips else on_device_any)(tokens, w_in, *rest)

    return jax.shard_map(
        on_device,
        mesh=mesh,
        in_specs=(
            P("ctx", None),
            P("ctx", None, "dp"),
            P(None, None, "dp"),
            P(None, "dp"),
            P(None, "dp"),
            P("dp", None),
        ),
        out_specs=P("ctx", "dp"),
        check_vma=False,
    )
```

```python
import functools

import jax
import jax.numpy as jnp
from jax import lax
from jax.experimental import pallas as pl
from jax.experimental.pallas import tpu as pltpu
from jax.sharding import PartitionSpec as P

BLK = 64
F32, BF16 = jnp.float32, jnp.bfloat16
VMEM_LIMIT = 12 * 1024 * 1024


def from_behind(block, axis, distance):
    devices = range(lax.axis_size(axis))
    route = [(i - distance, i) for i in devices if i - distance in devices]
    return lax.ppermute(block, axis, route)


def prefix(value, axis, join, neutral):
    count, mine = (lax.axis_size(axis), lax.axis_index(axis))
    pieces = jax.tree.map(lambda part: lax.all_gather(part, axis), value)
    subtotal = jax.tree.map(
        lambda part, zero: jnp.full_like(part, 0) + jnp.asarray(zero, part.dtype), value, neutral
    )

    def lap(position, subtotal):
        longer = join(subtotal, jax.tree.map(lambda part: part[position], pieces))
        return jax.tree.map(lambda new, old: jnp.where(position < mine, new, old), longer, subtotal)

    return lax.fori_loop(0, count - 1, lap, subtotal)


def on_device_any(tokens, w_in, short_filter, mode_decay, residue, w_out):
    row_count = tokens.shape[0]
    chan_count = w_in.shape[2]
    short_count = short_filter.shape[0]
    mode_count = mode_decay.shape[0]
    earlier_rows = from_behind(tokens[row_count - (short_count - 1) :], "ctx", 1)
    source = jnp.concatenate([earlier_rows, tokens], 0)
    projected = jnp.einsum(
        "td,dgc->tgc",
        source,
        lax.all_gather(w_in, "ctx", axis=0, tiled=True),
        preferred_element_type=jnp.float32,
    )
    featured = jnp.zeros((row_count, 3, chan_count), jnp.float32)
    for j in range(short_count):
        featured = (
            featured
            + short_filter[j] * projected[short_count - 1 - j : short_count - 1 - j + row_count]
        )
    mixed = (featured[:, 1] * featured[:, 2]).astype(jnp.bfloat16)
    medium = mixed.astype(jnp.float32)
    highest = lax.Precision.HIGHEST
    mode_gain = residue * jnp.sqrt(1.0 - mode_decay * mode_decay)
    block_len = BLK
    block_times = jnp.arange(block_len).astype(jnp.float32)
    power_in = jnp.power(mode_decay[None], block_times[:, None, None])
    kernel_head = jnp.sum(mode_gain[None] * power_in, 1)
    lag_index = jnp.arange(block_len)[:, None] - jnp.arange(block_len)[None, :]
    toeplitz = jnp.where(
        (lag_index >= 0)[:, :, None], kernel_head[jnp.clip(lag_index, 0, block_len - 1)], 0.0
    )
    carry_weights = mode_gain[None] * power_in * mode_decay[None]
    state_weights = power_in[::-1]
    decay_block = jnp.power(mode_decay, float(block_len))
    blocks = medium.reshape(row_count // block_len, block_len, chan_count)

    def block_step(carried, block_rows):
        inner = jnp.einsum("tsc,sc->tc", toeplitz, block_rows, precision=highest)
        inner = inner + jnp.einsum("tnc,nc->tc", carry_weights, carried, precision=highest)
        carried = decay_block * carried + jnp.einsum(
            "snc,sc->nc", state_weights, block_rows, precision=highest
        )
        return (carried, inner)

    zero_state = jnp.zeros((mode_count, chan_count), jnp.float32)
    local_end, local_part = lax.scan(block_step, zero_state, blocks)
    local_part = local_part.reshape(row_count, chan_count)
    decay_device = jnp.power(mode_decay, float(row_count))

    def combine_states(earlier, later):
        return (earlier[0] * later[0], later[0] * earlier[1] + later[1])

    identity = (jnp.ones((mode_count, chan_count), jnp.float32), zero_state)
    scanned = prefix((decay_device, local_end), "ctx", combine_states, identity)
    entering = scanned[1]
    row_times = jnp.arange(1, row_count + 1).astype(jnp.float32)
    entry_weights = mode_gain[None] * jnp.power(mode_decay[None], row_times[:, None, None])
    long_part = local_part + jnp.einsum("tnc,nc->tc", entry_weights, entering, precision=highest)
    gated = (featured[:, 0] * long_part).astype(jnp.bfloat16)
    out_term = jnp.dot(gated, w_out, preferred_element_type=jnp.float32)
    return lax.psum_scatter(out_term.astype(jnp.bfloat16), "dp", scatter_dimension=1, tiled=True)


def local(kernel, name, shapes, scalars, arrays, scratch=()):
    whole = pl.BlockSpec(memory_space=pltpu.VMEM)
    out = [jax.ShapeDtypeStruct(*shape) for shape in shapes]

    def placed(*refs):
        kernel(scalars() if scalars else None, *refs)

    return pl.pallas_call(
        placed,
        out_shape=out if len(out) > 1 else out[0],
        in_specs=[whole] * len(arrays),
        out_specs=[whole] * len(out) if len(out) > 1 else whole,
        scratch_shapes=list(scratch),
        compiler_params=pltpu.CompilerParams(vmem_limit_bytes=VMEM_LIMIT),
        name=name,
    )(*arrays)


def slot_order(chips):
    me, line = lax.axis_index("ctx"), lax.axis_index("dp")
    core, chip = lax.rem(me, 2), lax.div(me, 2)

    def chip_of(slot, core):
        high_bit, low_bit = slot >> 1, slot & 1
        one, two = high_bit + 2 * low_bit, 2 * high_bit + low_bit
        return chip ^ (one + (two - one) * core)

    mine = [chip_of(s, core) for s in range(chips)]
    other = [chip_of(s, 1 - core) for s in range(chips)]
    return mine + other + [core, me, lax.rem(line, 2)]


def columns(index, wide):
    return pl.ds(pl.multiple_of(index * wide, wide), wide)


def cut(order, tokens, pieces):
    high, wide = tokens.shape[0], tokens.shape[1] // pieces

    def kernel(order, tokens_ref, *out_refs):
        here = columns(order[2 * pieces + 2], high // 2)
        out_refs[pieces - 1][...] = tokens_ref[here, columns(order[pieces - 1], wide)]
        for s, out_ref in enumerate(out_refs[: pieces - 1]):
            out_ref[...] = tokens_ref[:, columns(order[s], wide)]

    shapes = [((high, wide), tokens.dtype)] * (pieces - 1) + [((high // 2, wide), tokens.dtype)]
    return local(kernel, "cut", shapes, order, [tokens])


def stage(array):
    def kernel(array_ref, out_ref, sem):
        copy = pltpu.make_async_copy(array_ref, out_ref, sem)
        copy.start()
        copy.wait()

    return pl.pallas_call(
        kernel,
        out_shape=jax.ShapeDtypeStruct(array.shape, array.dtype),
        in_specs=[pl.BlockSpec(memory_space=pl.ANY)],
        out_specs=pl.BlockSpec(memory_space=pltpu.VMEM),
        scratch_shapes=[pltpu.SemaphoreType.DMA],
        compiler_params=pltpu.CompilerParams(vmem_limit_bytes=VMEM_LIMIT),
        name="stage",
    )(array)


def gather_rows(core, x_refs, rows):
    high, depth = x_refs[0].shape[0], rows.shape[2]
    for i, x_ref in enumerate(x_refs):
        for h in range(2):
            rows[core ^ h, i * high : (i + 1) * high, :] = x_ref[:, h * depth : (h + 1) * depth]


def project_mix(order, xs, own, other, slots, kind, ends=0):
    chips = len(xs)
    streams, depth, chans = own.shape
    high = xs[0].shape[0]
    wide = chans // chips
    half = wide // 2

    def kernel(order, *refs):
        x_refs, (own_ref, other_ref, out_ref, *end_refs, rows) = refs[:chips], refs[chips:]
        core = order[2 * chips]
        gather_rows(core, x_refs, rows)
        for end_ref in end_refs:
            for s in range(chips):
                end_ref[s] = x_refs[s][high - ends :, :]
        for i, slot in enumerate(slots):
            at = columns(order[slot], wide)
            for g in range(1, streams):
                total = jnp.dot(rows[0], own_ref[g, :, at], preferred_element_type=F32)
                total += jnp.dot(rows[1], other_ref[g, :, at], preferred_element_type=F32)
                total = total.astype(kind)
                lanes = slice((g - 1) * half, g * half)
                for h in range(2):
                    out_ref[i, core ^ h, :, lanes] = total[:, h * half : (h + 1) * half]

    shape = (len(slots), 2, chips * high, (streams - 1) * half)
    scratch = [pltpu.VMEM((2, chips * high, depth), BF16)]
    shapes = [(shape, kind)] + ([((chips, ends, 2 * depth), BF16)] if ends else [])
    return local(kernel, "project_mix", shapes, order, [*xs, own, other], scratch)


def early_share(order, own_rows, mine, other_rows, own, other, slot, chips):
    half, wide_x = mine.shape
    high = 2 * half
    streams, depth, chans = own.shape
    wide = chans // chips
    lanes = wide // 2
    place = 2 * chips + 2

    def kernel(order, own_rows_ref, mine_ref, there_ref, own_ref, other_ref, joined_ref, out_ref, rows):
        core = order[2 * chips]
        joined_ref[columns(order[place], half), :] = mine_ref[...]
        joined_ref[columns(1 - order[place], half), :] = there_ref[...]
        gather_rows(core, (own_rows_ref, joined_ref), rows)
        at = columns(order[slot], wide)
        for g in range(1, streams):
            total = jnp.dot(rows[0], own_ref[g, :, at], preferred_element_type=F32)
            total += jnp.dot(rows[1], other_ref[g, :, at], preferred_element_type=F32)
            for h in range(2):
                to = slice((g - 1) * lanes, g * lanes)
                out_ref[core ^ h, :, to] = total[:, h * lanes : (h + 1) * lanes].astype(BF16)

    shapes = [((high, wide_x), BF16), ((2, 2 * high, (streams - 1) * lanes), BF16)]
    scratch = [pltpu.VMEM((2, 2 * high, depth), BF16)]
    arrays = [own_rows, mine, other_rows, own, other]
    return local(kernel, "early_share", shapes, order, arrays, scratch)


def rest_share(order, xs, early, own, other, slot, chips):
    high = xs[0].shape[0]
    streams, depth, chans = own.shape
    wide = chans // chips
    lanes = wide // 2

    def kernel(order, first_ref, second_ref, early_ref, own_ref, other_ref, out_ref, rows):
        core = order[2 * chips]
        gather_rows(core, (first_ref, second_ref), rows)
        at = columns(order[slot], wide)
        for h in range(2):
            out_ref[0, h, :high, :] = early_ref[h, :high, :]
            out_ref[0, h, 3 * high :, :] = early_ref[h, high:, :]
        for g in range(1, streams):
            total = jnp.dot(rows[0], own_ref[g, :, at], preferred_element_type=F32)
            total += jnp.dot(rows[1], other_ref[g, :, at], preferred_element_type=F32)
            for h in range(2):
                to = slice((g - 1) * lanes, g * lanes)
                out_ref[0, core ^ h, high : 3 * high, to] = total[
                    :, h * lanes : (h + 1) * lanes
                ].astype(BF16)

    shapes = [((1, 2, chips * high, (streams - 1) * lanes), BF16)]
    scratch = [pltpu.VMEM((2, 2 * high, depth), BF16)]
    return local(kernel, "rest_share", shapes, order, [*xs, early, own, other], scratch)


def project_query(order, xs, before, own, other, short_filter):
    chips = len(xs)
    _, depth, chans = own.shape
    high = xs[0].shape[0]
    some = before.shape[1]
    step = some + high
    taps = short_filter.shape[0]
    tile = min(chans, 256)

    def kernel(order, *refs):
        x_refs = refs[:chips]
        before_ref, own_ref, other_ref, filt_ref, *out_refs, rows, ends, total = refs[chips:]
        core = order[2 * chips]
        ends[0] = jnp.zeros_like(ends[0])
        for s in range(chips):
            ends[order[chips + s] + 1] = before_ref[s]
        for i, x_ref in enumerate(x_refs):
            end = ends[order[i] + core]
            for h in range(2):
                lanes = slice(h * depth, (h + 1) * depth)
                rows[core ^ h, i * step : i * step + some, :] = end[:, lanes]
                rows[core ^ h, i * step + some : (i + 1) * step, :] = x_ref[:, lanes]
        for at in (slice(i, i + tile) for i in range(0, chans, tile)):
            total[...] = jnp.dot(
                rows[0], own_ref[0, :, at], preferred_element_type=F32
            ) + jnp.dot(rows[1], other_ref[0, :, at], preferred_element_type=F32)
            for i in range(chips):
                first = i * step + some
                value = filt_ref[0, 0:1, at] * total[first : first + high, :]
                for j in range(1, taps):
                    value = value + filt_ref[j, 0:1, at] * total[first - j : first - j + high, :]
                out_refs[i][:, at] = value.astype(out_refs[i].dtype)

    shapes = [((high, chans), F32 if i < 2 else BF16) for i in range(chips)]
    scratch = [
        pltpu.VMEM((2, chips * step, depth), BF16),
        pltpu.VMEM((chips + 1, some, 2 * depth), BF16),
        pltpu.VMEM((chips * step, tile), F32),
    ]
    arrays = [*xs, before, own, other, short_filter]
    return local(kernel, "project_query", shapes, order, arrays, scratch)


def second_share(order, rest, both_in, chips):
    _, _, rows, lanes = rest.shape
    high = rows // chips

    def kernel(order, rest_ref, both_ref, *out_refs):
        for h, out_ref in enumerate(out_refs):
            for s in range(chips):
                here, there = (slice(i * high, (i + 1) * high) for i in (s, s ^ 2))
                term = both_ref[0, h, there, :].astype(F32)
                out_ref[here, :] = (rest_ref[0, h, here, :] + term).astype(BF16)

    shapes = [((rows, lanes), BF16)] * 2
    return local(kernel, "second_share", shapes, None, [rest, both_in])


def first_share(order, rest, first_in, chips):
    _, _, rows, lanes = rest.shape
    high = rows // chips

    def kernel(order, rest_ref, first_ref, own_ref, other_ref):
        for h, out_ref in ((1, other_ref), (0, own_ref)):
            for s in range(chips):
                here, first = (slice(i * high, (i + 1) * high) for i in (s, s ^ 2))
                total = rest_ref[1, h, here, :] + first_ref[0, h, first, :].astype(F32)
                out_ref[here, :] = total.astype(out_ref.dtype)

    shapes = [((rows, lanes), F32), ((rows, lanes), BF16)]
    return local(kernel, "first_share", shapes, None, [rest, first_in])


def hyena_kernel(
    order, own_ref, swap_ref, second_ref, swap_second_ref, filt_ref, decay_ref, residue_ref,
    keep_ref, send_ref, rows, mixed_s, state, enter, edge, *, blocks,
):
    high = rows.shape[1] // blocks
    chans = rows.shape[2]
    modes = decay_ref.shape[0]
    taps = filt_ref.shape[0]
    chips = blocks // 2
    core = order[2 * chips]
    channels = columns(order[2 * chips + 1], chans)

    for s in range(chips):
        here, second = (slice(i * high, (i + 1) * high) for i in (s, s ^ 1))
        own_at = columns(2 * order[s] + core, high)
        swap_at = columns(2 * order[chips + s] + 1 - core, high)
        for g in range(2):
            lanes = slice(g * chans, (g + 1) * chans)
            rows[g, own_at, :] = own_ref[here, lanes] + second_ref[second, lanes].astype(F32)
            rows[g, swap_at, :] = swap_ref[here, lanes].astype(F32) + swap_second_ref[
                second, lanes
            ].astype(F32)

    for k in range(1, taps):
        for g in range(2):
            edge[k - 1, g, 0:1, :] = jnp.zeros((1, chans), F32)
            for b in range(1, blocks):
                edge[k - 1, g, b : b + 1, :] = rows[g, b * high - k : b * high - k + 1, :]

    rate = decay_ref[:, channels]
    taps_of = [filt_ref[j, :, channels] for j in range(taps)]
    decay = [jnp.broadcast_to(rate[n : n + 1, :], (blocks, chans)) for n in range(modes)]
    filt = [
        [jnp.broadcast_to(taps_of[j][g + 1 : g + 2, :], (blocks, chans)) for g in range(2)]
        for j in range(taps)
    ]

    def first_pass(t, carry):
        states, earlier = carry
        now = [rows[g, pl.ds(t, blocks, stride=high), :] for g in range(2)]
        featured = []
        for g in range(2):
            value = filt[0][g] * now[g]
            for k in range(1, taps):
                value = value + filt[k][g] * earlier[k - 1][g]
            featured.append(value)
        mixed = (featured[0] * featured[1]).astype(BF16).astype(F32)
        mixed_s[t] = mixed
        states = tuple(decay[n] * states[n] + mixed for n in range(modes))
        return states, (tuple(now),) + tuple(earlier[:-1])

    zeros = tuple(jnp.zeros((blocks, chans), F32) for _ in range(modes))
    before = tuple(tuple(edge[k, g] for g in range(2)) for k in range(taps - 1))
    states, _ = lax.fori_loop(0, high, first_pass, (zeros, before), unroll=16)
    for n in range(modes):
        state[n * blocks : (n + 1) * blocks, :] = states[n]

    across = jnp.ones_like(rate)
    power, left = rate, high
    while left:
        if left & 1:
            across = across * power
        left >>= 1
        if left:
            power = power * power
    entering = jnp.zeros((modes, chans), F32)
    for b in range(blocks):
        enter[pl.ds(b, modes, stride=blocks), :] = entering
        entering = across * entering + state[pl.ds(b, modes, stride=blocks), :]

    gain = residue_ref[:, channels] * jnp.sqrt(1.0 - rate * rate)
    gains = [jnp.broadcast_to(gain[n : n + 1, :], (blocks, chans)) for n in range(modes)]

    def second_pass(t, states):
        mixed = mixed_s[t]
        states = tuple(decay[n] * states[n] + mixed for n in range(modes))
        terms = [gains[n] * states[n] for n in range(modes)]
        while len(terms) > 1:
            terms = [sum(terms[i : i + 2][1:], terms[i]) for i in range(0, len(terms), 2)]
        rows[0, pl.ds(t, blocks, stride=high), :] = terms[0]
        return states

    begin = tuple(enter[n * blocks : (n + 1) * blocks, :] for n in range(modes))
    lax.fori_loop(0, high, second_pass, begin, unroll=16)
    for s in range(chips):
        keep_ref[s] = rows[0, columns(2 * order[s] + core, high), :].astype(BF16)
        send_ref[s] = rows[0, columns(2 * order[chips + s] + 1 - core, high), :].astype(BF16)


def hyena(order, parts, short_filter, mode_decay, residue, blocks):
    rows_count, lanes = parts[0].shape
    chans = lanes // 2
    total = 2 * rows_count
    high = total // blocks
    modes, taps = mode_decay.shape[0], short_filter.shape[0]
    scratch = [
        pltpu.VMEM((2, total, chans), F32),
        pltpu.VMEM((high, blocks, chans), F32),
        pltpu.VMEM((modes * blocks, chans), F32),
        pltpu.VMEM((modes * blocks, chans), F32),
        pltpu.VMEM((taps - 1, 2, blocks, chans), F32),
    ]
    arrays = [*parts, short_filter, mode_decay, residue]
    kernel = functools.partial(hyena_kernel, blocks=blocks)
    shapes = [((blocks // 2, high, chans), BF16)] * 2
    return local(kernel, "hyena", shapes, order, arrays, scratch)


def payloads(order, q_next, q_in, keep, other):
    chips, high, _ = keep.shape
    chans = q_next.shape[1]

    def kernel(order, next_ref, in_ref, keep_ref, other_ref, second_ref, *out_refs):
        second_ref[...] = (next_ref[...] + in_ref[:, :chans].astype(F32)).astype(BF16)
        for s, out_ref in enumerate(out_refs):
            out_ref[0] = keep_ref[s]
            out_ref[1] = other_ref[s]

    shapes = [(q_next.shape, BF16)] + [((2, high, keep.shape[2]), BF16)] * chips
    return local(kernel, "payloads", shapes, None, [q_next, q_in, keep, other])


def gate(scalars, queries, long_parts, w_out, groups):
    rows, chans = queries[0].shape
    chips = len(long_parts)
    part = long_parts[0].shape[2]
    wide = w_out.shape[1] // groups
    first_pick = 2 * chips + 3

    def kernel(scalars, *refs):
        query_refs, long_refs = refs[: len(queries)], refs[len(queries) : len(queries) + chips]
        w_ref, gated_ref, pair_ref, query = refs[len(queries) + chips :]
        core = scalars[2 * chips]
        own_ref, second_ref, first_ref = query_refs
        query[...] = own_ref[...] + second_ref[...].astype(F32) + first_ref[...].astype(F32)
        for s, ref in enumerate(long_refs):
            for h in range(2):
                at = columns(2 * scalars[s] + (core ^ h), part)
                gated_ref[:, at] = (query[:, at] * ref[h].astype(F32)).astype(BF16)
        total = jnp.dot(
            gated_ref[...], w_ref[:, columns(scalars[first_pick], wide)], preferred_element_type=F32
        )
        pair_ref[...] = total.astype(BF16)

    shapes = [((rows, chans), BF16), ((rows, wide), BF16)]
    arrays = [*queries, *long_parts, w_out]
    scratch = [pltpu.VMEM((rows, chans), F32)]
    return local(kernel, "gate", shapes, scalars, arrays, scratch)


def out_columns(picks, pick, x, w_out, groups, kind):
    wide = w_out.shape[1] // groups

    def kernel(picks, x_ref, w_ref, out_ref):
        total = jnp.dot(
            x_ref[...], w_ref[:, columns(picks[pick], wide)], preferred_element_type=F32
        )
        out_ref[...] = total.astype(kind)

    return local(kernel, "out_columns", [((x.shape[0], wide), kind)], picks, [x, w_out])


def line_picks():
    z = lax.axis_index("dp")
    table = [[3, 0, 3, 0], [1, 2, 1, 2], [2, 3, 0, 1], [0, 1, 2, 3], [0, 1, 1, 0]]
    return [sum(jnp.where(z == i, v, 0) for i, v in enumerate(row)) for row in table]


def output_over_line(picks, gated, pair, w_out, groups):
    pair_in = lax.ppermute(pair, "dp", [(0, 1), (1, 0), (2, 3), (3, 2)])
    side = out_columns(picks, 1, gated, w_out, groups, BF16)
    middle_in = lax.ppermute(side, "dp", [(1, 2), (2, 1)])
    gated, side = lax.optimization_barrier((gated, side))
    far = out_columns(picks, 2, gated, w_out, groups, BF16)
    end_in = lax.ppermute(far, "dp", [(0, 2), (3, 1)])

    def add(picks, far_ref, pair_ref, side_ref, out_ref):
        value = far_ref[...].astype(F32) + pair_ref[...].astype(F32)
        out_ref[...] = jnp.where(picks[4] == 1, value.astype(BF16), side_ref[...])

    last = local(add, "last_step", [(far.shape, BF16)], picks, [far, pair_in, side])
    gated, last = lax.optimization_barrier((gated, last))
    last_in = lax.ppermute(last, "dp", [(0, 1), (1, 3), (2, 0), (3, 2)])
    own = out_columns(picks, 3, gated, w_out, groups, F32)

    def early(picks, own_ref, pair_ref, *refs):
        inner = picks[4] == 1
        value = own_ref[...] + jnp.where(inner, 0.0, pair_ref[...].astype(F32))
        for ref in refs[:-1]:
            value = value + ref[...].astype(F32)
        refs[-1][...] = value

    own = local(early, "early", [(own.shape, F32)], picks, [own, pair_in, middle_in, end_in])
    return (own + last_in.astype(F32)).astype(BF16)


def on_device_chips(tokens, w_in, short_filter, mode_decay, residue, w_out):
    count, groups = lax.axis_size("ctx"), lax.axis_size("dp")
    chips = count // 2

    def across(i, slot):
        high_bit, low_bit = slot >> 1, slot & 1
        step = (high_bit + 2 * low_bit) if i % 2 == 0 else (2 * high_bit + low_bit)
        return i ^ (2 * step)

    def route(slot):
        return [(i, across(i, slot)) for i in range(count)]

    order, picks = functools.partial(slot_order, chips), line_picks

    def both_scalars():
        return order() + picks()

    own_w = jnp.transpose(w_in, (1, 0, 2))
    swap = [(i, i ^ 1) for i in range(count)]

    other_w = lax.ppermute(own_w, "ctx", swap)
    xs = cut(order, tokens, chips)
    own_w, xs = lax.optimization_barrier((own_w, xs))
    own_w = stage(own_w)
    half = lax.ppermute(xs[3], "ctx", route(3))
    other = lax.ppermute(half, "dp", [(i, i ^ 1) for i in range(groups)])
    xs = [xs[0]] + [lax.ppermute(xs[s], "ctx", route(s)) for s in (1, 2)]
    joined, early = early_share(order, xs[0], half, other, own_w, other_w, 3, chips)
    xs.append(joined)

    both = rest_share(order, xs[1:3], early, own_w, other_w, 3, chips)
    both_in = lax.ppermute(both, "ctx", route(2))
    xs, both = lax.optimization_barrier((xs, both))
    first = project_mix(order, xs, own_w, other_w, [2], BF16)
    first_in = lax.ppermute(first, "ctx", route(2))
    xs, first = lax.optimization_barrier((xs, first))
    rest, ends = project_mix(order, xs, own_w, other_w, [1, 0], F32, 16)
    second, swap_second = second_share(order, rest, both_in, chips)
    second_in = lax.ppermute(second, "ctx", route(1))
    swap_second = lax.ppermute(swap_second, "ctx", [(i, j ^ 1) for i, j in route(1)])

    xs, ends, second = lax.optimization_barrier((xs, ends, second))
    before = lax.ppermute(ends, "ctx", swap)
    q_own, q_next, q_first, q_both = project_query(order, xs, before, own_w, other_w, short_filter)
    q_own, w_out = lax.optimization_barrier((q_own, w_out))
    w_out = stage(w_out)
    q_own, w_out, rest = lax.optimization_barrier((q_own, w_out, rest))

    own, other_half = first_share(order, rest, first_in, chips)
    other_half = lax.ppermute(other_half, "ctx", swap)
    q_both, q_first, own = lax.optimization_barrier((q_both, q_first, own))
    q_both = lax.ppermute(q_both, "ctx", route(2))
    q_first = lax.ppermute(q_first, "ctx", route(2))
    parts = [own, other_half, second_in, swap_second]
    keep, send = hyena(order, parts, short_filter, mode_decay, residue, count)
    other_long = lax.ppermute(send, "ctx", swap)
    q_second, *long_parts = payloads(order, q_next, q_both, keep, other_long)
    q_second = lax.ppermute(q_second, "ctx", route(1))
    long_parts = [long_parts[0]] + [lax.ppermute(long_parts[s], "ctx", route(s)) for s in (1, 2, 3)]
    queries = [q_own, q_second, q_first]
    gated, pair = gate(both_scalars, queries, long_parts, w_out, groups)
    return output_over_line(picks, gated, pair, w_out, groups)


def solution(mesh):
    count, groups = mesh.shape["ctx"], mesh.shape["dp"]

    def on_device(tokens, w_in, *rest):
        lanes = w_in.shape[2] // count
        chips = count == 8 and groups == 4 and w_in.shape[2] % count == 0 and lanes % 128 == 0
        return (on_device_chips if chips else on_device_any)(tokens, w_in, *rest)

    return jax.shard_map(
        on_device,
        mesh=mesh,
        in_specs=(
            P("ctx", None),
            P("ctx", None, "dp"),
            P(None, None, "dp"),
            P(None, "dp"),
            P(None, "dp"),
            P("dp", None),
        ),
        out_specs=P("ctx", "dp"),
        check_vma=False,
    )
```

```python
import functools

import jax
import jax.numpy as jnp
from jax import lax
from jax.experimental import pallas as pl
from jax.experimental.pallas import tpu as pltpu
from jax.sharding import PartitionSpec as P

BLK = 64
F32, BF16 = jnp.float32, jnp.bfloat16
VMEM_LIMIT = 12 * 1024 * 1024


def from_behind(block, axis, distance):
    devices = range(lax.axis_size(axis))
    route = [(i - distance, i) for i in devices if i - distance in devices]
    return lax.ppermute(block, axis, route)


def prefix(value, axis, join, neutral):
    count, mine = (lax.axis_size(axis), lax.axis_index(axis))
    pieces = jax.tree.map(lambda part: lax.all_gather(part, axis), value)
    subtotal = jax.tree.map(
        lambda part, zero: jnp.full_like(part, 0) + jnp.asarray(zero, part.dtype), value, neutral
    )

    def lap(position, subtotal):
        longer = join(subtotal, jax.tree.map(lambda part: part[position], pieces))
        return jax.tree.map(lambda new, old: jnp.where(position < mine, new, old), longer, subtotal)

    return lax.fori_loop(0, count - 1, lap, subtotal)


def on_device_any(tokens, w_in, short_filter, mode_decay, residue, w_out):
    row_count = tokens.shape[0]
    chan_count = w_in.shape[2]
    short_count = short_filter.shape[0]
    mode_count = mode_decay.shape[0]
    earlier_rows = from_behind(tokens[row_count - (short_count - 1) :], "ctx", 1)
    source = jnp.concatenate([earlier_rows, tokens], 0)
    projected = jnp.einsum(
        "td,dgc->tgc",
        source,
        lax.all_gather(w_in, "ctx", axis=0, tiled=True),
        preferred_element_type=jnp.float32,
    )
    featured = jnp.zeros((row_count, 3, chan_count), jnp.float32)
    for j in range(short_count):
        featured = (
            featured
            + short_filter[j] * projected[short_count - 1 - j : short_count - 1 - j + row_count]
        )
    mixed = (featured[:, 1] * featured[:, 2]).astype(jnp.bfloat16)
    medium = mixed.astype(jnp.float32)
    highest = lax.Precision.HIGHEST
    mode_gain = residue * jnp.sqrt(1.0 - mode_decay * mode_decay)
    block_len = BLK
    block_times = jnp.arange(block_len).astype(jnp.float32)
    power_in = jnp.power(mode_decay[None], block_times[:, None, None])
    kernel_head = jnp.sum(mode_gain[None] * power_in, 1)
    lag_index = jnp.arange(block_len)[:, None] - jnp.arange(block_len)[None, :]
    toeplitz = jnp.where(
        (lag_index >= 0)[:, :, None], kernel_head[jnp.clip(lag_index, 0, block_len - 1)], 0.0
    )
    carry_weights = mode_gain[None] * power_in * mode_decay[None]
    state_weights = power_in[::-1]
    decay_block = jnp.power(mode_decay, float(block_len))
    blocks = medium.reshape(row_count // block_len, block_len, chan_count)

    def block_step(carried, block_rows):
        inner = jnp.einsum("tsc,sc->tc", toeplitz, block_rows, precision=highest)
        inner = inner + jnp.einsum("tnc,nc->tc", carry_weights, carried, precision=highest)
        carried = decay_block * carried + jnp.einsum(
            "snc,sc->nc", state_weights, block_rows, precision=highest
        )
        return (carried, inner)

    zero_state = jnp.zeros((mode_count, chan_count), jnp.float32)
    local_end, local_part = lax.scan(block_step, zero_state, blocks)
    local_part = local_part.reshape(row_count, chan_count)
    decay_device = jnp.power(mode_decay, float(row_count))

    def combine_states(earlier, later):
        return (earlier[0] * later[0], later[0] * earlier[1] + later[1])

    identity = (jnp.ones((mode_count, chan_count), jnp.float32), zero_state)
    scanned = prefix((decay_device, local_end), "ctx", combine_states, identity)
    entering = scanned[1]
    row_times = jnp.arange(1, row_count + 1).astype(jnp.float32)
    entry_weights = mode_gain[None] * jnp.power(mode_decay[None], row_times[:, None, None])
    long_part = local_part + jnp.einsum("tnc,nc->tc", entry_weights, entering, precision=highest)
    gated = (featured[:, 0] * long_part).astype(jnp.bfloat16)
    out_term = jnp.dot(gated, w_out, preferred_element_type=jnp.float32)
    return lax.psum_scatter(out_term.astype(jnp.bfloat16), "dp", scatter_dimension=1, tiled=True)


def local(kernel, name, shapes, scalars, arrays, scratch=()):
    whole = pl.BlockSpec(memory_space=pltpu.VMEM)
    out = [jax.ShapeDtypeStruct(*shape) for shape in shapes]

    def placed(*refs):
        kernel(scalars() if scalars else None, *refs)

    return pl.pallas_call(
        placed,
        out_shape=out if len(out) > 1 else out[0],
        in_specs=[whole] * len(arrays),
        out_specs=[whole] * len(out) if len(out) > 1 else whole,
        scratch_shapes=list(scratch),
        compiler_params=pltpu.CompilerParams(vmem_limit_bytes=VMEM_LIMIT),
        name=name,
    )(*arrays)


def slot_order(chips):
    me, line = lax.axis_index("ctx"), lax.axis_index("dp")
    core, chip = lax.rem(me, 2), lax.div(me, 2)

    def chip_of(slot, core):
        high_bit, low_bit = slot >> 1, slot & 1
        one, two = high_bit + 2 * low_bit, 2 * high_bit + low_bit
        return chip ^ (one + (two - one) * core)

    mine = [chip_of(s, core) for s in range(chips)]
    other = [chip_of(s, 1 - core) for s in range(chips)]
    return mine + other + [core, me, lax.rem(line, 2)]


def columns(index, wide):
    return pl.ds(pl.multiple_of(index * wide, wide), wide)


def cut(order, tokens, pieces):
    high, wide = tokens.shape[0], tokens.shape[1] // pieces

    def kernel(order, tokens_ref, *out_refs):
        here = columns(order[2 * pieces + 2], high // 2)
        out_refs[pieces - 1][...] = tokens_ref[here, columns(order[pieces - 1], wide)]
        for s, out_ref in enumerate(out_refs[: pieces - 1]):
            out_ref[...] = tokens_ref[:, columns(order[s], wide)]

    shapes = [((high, wide), tokens.dtype)] * (pieces - 1) + [((high // 2, wide), tokens.dtype)]
    return local(kernel, "cut", shapes, order, [tokens])


def stage(array):
    def kernel(array_ref, out_ref, sem):
        copy = pltpu.make_async_copy(array_ref, out_ref, sem)
        copy.start()
        copy.wait()

    return pl.pallas_call(
        kernel,
        out_shape=jax.ShapeDtypeStruct(array.shape, array.dtype),
        in_specs=[pl.BlockSpec(memory_space=pl.ANY)],
        out_specs=pl.BlockSpec(memory_space=pltpu.VMEM),
        scratch_shapes=[pltpu.SemaphoreType.DMA],
        compiler_params=pltpu.CompilerParams(vmem_limit_bytes=VMEM_LIMIT),
        name="stage",
    )(array)


def gather_rows(core, x_refs, rows):
    high, depth = x_refs[0].shape[0], rows.shape[2]
    for i, x_ref in enumerate(x_refs):
        for h in range(2):
            rows[core ^ h, i * high : (i + 1) * high, :] = x_ref[:, h * depth : (h + 1) * depth]


def project_mix(order, xs, own, other, slots, kind, ends=0):
    chips = len(xs)
    streams, depth, chans = own.shape
    high = xs[0].shape[0]
    wide = chans // chips
    half = wide // 2

    def kernel(order, *refs):
        x_refs, (own_ref, other_ref, out_ref, *end_refs, rows) = refs[:chips], refs[chips:]
        core = order[2 * chips]
        gather_rows(core, x_refs, rows)
        for end_ref in end_refs:
            for s in range(chips):
                end_ref[s] = x_refs[s][high - ends :, :]
        for i, slot in enumerate(slots):
            at = columns(order[slot], wide)
            for g in range(1, streams):
                total = jnp.dot(rows[0], own_ref[g, :, at], preferred_element_type=F32)
                total += jnp.dot(rows[1], other_ref[g, :, at], preferred_element_type=F32)
                total = total.astype(kind)
                lanes = slice((g - 1) * half, g * half)
                for h in range(2):
                    out_ref[i, core ^ h, :, lanes] = total[:, h * half : (h + 1) * half]

    shape = (len(slots), 2, chips * high, (streams - 1) * half)
    scratch = [pltpu.VMEM((2, chips * high, depth), BF16)]
    shapes = [(shape, kind)] + ([((chips, ends, 2 * depth), BF16)] if ends else [])
    return local(kernel, "project_mix", shapes, order, [*xs, own, other], scratch)


def early_share(order, own_rows, mine, other_rows, own, other, slot, chips):
    half, wide_x = mine.shape
    high = 2 * half
    streams, depth, chans = own.shape
    wide = chans // chips
    lanes = wide // 2
    place = 2 * chips + 2

    def kernel(order, own_rows_ref, mine_ref, there_ref, own_ref, other_ref, joined_ref, out_ref, rows):
        core = order[2 * chips]
        joined_ref[columns(order[place], half), :] = mine_ref[...]
        joined_ref[columns(1 - order[place], half), :] = there_ref[...]
        gather_rows(core, (own_rows_ref, joined_ref), rows)
        at = columns(order[slot], wide)
        for g in range(1, streams):
            total = jnp.dot(rows[0], own_ref[g, :, at], preferred_element_type=F32)
            total += jnp.dot(rows[1], other_ref[g, :, at], preferred_element_type=F32)
            for h in range(2):
                to = slice((g - 1) * lanes, g * lanes)
                out_ref[core ^ h, :, to] = total[:, h * lanes : (h + 1) * lanes].astype(BF16)

    shapes = [((high, wide_x), BF16), ((2, 2 * high, (streams - 1) * lanes), BF16)]
    scratch = [pltpu.VMEM((2, 2 * high, depth), BF16)]
    arrays = [own_rows, mine, other_rows, own, other]
    return local(kernel, "early_share", shapes, order, arrays, scratch)


def rest_share(order, xs, early, own, other, slot, chips):
    high = xs[0].shape[0]
    streams, depth, chans = own.shape
    wide = chans // chips
    lanes = wide // 2

    def kernel(order, first_ref, second_ref, early_ref, own_ref, other_ref, out_ref, rows):
        core = order[2 * chips]
        gather_rows(core, (first_ref, second_ref), rows)
        at = columns(order[slot], wide)
        for h in range(2):
            out_ref[0, h, :high, :] = early_ref[h, :high, :]
            out_ref[0, h, 3 * high :, :] = early_ref[h, high:, :]
        for g in range(1, streams):
            total = jnp.dot(rows[0], own_ref[g, :, at], preferred_element_type=F32)
            total += jnp.dot(rows[1], other_ref[g, :, at], preferred_element_type=F32)
            for h in range(2):
                to = slice((g - 1) * lanes, g * lanes)
                out_ref[0, core ^ h, high : 3 * high, to] = total[
                    :, h * lanes : (h + 1) * lanes
                ].astype(BF16)

    shapes = [((1, 2, chips * high, (streams - 1) * lanes), BF16)]
    scratch = [pltpu.VMEM((2, 2 * high, depth), BF16)]
    return local(kernel, "rest_share", shapes, order, [*xs, early, own, other], scratch)


def project_query(order, xs, before, own, other, short_filter):
    chips = len(xs)
    _, depth, chans = own.shape
    high = xs[0].shape[0]
    some = before.shape[1]
    step = some + high
    taps = short_filter.shape[0]
    tile = min(chans, 256)

    def kernel(order, *refs):
        x_refs = refs[:chips]
        before_ref, own_ref, other_ref, filt_ref, *out_refs, rows, ends, total = refs[chips:]
        core = order[2 * chips]
        ends[0] = jnp.zeros_like(ends[0])
        for s in range(chips):
            ends[order[chips + s] + 1] = before_ref[s]
        for i, x_ref in enumerate(x_refs):
            end = ends[order[i] + core]
            for h in range(2):
                lanes = slice(h * depth, (h + 1) * depth)
                rows[core ^ h, i * step : i * step + some, :] = end[:, lanes]
                rows[core ^ h, i * step + some : (i + 1) * step, :] = x_ref[:, lanes]
        for at in (slice(i, i + tile) for i in range(0, chans, tile)):
            total[...] = jnp.dot(
                rows[0], own_ref[0, :, at], preferred_element_type=F32
            ) + jnp.dot(rows[1], other_ref[0, :, at], preferred_element_type=F32)
            for i in range(chips):
                first = i * step + some
                value = filt_ref[0, 0:1, at] * total[first : first + high, :]
                for j in range(1, taps):
                    value = value + filt_ref[j, 0:1, at] * total[first - j : first - j + high, :]
                out_refs[i][:, at] = value.astype(out_refs[i].dtype)

    shapes = [((high, chans), F32 if i < 2 else BF16) for i in range(chips)]
    scratch = [
        pltpu.VMEM((2, chips * step, depth), BF16),
        pltpu.VMEM((chips + 1, some, 2 * depth), BF16),
        pltpu.VMEM((chips * step, tile), F32),
    ]
    arrays = [*xs, before, own, other, short_filter]
    return local(kernel, "project_query", shapes, order, arrays, scratch)


def second_share(order, rest, both_in, chips):
    _, _, rows, lanes = rest.shape
    high = rows // chips

    def kernel(order, rest_ref, both_ref, *out_refs):
        for h, out_ref in enumerate(out_refs):
            for s in range(chips):
                here, there = (slice(i * high, (i + 1) * high) for i in (s, s ^ 2))
                term = both_ref[0, h, there, :].astype(F32)
                out_ref[here, :] = (rest_ref[0, h, here, :] + term).astype(BF16)

    shapes = [((rows, lanes), BF16)] * 2
    return local(kernel, "second_share", shapes, None, [rest, both_in])


def first_share(order, rest, first_in, chips):
    _, _, rows, lanes = rest.shape
    high = rows // chips

    def kernel(order, rest_ref, first_ref, own_ref, other_ref):
        for h, out_ref in ((1, other_ref), (0, own_ref)):
            for s in range(chips):
                here, first = (slice(i * high, (i + 1) * high) for i in (s, s ^ 2))
                total = rest_ref[1, h, here, :] + first_ref[0, h, first, :].astype(F32)
                out_ref[here, :] = total.astype(out_ref.dtype)

    shapes = [((rows, lanes), F32), ((rows, lanes), BF16)]
    return local(kernel, "first_share", shapes, None, [rest, first_in])


def hyena_kernel(
    order, own_ref, swap_ref, second_ref, swap_second_ref, filt_ref, decay_ref, residue_ref,
    keep_ref, send_ref, rows, mixed_s, state, enter, edge, *, blocks,
):
    high = rows.shape[1] // blocks
    chans = rows.shape[2]
    modes = decay_ref.shape[0]
    taps = filt_ref.shape[0]
    chips = blocks // 2
    core = order[2 * chips]
    channels = columns(order[2 * chips + 1], chans)

    for s in range(chips):
        here, second = (slice(i * high, (i + 1) * high) for i in (s, s ^ 1))
        own_at = columns(2 * order[s] + core, high)
        swap_at = columns(2 * order[chips + s] + 1 - core, high)
        for g in range(2):
            lanes = slice(g * chans, (g + 1) * chans)
            rows[g, own_at, :] = own_ref[here, lanes] + second_ref[second, lanes].astype(F32)
            rows[g, swap_at, :] = swap_ref[here, lanes].astype(F32) + swap_second_ref[
                second, lanes
            ].astype(F32)

    for k in range(1, taps):
        for g in range(2):
            edge[k - 1, g, 0:1, :] = jnp.zeros((1, chans), F32)
            for b in range(1, blocks):
                edge[k - 1, g, b : b + 1, :] = rows[g, b * high - k : b * high - k + 1, :]

    rate = decay_ref[:, channels]
    taps_of = [filt_ref[j, :, channels] for j in range(taps)]
    decay = [jnp.broadcast_to(rate[n : n + 1, :], (blocks, chans)) for n in range(modes)]
    filt = [
        [jnp.broadcast_to(taps_of[j][g + 1 : g + 2, :], (blocks, chans)) for g in range(2)]
        for j in range(taps)
    ]

    def first_pass(t, carry):
        states, earlier = carry
        now = [rows[g, pl.ds(t, blocks, stride=high), :] for g in range(2)]
        featured = []
        for g in range(2):
            value = filt[0][g] * now[g]
            for k in range(1, taps):
                value = value + filt[k][g] * earlier[k - 1][g]
            featured.append(value)
        mixed = (featured[0] * featured[1]).astype(BF16).astype(F32)
        mixed_s[t] = mixed
        states = tuple(decay[n] * states[n] + mixed for n in range(modes))
        return states, (tuple(now),) + tuple(earlier[:-1])

    zeros = tuple(jnp.zeros((blocks, chans), F32) for _ in range(modes))
    before = tuple(tuple(edge[k, g] for g in range(2)) for k in range(taps - 1))
    states, _ = lax.fori_loop(0, high, first_pass, (zeros, before), unroll=16)
    for n in range(modes):
        state[n * blocks : (n + 1) * blocks, :] = states[n]

    across = jnp.ones_like(rate)
    power, left = rate, high
    while left:
        if left & 1:
            across = across * power
        left >>= 1
        if left:
            power = power * power
    entering = jnp.zeros((modes, chans), F32)
    for b in range(blocks):
        enter[pl.ds(b, modes, stride=blocks), :] = entering
        entering = across * entering + state[pl.ds(b, modes, stride=blocks), :]

    gain = residue_ref[:, channels] * jnp.sqrt(1.0 - rate * rate)
    gains = [jnp.broadcast_to(gain[n : n + 1, :], (blocks, chans)) for n in range(modes)]

    def second_pass(t, states):
        mixed = mixed_s[t]
        states = tuple(decay[n] * states[n] + mixed for n in range(modes))
        terms = [gains[n] * states[n] for n in range(modes)]
        while len(terms) > 1:
            terms = [sum(terms[i : i + 2][1:], terms[i]) for i in range(0, len(terms), 2)]
        rows[0, pl.ds(t, blocks, stride=high), :] = terms[0]
        return states

    begin = tuple(enter[n * blocks : (n + 1) * blocks, :] for n in range(modes))
    lax.fori_loop(0, high, second_pass, begin, unroll=16)
    for s in range(chips):
        keep_ref[s] = rows[0, columns(2 * order[s] + core, high), :].astype(BF16)
        send_ref[s] = rows[0, columns(2 * order[chips + s] + 1 - core, high), :].astype(BF16)


def hyena(order, parts, short_filter, mode_decay, residue, blocks):
    rows_count, lanes = parts[0].shape
    chans = lanes // 2
    total = 2 * rows_count
    high = total // blocks
    modes, taps = mode_decay.shape[0], short_filter.shape[0]
    scratch = [
        pltpu.VMEM((2, total, chans), F32),
        pltpu.VMEM((high, blocks, chans), F32),
        pltpu.VMEM((modes * blocks, chans), F32),
        pltpu.VMEM((modes * blocks, chans), F32),
        pltpu.VMEM((taps - 1, 2, blocks, chans), F32),
    ]
    arrays = [*parts, short_filter, mode_decay, residue]
    kernel = functools.partial(hyena_kernel, blocks=blocks)
    shapes = [((blocks // 2, high, chans), BF16)] * 2
    return local(kernel, "hyena", shapes, order, arrays, scratch)


def payloads(order, q_next, q_in, keep, other):
    chips, high, _ = keep.shape
    chans = q_next.shape[1]

    def kernel(order, next_ref, in_ref, keep_ref, other_ref, second_ref, *out_refs):
        second_ref[...] = (next_ref[...] + in_ref[:, :chans].astype(F32)).astype(BF16)
        for s, out_ref in enumerate(out_refs):
            out_ref[0] = keep_ref[s]
            out_ref[1] = other_ref[s]

    shapes = [(q_next.shape, BF16)] + [((2, high, keep.shape[2]), BF16)] * chips
    return local(kernel, "payloads", shapes, None, [q_next, q_in, keep, other])


def gate(scalars, queries, long_parts, w_out, groups):
    rows, chans = queries[0].shape
    chips = len(long_parts)
    part = long_parts[0].shape[2]
    wide = w_out.shape[1] // groups
    first_pick = 2 * chips + 3

    def kernel(scalars, *refs):
        query_refs, long_refs = refs[: len(queries)], refs[len(queries) : len(queries) + chips]
        w_ref, gated_ref, pair_ref, query = refs[len(queries) + chips :]
        core = scalars[2 * chips]
        own_ref, second_ref, first_ref = query_refs
        query[...] = own_ref[...] + second_ref[...].astype(F32) + first_ref[...].astype(F32)
        for s, ref in enumerate(long_refs):
            for h in range(2):
                at = columns(2 * scalars[s] + (core ^ h), part)
                gated_ref[:, at] = (query[:, at] * ref[h].astype(F32)).astype(BF16)
        total = jnp.dot(
            gated_ref[...], w_ref[:, columns(scalars[first_pick], wide)], preferred_element_type=F32
        )
        pair_ref[...] = total.astype(BF16)

    shapes = [((rows, chans), BF16), ((rows, wide), BF16)]
    arrays = [*queries, *long_parts, w_out]
    scratch = [pltpu.VMEM((rows, chans), F32)]
    return local(kernel, "gate", shapes, scalars, arrays, scratch)


def out_columns(picks, pick, x, w_out, groups, kind):
    wide = w_out.shape[1] // groups

    def kernel(picks, x_ref, w_ref, out_ref):
        total = jnp.dot(
            x_ref[...], w_ref[:, columns(picks[pick], wide)], preferred_element_type=F32
        )
        out_ref[...] = total.astype(kind)

    return local(kernel, "out_columns", [((x.shape[0], wide), kind)], picks, [x, w_out])


def line_picks():
    z = lax.axis_index("dp")
    table = [[3, 0, 3, 0], [1, 2, 1, 2], [2, 3, 0, 1], [0, 1, 2, 3], [0, 1, 1, 0]]
    return [sum(jnp.where(z == i, v, 0) for i, v in enumerate(row)) for row in table]


def output_over_line(picks, gated, pair, w_out, groups):
    pair_in = lax.ppermute(pair, "dp", [(0, 1), (1, 0), (2, 3), (3, 2)])
    side = out_columns(picks, 1, gated, w_out, groups, BF16)
    middle_in = lax.ppermute(side, "dp", [(1, 2), (2, 1)])
    gated, side = lax.optimization_barrier((gated, side))
    far = out_columns(picks, 2, gated, w_out, groups, BF16)
    end_in = lax.ppermute(far, "dp", [(0, 2), (3, 1)])

    def add(picks, far_ref, pair_ref, side_ref, out_ref):
        value = far_ref[...].astype(F32) + pair_ref[...].astype(F32)
        out_ref[...] = jnp.where(picks[4] == 1, value.astype(BF16), side_ref[...])

    last = local(add, "last_step", [(far.shape, BF16)], picks, [far, pair_in, side])
    gated, last = lax.optimization_barrier((gated, last))
    last_in = lax.ppermute(last, "dp", [(0, 1), (1, 3), (2, 0), (3, 2)])
    own = out_columns(picks, 3, gated, w_out, groups, F32)

    def early(picks, own_ref, pair_ref, *refs):
        inner = picks[4] == 1
        value = own_ref[...] + jnp.where(inner, 0.0, pair_ref[...].astype(F32))
        for ref in refs[:-1]:
            value = value + ref[...].astype(F32)
        refs[-1][...] = value

    own = local(early, "early", [(own.shape, F32)], picks, [own, pair_in, middle_in, end_in])
    return (own + last_in.astype(F32)).astype(BF16)


def on_device_chips(tokens, w_in, short_filter, mode_decay, residue, w_out):
    count, groups = lax.axis_size("ctx"), lax.axis_size("dp")
    chips = count // 2

    def across(i, slot):
        high_bit, low_bit = slot >> 1, slot & 1
        step = (high_bit + 2 * low_bit) if i % 2 == 0 else (2 * high_bit + low_bit)
        return i ^ (2 * step)

    def route(slot):
        return [(i, across(i, slot)) for i in range(count)]

    order, picks = functools.partial(slot_order, chips), line_picks

    def both_scalars():
        return order() + picks()

    own_w = jnp.transpose(w_in, (1, 0, 2))
    swap = [(i, i ^ 1) for i in range(count)]

    other_w = lax.ppermute(own_w, "ctx", swap)
    xs = cut(order, tokens, chips)
    own_w, xs = lax.optimization_barrier((own_w, xs))
    own_w = stage(own_w)
    half = lax.ppermute(xs[3], "ctx", route(3))
    other = lax.ppermute(half, "dp", [(i, i ^ 1) for i in range(groups)])
    xs = [xs[0]] + [lax.ppermute(xs[s], "ctx", route(s)) for s in (1, 2)]
    joined, early = early_share(order, xs[0], half, other, own_w, other_w, 3, chips)
    xs.append(joined)

    both = rest_share(order, xs[1:3], early, own_w, other_w, 3, chips)
    both_in = lax.ppermute(both, "ctx", route(2))
    xs, both = lax.optimization_barrier((xs, both))
    first = project_mix(order, xs, own_w, other_w, [2], BF16)
    first_in = lax.ppermute(first, "ctx", route(2))
    xs, first = lax.optimization_barrier((xs, first))
    rest, ends = project_mix(order, xs, own_w, other_w, [1, 0], F32, 16)
    second, swap_second = second_share(order, rest, both_in, chips)
    second_in = lax.ppermute(second, "ctx", route(1))
    swap_second = lax.ppermute(swap_second, "ctx", [(i, j ^ 1) for i, j in route(1)])

    xs, ends, second = lax.optimization_barrier((xs, ends, second))
    before = lax.ppermute(ends, "ctx", swap)
    q_own, q_next, q_first, q_both = project_query(order, xs, before, own_w, other_w, short_filter)
    q_own, w_out = lax.optimization_barrier((q_own, w_out))
    w_out = stage(w_out)
    q_own, w_out, rest = lax.optimization_barrier((q_own, w_out, rest))

    q_both, first_in = lax.optimization_barrier((q_both, first_in))
    own, other_half = first_share(order, rest, first_in, chips)
    other_half = lax.ppermute(other_half, "ctx", swap)
    q_first, own = lax.optimization_barrier((q_first, own))
    q_both = lax.ppermute(q_both, "ctx", route(2))
    q_first = lax.ppermute(q_first, "ctx", route(2))
    parts = [own, other_half, second_in, swap_second]
    keep, send = hyena(order, parts, short_filter, mode_decay, residue, count)
    other_long = lax.ppermute(send, "ctx", swap)
    q_second, *long_parts = payloads(order, q_next, q_both, keep, other_long)
    q_second = lax.ppermute(q_second, "ctx", route(1))
    long_parts = [long_parts[0]] + [lax.ppermute(long_parts[s], "ctx", route(s)) for s in (1, 2, 3)]
    queries = [q_own, q_second, q_first]
    gated, pair = gate(both_scalars, queries, long_parts, w_out, groups)
    return output_over_line(picks, gated, pair, w_out, groups)


def solution(mesh):
    count, groups = mesh.shape["ctx"], mesh.shape["dp"]

    def on_device(tokens, w_in, *rest):
        lanes = w_in.shape[2] // count
        chips = count == 8 and groups == 4 and w_in.shape[2] % count == 0 and lanes % 128 == 0
        return (on_device_chips if chips else on_device_any)(tokens, w_in, *rest)

    return jax.shard_map(
        on_device,
        mesh=mesh,
        in_specs=(
            P("ctx", None),
            P("ctx", None, "dp"),
            P(None, None, "dp"),
            P(None, "dp"),
            P(None, "dp"),
            P("dp", None),
        ),
        out_specs=P("ctx", "dp"),
        check_vma=False,
    )
```

```python
import functools

import jax
import jax.numpy as jnp
from jax import lax
from jax.experimental import pallas as pl
from jax.experimental.pallas import tpu as pltpu
from jax.sharding import PartitionSpec as P

BLK = 64
F32, BF16 = jnp.float32, jnp.bfloat16
VMEM_LIMIT = 12 * 1024 * 1024


def from_behind(block, axis, distance):
    devices = range(lax.axis_size(axis))
    route = [(i - distance, i) for i in devices if i - distance in devices]
    return lax.ppermute(block, axis, route)


def prefix(value, axis, join, neutral):
    count, mine = (lax.axis_size(axis), lax.axis_index(axis))
    pieces = jax.tree.map(lambda part: lax.all_gather(part, axis), value)
    subtotal = jax.tree.map(
        lambda part, zero: jnp.full_like(part, 0) + jnp.asarray(zero, part.dtype), value, neutral
    )

    def lap(position, subtotal):
        longer = join(subtotal, jax.tree.map(lambda part: part[position], pieces))
        return jax.tree.map(lambda new, old: jnp.where(position < mine, new, old), longer, subtotal)

    return lax.fori_loop(0, count - 1, lap, subtotal)


def on_device_any(tokens, w_in, short_filter, mode_decay, residue, w_out):
    row_count = tokens.shape[0]
    chan_count = w_in.shape[2]
    short_count = short_filter.shape[0]
    mode_count = mode_decay.shape[0]
    earlier_rows = from_behind(tokens[row_count - (short_count - 1) :], "ctx", 1)
    source = jnp.concatenate([earlier_rows, tokens], 0)
    projected = jnp.einsum(
        "td,dgc->tgc",
        source,
        lax.all_gather(w_in, "ctx", axis=0, tiled=True),
        preferred_element_type=jnp.float32,
    )
    featured = jnp.zeros((row_count, 3, chan_count), jnp.float32)
    for j in range(short_count):
        featured = (
            featured
            + short_filter[j] * projected[short_count - 1 - j : short_count - 1 - j + row_count]
        )
    mixed = (featured[:, 1] * featured[:, 2]).astype(jnp.bfloat16)
    medium = mixed.astype(jnp.float32)
    highest = lax.Precision.HIGHEST
    mode_gain = residue * jnp.sqrt(1.0 - mode_decay * mode_decay)
    block_len = BLK
    block_times = jnp.arange(block_len).astype(jnp.float32)
    power_in = jnp.power(mode_decay[None], block_times[:, None, None])
    kernel_head = jnp.sum(mode_gain[None] * power_in, 1)
    lag_index = jnp.arange(block_len)[:, None] - jnp.arange(block_len)[None, :]
    toeplitz = jnp.where(
        (lag_index >= 0)[:, :, None], kernel_head[jnp.clip(lag_index, 0, block_len - 1)], 0.0
    )
    carry_weights = mode_gain[None] * power_in * mode_decay[None]
    state_weights = power_in[::-1]
    decay_block = jnp.power(mode_decay, float(block_len))
    blocks = medium.reshape(row_count // block_len, block_len, chan_count)

    def block_step(carried, block_rows):
        inner = jnp.einsum("tsc,sc->tc", toeplitz, block_rows, precision=highest)
        inner = inner + jnp.einsum("tnc,nc->tc", carry_weights, carried, precision=highest)
        carried = decay_block * carried + jnp.einsum(
            "snc,sc->nc", state_weights, block_rows, precision=highest
        )
        return (carried, inner)

    zero_state = jnp.zeros((mode_count, chan_count), jnp.float32)
    local_end, local_part = lax.scan(block_step, zero_state, blocks)
    local_part = local_part.reshape(row_count, chan_count)
    decay_device = jnp.power(mode_decay, float(row_count))

    def combine_states(earlier, later):
        return (earlier[0] * later[0], later[0] * earlier[1] + later[1])

    identity = (jnp.ones((mode_count, chan_count), jnp.float32), zero_state)
    scanned = prefix((decay_device, local_end), "ctx", combine_states, identity)
    entering = scanned[1]
    row_times = jnp.arange(1, row_count + 1).astype(jnp.float32)
    entry_weights = mode_gain[None] * jnp.power(mode_decay[None], row_times[:, None, None])
    long_part = local_part + jnp.einsum("tnc,nc->tc", entry_weights, entering, precision=highest)
    gated = (featured[:, 0] * long_part).astype(jnp.bfloat16)
    out_term = jnp.dot(gated, w_out, preferred_element_type=jnp.float32)
    return lax.psum_scatter(out_term.astype(jnp.bfloat16), "dp", scatter_dimension=1, tiled=True)


def local(kernel, name, shapes, scalars, arrays, scratch=()):
    whole = pl.BlockSpec(memory_space=pltpu.VMEM)
    out = [jax.ShapeDtypeStruct(*shape) for shape in shapes]

    def placed(*refs):
        kernel(scalars() if scalars else None, *refs)

    return pl.pallas_call(
        placed,
        out_shape=out if len(out) > 1 else out[0],
        in_specs=[whole] * len(arrays),
        out_specs=[whole] * len(out) if len(out) > 1 else whole,
        scratch_shapes=list(scratch),
        compiler_params=pltpu.CompilerParams(vmem_limit_bytes=VMEM_LIMIT),
        name=name,
    )(*arrays)


def slot_order(chips):
    me, line = lax.axis_index("ctx"), lax.axis_index("dp")
    core, chip = lax.rem(me, 2), lax.div(me, 2)

    def chip_of(slot, core):
        high_bit, low_bit = slot >> 1, slot & 1
        one, two = high_bit + 2 * low_bit, 2 * high_bit + low_bit
        return chip ^ (one + (two - one) * core)

    mine = [chip_of(s, core) for s in range(chips)]
    other = [chip_of(s, 1 - core) for s in range(chips)]
    return mine + other + [core, me, lax.rem(line, 2)]


def columns(index, wide):
    return pl.ds(pl.multiple_of(index * wide, wide), wide)


def cut(order, tokens, pieces):
    high, wide = tokens.shape[0], tokens.shape[1] // pieces

    def kernel(order, tokens_ref, *out_refs):
        here = columns(order[2 * pieces + 2], high // 2)
        out_refs[pieces - 1][...] = tokens_ref[here, columns(order[pieces - 1], wide)]
        for s, out_ref in enumerate(out_refs[: pieces - 1]):
            out_ref[...] = tokens_ref[:, columns(order[s], wide)]

    shapes = [((high, wide), tokens.dtype)] * (pieces - 1) + [((high // 2, wide), tokens.dtype)]
    return local(kernel, "cut", shapes, order, [tokens])


def stage(array):
    def kernel(array_ref, out_ref, sem):
        copy = pltpu.make_async_copy(array_ref, out_ref, sem)
        copy.start()
        copy.wait()

    return pl.pallas_call(
        kernel,
        out_shape=jax.ShapeDtypeStruct(array.shape, array.dtype),
        in_specs=[pl.BlockSpec(memory_space=pl.ANY)],
        out_specs=pl.BlockSpec(memory_space=pltpu.VMEM),
        scratch_shapes=[pltpu.SemaphoreType.DMA],
        compiler_params=pltpu.CompilerParams(vmem_limit_bytes=VMEM_LIMIT),
        name="stage",
    )(array)


def gather_rows(core, x_refs, rows):
    high, depth = x_refs[0].shape[0], rows.shape[2]
    for i, x_ref in enumerate(x_refs):
        for h in range(2):
            rows[core ^ h, i * high : (i + 1) * high, :] = x_ref[:, h * depth : (h + 1) * depth]


def project_mix(order, xs, own, other, slots, kind, ends=0):
    chips = len(xs)
    streams, depth, chans = own.shape
    high = xs[0].shape[0]
    wide = chans // chips
    half = wide // 2

    def kernel(order, *refs):
        x_refs, (own_ref, other_ref, out_ref, *end_refs, rows) = refs[:chips], refs[chips:]
        core = order[2 * chips]
        gather_rows(core, x_refs, rows)
        for end_ref in end_refs:
            for s in range(chips):
                end_ref[s] = x_refs[s][high - ends :, :]
        for i, slot in enumerate(slots):
            at = columns(order[slot], wide)
            for g in range(1, streams):
                total = jnp.dot(rows[0], own_ref[g, :, at], preferred_element_type=F32)
                total += jnp.dot(rows[1], other_ref[g, :, at], preferred_element_type=F32)
                total = total.astype(kind)
                lanes = slice((g - 1) * half, g * half)
                for h in range(2):
                    out_ref[i, core ^ h, :, lanes] = total[:, h * half : (h + 1) * half]

    shape = (len(slots), 2, chips * high, (streams - 1) * half)
    scratch = [pltpu.VMEM((2, chips * high, depth), BF16)]
    shapes = [(shape, kind)] + ([((chips, ends, 2 * depth), BF16)] if ends else [])
    return local(kernel, "project_mix", shapes, order, [*xs, own, other], scratch)


def early_share(order, own_rows, mine, other_rows, own, other, slot, chips):
    half, wide_x = mine.shape
    high = 2 * half
    streams, depth, chans = own.shape
    wide = chans // chips
    lanes = wide // 2
    place = 2 * chips + 2

    def kernel(order, own_rows_ref, mine_ref, there_ref, own_ref, other_ref, joined_ref, out_ref, rows):
        core = order[2 * chips]
        joined_ref[columns(order[place], half), :] = mine_ref[...]
        joined_ref[columns(1 - order[place], half), :] = there_ref[...]
        gather_rows(core, (own_rows_ref, joined_ref), rows)
        at = columns(order[slot], wide)
        for g in range(1, streams):
            total = jnp.dot(rows[0], own_ref[g, :, at], preferred_element_type=F32)
            total += jnp.dot(rows[1], other_ref[g, :, at], preferred_element_type=F32)
            for h in range(2):
                to = slice((g - 1) * lanes, g * lanes)
                out_ref[core ^ h, :, to] = total[:, h * lanes : (h + 1) * lanes].astype(BF16)

    shapes = [((high, wide_x), BF16), ((2, 2 * high, (streams - 1) * lanes), BF16)]
    scratch = [pltpu.VMEM((2, 2 * high, depth), BF16)]
    arrays = [own_rows, mine, other_rows, own, other]
    return local(kernel, "early_share", shapes, order, arrays, scratch)


def rest_share(order, xs, early, own, other, slot, chips):
    high = xs[0].shape[0]
    streams, depth, chans = own.shape
    wide = chans // chips
    lanes = wide // 2

    def kernel(order, first_ref, second_ref, early_ref, own_ref, other_ref, out_ref, rows):
        core = order[2 * chips]
        gather_rows(core, (first_ref, second_ref), rows)
        at = columns(order[slot], wide)
        for h in range(2):
            out_ref[0, h, :high, :] = early_ref[h, :high, :]
            out_ref[0, h, 3 * high :, :] = early_ref[h, high:, :]
        for g in range(1, streams):
            total = jnp.dot(rows[0], own_ref[g, :, at], preferred_element_type=F32)
            total += jnp.dot(rows[1], other_ref[g, :, at], preferred_element_type=F32)
            for h in range(2):
                to = slice((g - 1) * lanes, g * lanes)
                out_ref[0, core ^ h, high : 3 * high, to] = total[
                    :, h * lanes : (h + 1) * lanes
                ].astype(BF16)

    shapes = [((1, 2, chips * high, (streams - 1) * lanes), BF16)]
    scratch = [pltpu.VMEM((2, 2 * high, depth), BF16)]
    return local(kernel, "rest_share", shapes, order, [*xs, early, own, other], scratch)


def project_query(order, xs, before, own, other, short_filter):
    chips = len(xs)
    _, depth, chans = own.shape
    high = xs[0].shape[0]
    some = before.shape[1]
    step = some + high
    taps = short_filter.shape[0]
    tile = min(chans, 256)

    def kernel(order, *refs):
        x_refs = refs[:chips]
        before_ref, own_ref, other_ref, filt_ref, *out_refs, rows, ends, total = refs[chips:]
        core = order[2 * chips]
        ends[0] = jnp.zeros_like(ends[0])
        for s in range(chips):
            ends[order[chips + s] + 1] = before_ref[s]
        for i, x_ref in enumerate(x_refs):
            end = ends[order[i] + core]
            for h in range(2):
                lanes = slice(h * depth, (h + 1) * depth)
                rows[core ^ h, i * step : i * step + some, :] = end[:, lanes]
                rows[core ^ h, i * step + some : (i + 1) * step, :] = x_ref[:, lanes]
        for at in (slice(i, i + tile) for i in range(0, chans, tile)):
            total[...] = jnp.dot(
                rows[0], own_ref[0, :, at], preferred_element_type=F32
            ) + jnp.dot(rows[1], other_ref[0, :, at], preferred_element_type=F32)
            for i in range(chips):
                first = i * step + some
                value = filt_ref[0, 0:1, at] * total[first : first + high, :]
                for j in range(1, taps):
                    value = value + filt_ref[j, 0:1, at] * total[first - j : first - j + high, :]
                out_refs[i][:, at] = value.astype(out_refs[i].dtype)

    shapes = [((high, chans), F32 if i < 2 else BF16) for i in range(chips)]
    scratch = [
        pltpu.VMEM((2, chips * step, depth), BF16),
        pltpu.VMEM((chips + 1, some, 2 * depth), BF16),
        pltpu.VMEM((chips * step, tile), F32),
    ]
    arrays = [*xs, before, own, other, short_filter]
    return local(kernel, "project_query", shapes, order, arrays, scratch)


def second_share(order, rest, both_in, chips):
    _, _, rows, lanes = rest.shape
    high = rows // chips

    def kernel(order, rest_ref, both_ref, *out_refs):
        for h, out_ref in enumerate(out_refs):
            for s in range(chips):
                here, there = (slice(i * high, (i + 1) * high) for i in (s, s ^ 2))
                term = both_ref[0, h, there, :].astype(F32)
                out_ref[here, :] = (rest_ref[0, h, here, :] + term).astype(BF16)

    shapes = [((rows, lanes), BF16)] * 2
    return local(kernel, "second_share", shapes, None, [rest, both_in])


def first_share(order, rest, first_in, chips):
    _, _, rows, lanes = rest.shape
    high = rows // chips

    def kernel(order, rest_ref, first_ref, own_ref, other_ref):
        for h, out_ref in ((1, other_ref), (0, own_ref)):
            for s in range(chips):
                here, first = (slice(i * high, (i + 1) * high) for i in (s, s ^ 2))
                total = rest_ref[1, h, here, :] + first_ref[0, h, first, :].astype(F32)
                out_ref[here, :] = total.astype(out_ref.dtype)

    shapes = [((rows, lanes), F32), ((rows, lanes), BF16)]
    return local(kernel, "first_share", shapes, None, [rest, first_in])


def hyena_kernel(
    order, own_ref, swap_ref, second_ref, swap_second_ref, filt_ref, decay_ref, residue_ref,
    keep_ref, send_ref, rows, mixed_s, state, enter, edge, *, blocks,
):
    high = rows.shape[1] // blocks
    chans = rows.shape[2]
    modes = decay_ref.shape[0]
    taps = filt_ref.shape[0]
    chips = blocks // 2
    core = order[2 * chips]
    channels = columns(order[2 * chips + 1], chans)

    for s in range(chips):
        here, second = (slice(i * high, (i + 1) * high) for i in (s, s ^ 1))
        own_at = columns(2 * order[s] + core, high)
        swap_at = columns(2 * order[chips + s] + 1 - core, high)
        for g in range(2):
            lanes = slice(g * chans, (g + 1) * chans)
            rows[g, own_at, :] = own_ref[here, lanes] + second_ref[second, lanes].astype(F32)
            rows[g, swap_at, :] = swap_ref[here, lanes].astype(F32) + swap_second_ref[
                second, lanes
            ].astype(F32)

    for k in range(1, taps):
        for g in range(2):
            edge[k - 1, g, 0:1, :] = jnp.zeros((1, chans), F32)
            for b in range(1, blocks):
                edge[k - 1, g, b : b + 1, :] = rows[g, b * high - k : b * high - k + 1, :]

    rate = decay_ref[:, channels]
    taps_of = [filt_ref[j, :, channels] for j in range(taps)]
    decay = [jnp.broadcast_to(rate[n : n + 1, :], (blocks, chans)) for n in range(modes)]
    filt = [
        [jnp.broadcast_to(taps_of[j][g + 1 : g + 2, :], (blocks, chans)) for g in range(2)]
        for j in range(taps)
    ]

    def first_pass(t, carry):
        states, earlier = carry
        now = [rows[g, pl.ds(t, blocks, stride=high), :] for g in range(2)]
        featured = []
        for g in range(2):
            value = filt[0][g] * now[g]
            for k in range(1, taps):
                value = value + filt[k][g] * earlier[k - 1][g]
            featured.append(value)
        mixed = (featured[0] * featured[1]).astype(BF16).astype(F32)
        mixed_s[t] = mixed
        states = tuple(decay[n] * states[n] + mixed for n in range(modes))
        return states, (tuple(now),) + tuple(earlier[:-1])

    zeros = tuple(jnp.zeros((blocks, chans), F32) for _ in range(modes))
    before = tuple(tuple(edge[k, g] for g in range(2)) for k in range(taps - 1))
    states, _ = lax.fori_loop(0, high, first_pass, (zeros, before), unroll=16)
    for n in range(modes):
        state[n * blocks : (n + 1) * blocks, :] = states[n]

    across = jnp.ones_like(rate)
    power, left = rate, high
    while left:
        if left & 1:
            across = across * power
        left >>= 1
        if left:
            power = power * power
    entering = jnp.zeros((modes, chans), F32)
    for b in range(blocks):
        enter[pl.ds(b, modes, stride=blocks), :] = entering
        entering = across * entering + state[pl.ds(b, modes, stride=blocks), :]

    gain = residue_ref[:, channels] * jnp.sqrt(1.0 - rate * rate)
    gains = [jnp.broadcast_to(gain[n : n + 1, :], (blocks, chans)) for n in range(modes)]

    def second_pass(t, states):
        mixed = mixed_s[t]
        states = tuple(decay[n] * states[n] + mixed for n in range(modes))
        terms = [gains[n] * states[n] for n in range(modes)]
        while len(terms) > 1:
            terms = [sum(terms[i : i + 2][1:], terms[i]) for i in range(0, len(terms), 2)]
        rows[0, pl.ds(t, blocks, stride=high), :] = terms[0]
        return states

    begin = tuple(enter[n * blocks : (n + 1) * blocks, :] for n in range(modes))
    lax.fori_loop(0, high, second_pass, begin, unroll=16)
    for s in range(chips):
        keep_ref[s] = rows[0, columns(2 * order[s] + core, high), :].astype(BF16)
        send_ref[s] = rows[0, columns(2 * order[chips + s] + 1 - core, high), :].astype(BF16)


def hyena(order, parts, short_filter, mode_decay, residue, blocks):
    rows_count, lanes = parts[0].shape
    chans = lanes // 2
    total = 2 * rows_count
    high = total // blocks
    modes, taps = mode_decay.shape[0], short_filter.shape[0]
    scratch = [
        pltpu.VMEM((2, total, chans), F32),
        pltpu.VMEM((high, blocks, chans), F32),
        pltpu.VMEM((modes * blocks, chans), F32),
        pltpu.VMEM((modes * blocks, chans), F32),
        pltpu.VMEM((taps - 1, 2, blocks, chans), F32),
    ]
    arrays = [*parts, short_filter, mode_decay, residue]
    kernel = functools.partial(hyena_kernel, blocks=blocks)
    shapes = [((blocks // 2, high, chans), BF16)] * 2
    return local(kernel, "hyena", shapes, order, arrays, scratch)


def payloads(order, q_next, q_in, keep, other):
    chips, high, _ = keep.shape
    chans = q_next.shape[1]

    def kernel(order, next_ref, in_ref, keep_ref, other_ref, second_ref, *out_refs):
        second_ref[...] = (next_ref[...] + in_ref[:, :chans].astype(F32)).astype(BF16)
        for s, out_ref in enumerate(out_refs):
            out_ref[0] = keep_ref[s]
            out_ref[1] = other_ref[s]

    shapes = [(q_next.shape, BF16)] + [((2, high, keep.shape[2]), BF16)] * chips
    return local(kernel, "payloads", shapes, None, [q_next, q_in, keep, other])


def gate(scalars, queries, long_parts, w_out, groups):
    rows, chans = queries[0].shape
    chips = len(long_parts)
    part = long_parts[0].shape[2]
    wide = w_out.shape[1] // groups
    first_pick = 2 * chips + 3

    def kernel(scalars, *refs):
        query_refs, long_refs = refs[: len(queries)], refs[len(queries) : len(queries) + chips]
        w_ref, gated_ref, pair_ref, query = refs[len(queries) + chips :]
        core = scalars[2 * chips]
        own_ref, second_ref, first_ref = query_refs
        query[...] = own_ref[...] + second_ref[...].astype(F32) + first_ref[...].astype(F32)
        for s, ref in enumerate(long_refs):
            for h in range(2):
                at = columns(2 * scalars[s] + (core ^ h), part)
                gated_ref[:, at] = (query[:, at] * ref[h].astype(F32)).astype(BF16)
        total = jnp.dot(
            gated_ref[...], w_ref[:, columns(scalars[first_pick], wide)], preferred_element_type=F32
        )
        pair_ref[...] = total.astype(BF16)

    shapes = [((rows, chans), BF16), ((rows, wide), BF16)]
    arrays = [*queries, *long_parts, w_out]
    scratch = [pltpu.VMEM((rows, chans), F32)]
    return local(kernel, "gate", shapes, scalars, arrays, scratch)


def out_columns(picks, pick, x, w_out, groups, kind):
    wide = w_out.shape[1] // groups

    def kernel(picks, x_ref, w_ref, out_ref):
        total = jnp.dot(
            x_ref[...], w_ref[:, columns(picks[pick], wide)], preferred_element_type=F32
        )
        out_ref[...] = total.astype(kind)

    return local(kernel, "out_columns", [((x.shape[0], wide), kind)], picks, [x, w_out])


def line_picks():
    z = lax.axis_index("dp")
    table = [[3, 0, 3, 0], [1, 2, 1, 2], [2, 3, 0, 1], [0, 1, 2, 3], [0, 1, 1, 0]]
    return [sum(jnp.where(z == i, v, 0) for i, v in enumerate(row)) for row in table]


def output_over_line(picks, gated, pair, w_out, groups):
    pair_in = lax.ppermute(pair, "dp", [(0, 1), (1, 0), (2, 3), (3, 2)])
    side = out_columns(picks, 1, gated, w_out, groups, BF16)
    middle_in = lax.ppermute(side, "dp", [(1, 2), (2, 1)])
    gated, side = lax.optimization_barrier((gated, side))
    far = out_columns(picks, 2, gated, w_out, groups, BF16)
    end_in = lax.ppermute(far, "dp", [(0, 2), (3, 1)])

    def add(picks, far_ref, pair_ref, side_ref, out_ref):
        value = far_ref[...].astype(F32) + pair_ref[...].astype(F32)
        out_ref[...] = jnp.where(picks[4] == 1, value.astype(BF16), side_ref[...])

    last = local(add, "last_step", [(far.shape, BF16)], picks, [far, pair_in, side])
    gated, last = lax.optimization_barrier((gated, last))
    last_in = lax.ppermute(last, "dp", [(0, 1), (1, 3), (2, 0), (3, 2)])
    own = out_columns(picks, 3, gated, w_out, groups, F32)

    def early(picks, own_ref, pair_ref, *refs):
        inner = picks[4] == 1
        value = own_ref[...] + jnp.where(inner, 0.0, pair_ref[...].astype(F32))
        for ref in refs[:-1]:
            value = value + ref[...].astype(F32)
        refs[-1][...] = value

    own = local(early, "early", [(own.shape, F32)], picks, [own, pair_in, middle_in, end_in])
    return (own + last_in.astype(F32)).astype(BF16)


def on_device_chips(tokens, w_in, short_filter, mode_decay, residue, w_out):
    count, groups = lax.axis_size("ctx"), lax.axis_size("dp")
    chips = count // 2

    def across(i, slot):
        high_bit, low_bit = slot >> 1, slot & 1
        step = (high_bit + 2 * low_bit) if i % 2 == 0 else (2 * high_bit + low_bit)
        return i ^ (2 * step)

    def route(slot):
        return [(i, across(i, slot)) for i in range(count)]

    order, picks = functools.partial(slot_order, chips), line_picks

    def both_scalars():
        return order() + picks()

    own_w = jnp.transpose(w_in, (1, 0, 2))
    swap = [(i, i ^ 1) for i in range(count)]

    other_w = lax.ppermute(own_w, "ctx", swap)
    xs = cut(order, tokens, chips)
    own_w, xs = lax.optimization_barrier((own_w, xs))
    own_w = stage(own_w)
    half = lax.ppermute(xs[3], "ctx", route(3))
    other = lax.ppermute(half, "dp", [(i, i ^ 1) for i in range(groups)])
    xs = [xs[0]] + [lax.ppermute(xs[s], "ctx", route(s)) for s in (1, 2)]
    joined, early = early_share(order, xs[0], half, other, own_w, other_w, 3, chips)
    xs.append(joined)

    both = rest_share(order, xs[1:3], early, own_w, other_w, 3, chips)
    both_in = lax.ppermute(both, "ctx", route(2))
    xs, both = lax.optimization_barrier((xs, both))
    first = project_mix(order, xs, own_w, other_w, [2], BF16)
    first_in = lax.ppermute(first, "ctx", route(2))
    xs, first = lax.optimization_barrier((xs, first))
    rest, ends = project_mix(order, xs, own_w, other_w, [1, 0], F32, 16)
    second, swap_second = second_share(order, rest, both_in, chips)
    second_in = lax.ppermute(second, "ctx", route(1))
    swap_second = lax.ppermute(swap_second, "ctx", [(i, j ^ 1) for i, j in route(1)])

    xs, ends, second = lax.optimization_barrier((xs, ends, second))
    before = lax.ppermute(ends, "ctx", swap)
    q_own, q_next, q_first, q_both = project_query(order, xs, before, own_w, other_w, short_filter)
    q_own, w_out = lax.optimization_barrier((q_own, w_out))
    w_out = stage(w_out)
    q_own, w_out, rest = lax.optimization_barrier((q_own, w_out, rest))

    q_both, q_first, first_in = lax.optimization_barrier((q_both, q_first, first_in))
    own, other_half = first_share(order, rest, first_in, chips)
    other_half = lax.ppermute(other_half, "ctx", swap)
    q_both = lax.ppermute(q_both, "ctx", route(2))
    q_first = lax.ppermute(q_first, "ctx", route(2))
    parts = [own, other_half, second_in, swap_second]
    keep, send = hyena(order, parts, short_filter, mode_decay, residue, count)
    other_long = lax.ppermute(send, "ctx", swap)
    q_second, *long_parts = payloads(order, q_next, q_both, keep, other_long)
    q_second = lax.ppermute(q_second, "ctx", route(1))
    long_parts = [long_parts[0]] + [lax.ppermute(long_parts[s], "ctx", route(s)) for s in (1, 2, 3)]
    queries = [q_own, q_second, q_first]
    gated, pair = gate(both_scalars, queries, long_parts, w_out, groups)
    return output_over_line(picks, gated, pair, w_out, groups)


def solution(mesh):
    count, groups = mesh.shape["ctx"], mesh.shape["dp"]

    def on_device(tokens, w_in, *rest):
        lanes = w_in.shape[2] // count
        chips = count == 8 and groups == 4 and w_in.shape[2] % count == 0 and lanes % 128 == 0
        return (on_device_chips if chips else on_device_any)(tokens, w_in, *rest)

    return jax.shard_map(
        on_device,
        mesh=mesh,
        in_specs=(
            P("ctx", None),
            P("ctx", None, "dp"),
            P(None, None, "dp"),
            P(None, "dp"),
            P(None, "dp"),
            P("dp", None),
        ),
        out_specs=P("ctx", "dp"),
        check_vma=False,
    )
```
